32 devices in a mesh: rows: 32 (over z, y, x, core).
Axes of the slice: x: 2, y: 2, z: 4, core: 2. Of those that a mesh axis runs over, the one named last changes fastest.
Arguments:
- hamiltonian: float32 [49152, 1728], P('rows'), may hold values from -0.15625 to 0.15625
- subspace: float32 [49152, 128], P('rows'), may hold values from -6 to 6
- block_cols: int32 [768, 27], P('rows'), may hold values from 0 to 775, as said below
- far_list: int32 [32, 8], P('rows'), may hold values from -1 to 767, as said below
Outputs:
- filtered: float32 [49152, 128], P('rows')
The draws below stay inside these ranges and needn't reach their ends.
Inputs may be any that keep to these rules, and one draw needn't show every extreme that they name: `far_list`: row d holds in slots 0 to c_d - 1 distinct block indices owned by device d xor (4) (that device owns blocks k * 24 to k * 24 + 23 for its index k), and -1 in its other slots; c_d is 2 or more, and device 0 fills all 8 slots. `block_cols`: entry 0 of row i is i; the next 24 entries are distinct blocks (i + o) mod 768 with 0 < |o| <= 13; the last two are 768 + s for two distinct filled slots s of far_list's row of the device that owns row i.
All inputs are finite; a program needn't handle non-finite values.
Results may differ from the reference program's by a relative error of at most 0.000058.
Values sent between devices are 32-bit elements; how exact they have to be, the bound alone decides.
No kernel may reach another device: no remote copies, remote signals or barrier semaphores. Data moves between devices by JAX's collectives and lax.ppermute only.
A program may use at most 128 MiB of HBM per device.

```python
import jax
import jax.numpy as jnp
from jax import lax

B = 64
K = 128
REACH = 13
NBD = 24
NNZ = 27
M = 8
NROW = 49152
N_ROWS = 32


def layout(key):
    folded = jax.random.fold_in(key, 7)
    subkeys = jax.random.split(folded, 7)
    block_total = NBD * N_ROWS
    device = jnp.arange(N_ROWS, dtype=jnp.int32)
    partner = jnp.bitwise_xor(device, N_ROWS // 8)
    crowded = jax.random.randint(subkeys[0], (N_ROWS,), 0, 20) < 3
    sparse_count = jax.random.randint(subkeys[1], (N_ROWS,), 2, max(3, M // 3 + 1))
    filled = jnp.where(crowded | (device == 0), M, sparse_count).astype(jnp.int32)
    scores = jax.random.randint(subkeys[2], (N_ROWS, NBD), 0, 1 << 20) * NBD + jnp.arange(NBD, dtype=jnp.int32)[None, :]
    chosen = jnp.argsort(scores, axis=1)[:, :M].astype(jnp.int32)
    slot_ids = jnp.arange(M, dtype=jnp.int32)[None, :]
    far_list = jnp.where(slot_ids < filled[:, None], partner[:, None] * NBD + chosen, -1).astype(jnp.int32)
    row_index = jnp.arange(block_total, dtype=jnp.int32)
    owner_device = row_index // NBD
    span = 2 * REACH
    first_drop = jax.random.randint(subkeys[3], (block_total,), 0, span)
    second_drop = (first_drop + 1 + jax.random.randint(subkeys[4], (block_total,), 0, span - 1)) % span
    offset_index = jnp.arange(span, dtype=jnp.int32)[None, :]
    dropped = (offset_index == first_drop[:, None]) | (offset_index == second_drop[:, None])
    keeping = jnp.argsort(offset_index + 4 * REACH * dropped.astype(jnp.int32), axis=1)[:, :span - 2]
    offsets_all = jnp.concatenate([jnp.arange(-REACH, 0, dtype=jnp.int32), jnp.arange(1, REACH + 1, dtype=jnp.int32)])
    kept_offsets = offsets_all[keeping]
    with_self = jnp.concatenate([jnp.zeros((block_total, 1), jnp.int32), kept_offsets], axis=1)
    banded = (row_index[:, None] + with_self) % block_total
    slot_count = filled[owner_device]
    first_slot = jax.random.randint(subkeys[5], (block_total,), 0, slot_count)
    second_slot = (first_slot + 1 + jax.random.randint(subkeys[6], (block_total,), 0, slot_count - 1)) % slot_count
    block_cols = jnp.concatenate([banded, (block_total + first_slot)[:, None], (block_total + second_slot)[:, None]], axis=1)
    return (far_list, block_cols.astype(jnp.int32))


def draw_block_cols(key, part):
    return layout(key)[1]


def draw_far_list(key, part):
    return layout(key)[0]


def steps_of(rng, dims, pieces, least, largest):
    level, own = 1.0, jax.random.fold_in(rng, 6)
    for position, blocks in pieces:
        steps = jnp.exp(jax.random.uniform(jax.random.fold_in(own, position), (blocks,), jnp.float32, least / len(pieces), largest / len(pieces)))
        level = level * jnp.repeat(steps, dims[position] // blocks).reshape([-1 if axis == position else 1 for axis in range(len(dims))])
    return level


def bell_draw(rng, extent, deviation, bound, cuts=(), held_as=jnp.bfloat16):
    values = jax.random.normal(rng, extent, jnp.float32) * deviation
    if len(cuts) > 0:
        values = steps_of(rng, extent, cuts, -0.22, 0.18) * values
    return jnp.clip(values, min=-bound, max=bound).astype(held_as)


def setup_inputs(seed: int = 0) -> dict:
    seeds = jax.random.split(jax.random.key(seed), 5)
    hamiltonian = bell_draw(seeds[0], (NROW, NNZ * B), (NNZ * B) ** -0.5, 0.15625, ((0, 32),), jnp.float32)
    subspace = bell_draw(seeds[1], (NROW, K), 1.0, 6.0, ((0, 32),), jnp.float32)
    block_cols = draw_block_cols(jax.random.fold_in(seeds[4], 71), 0)
    far_list = draw_far_list(jax.random.fold_in(seeds[4], 71), 0)
    return dict(hamiltonian=hamiltonian, subspace=subspace, block_cols=block_cols, far_list=far_list)


CENTER = 0.25
HALF_WIDTH = 1.5


def resolve(block_cols, far_list):
    block_total = NBD * N_ROWS
    owner_row = (jnp.arange(block_total, dtype=jnp.int32) // NBD)[:, None]
    slot_index = jnp.clip(block_cols - block_total, 0, M - 1).astype(jnp.int32)
    remote = far_list[owner_row, slot_index]
    return jnp.where(block_cols < block_total, block_cols, remote).astype(jnp.int32)


def apply_operator(hamiltonian, vectors, columns):
    blocks = vectors.reshape(N_ROWS * NBD, B, K)
    ham_slabs = hamiltonian.reshape(N_ROWS, NBD, B, NNZ * B)
    col_slabs = columns.reshape(N_ROWS, NBD, NNZ)

    def product_slab(operands):
        ham_slab, cols_slab = operands
        picked = blocks[cols_slab].reshape(NBD, NNZ * B, K)
        return jnp.einsum("irm,imk->irk", ham_slab, picked, precision=lax.Precision.HIGHEST)

    result = lax.map(product_slab, (ham_slabs, col_slabs))
    return result.reshape(N_ROWS * NBD * B, K)


def reference(hamiltonian, subspace, block_cols, far_list):
    columns = resolve(block_cols, far_list)
    first_term = (apply_operator(hamiltonian, subspace, columns) - CENTER * subspace) / HALF_WIDTH
    second = apply_operator(hamiltonian, first_term, columns)
    return (2.0 / HALF_WIDTH) * (second - CENTER * first_term) - subspace
```

```python
import functools

import jax
import jax.numpy as jnp
from jax import lax
from jax.experimental import pallas as pl
from jax.experimental.pallas import tpu as pltpu
from jax.sharding import PartitionSpec as P

CENTER = 0.25
HALF_WIDTH = 1.5
REACH = 13


def partner(value, axis, bit):
    mask = 2**bit
    pairs = [(source, source ^ mask) for source in range(lax.axis_size(axis))]
    return lax.ppermute(value, axis, pairs)


def halo(above, below, axis):
    devices = lax.axis_size(axis)
    up = [(i, (i + 1) % devices) for i in range(devices)]
    down = [(j, i) for i, j in up]
    return lax.ppermute(above, axis, up), lax.ppermute(below, axis, down)


def split(value):
    high = value.astype(jnp.bfloat16)
    return high, (value - high.astype(jnp.float32)).astype(jnp.bfloat16)


def band_kernel(pairs, entries, slots, size, inverse, ham_t, band, staged, sems):
    depth = entries * size
    lane = lax.broadcasted_iota(jnp.int32, (size, 2 * size), 1)

    def fetch(p):
        return pltpu.make_async_copy(
            ham_t.at[:, pl.ds(p * 2 * size, 2 * size)],
            staged.at[p, pl.ds(0, depth), :],
            sems.at[p],
        )

    for p in range(pairs):
        fetch(p).start()
    for p in range(pairs):
        staged[p, depth:, :] = jnp.zeros((size, 2 * size), jnp.float32)

    def one_pair(p, carry):
        fetch(p).wait()
        for q in range(slots):
            even = inverse[2 * p, q] * size
            odd = inverse[2 * p + 1, q] * size
            first = staged[p, pl.ds(pl.multiple_of(even, size), size), :]
            second = staged[p, pl.ds(pl.multiple_of(odd, size), size), :]
            high, low = split(jnp.where(lane < size, first, second))
            band[p, q * size : (q + 1) * size, : 2 * size] = high
            band[p, q * size : (q + 1) * size, 2 * size :] = low
        return carry

    lax.fori_loop(0, pairs, one_pair, 0)


def make_band(inverse, ham_t, size):
    depth, rows = ham_t.shape
    entries = depth // size
    pairs = rows // (2 * size)
    slots = inverse.shape[1]
    return pl.pallas_call(
        functools.partial(band_kernel, pairs, entries, slots, size),
        out_shape=pltpu.VMEM((pairs, slots * size, 4 * size), jnp.bfloat16),
        in_specs=[
            pl.BlockSpec(memory_space=pltpu.SMEM),
            pl.BlockSpec(memory_space=pl.ANY),
        ],
        out_specs=pl.BlockSpec(memory_space=pltpu.VMEM),
        scratch_shapes=[
            pltpu.VMEM((pairs, depth + size, 2 * size), jnp.float32),
            pltpu.SemaphoreType.DMA((pairs,)),
        ],
        compiler_params=pltpu.CompilerParams(vmem_limit_bytes=16 * 2**20),
        cost_estimate=pl.CostEstimate(
            flops=0, bytes_accessed=2 * 4 * depth * rows, transcendentals=0
        ),
        name="band",
    )(inverse, ham_t)


def apply_kernel(size, first, asked, own, lower, upper, far, band, *rest):
    if first:
        result, to_lower, to_upper, to_far, turned = rest
    else:
        start, result, turned = rest
    width = own.shape[1]
    tile = 2 * size
    near = lower.shape[0]
    rows = own.shape[0]
    panel = rows + 2 * near
    pieces = [(0, lower), (near, own), (near + rows, upper), (panel, far)]
    total = panel + far.shape[0]

    def rows_of(begin):
        parts = []
        for offset, ref in pieces:
            lo = max(begin, offset)
            hi = min(begin + tile, offset + ref.shape[0])
            if lo < hi:
                parts.append(ref[lo - offset : hi - offset, :])
        return parts[0] if len(parts) == 1 else jnp.concatenate(parts, axis=0)

    for begin in range(0, total, tile):
        high, low = split(rows_of(begin).T)
        turned[:width, begin : begin + tile] = high
        turned[width:, begin : begin + tile] = low

    reach = tile + 2 * near
    for p in range(rows // tile):
        at = p * tile
        sums = jnp.dot(
            turned[:, at : at + reach],
            band[p, :reach, :],
            preferred_element_type=jnp.float32,
        ) + jnp.dot(
            turned[:, panel:], band[p, reach:, :], preferred_element_type=jnp.float32
        )
        small = sums[width:, tile:] + sums[width:, :tile] + sums[:width, tile:]
        product = (small + sums[:width, :tile]).T
        here = own[at : at + tile, :]
        shifted = product - CENTER * here
        if first:
            value = shifted * (1.0 / HALF_WIDTH)
            result[at : at + tile, :] = value
            count = min(tile, near - at)
            if count > 0:
                to_lower[at : at + count, :] = value[:count]
            skip = max(0, rows - near - at)
            if skip < tile:
                base = at + skip - (rows - near)
                to_upper[base : base + tile - skip, :] = value[skip:]
        else:
            result[at : at + tile, :] = (
                2.0 / HALF_WIDTH * shifted - start[at : at + tile, :]
            )
    if first:
        for slot in range(to_far.shape[0] // size):
            row = pl.multiple_of(asked[slot] * size, size)
            to_far[slot * size : (slot + 1) * size, :] = result[pl.ds(row, size), :]


def run_apply(size, asked, own, lower, upper, far, band, start=None):
    first = start is None
    rows, width = own.shape
    near = lower.shape[0]
    total = rows + 2 * near + far.shape[0]
    f32 = jnp.float32
    out_shape = [jax.ShapeDtypeStruct(own.shape, f32)]
    if first:
        out_shape += [
            jax.ShapeDtypeStruct(lower.shape, f32),
            jax.ShapeDtypeStruct(upper.shape, f32),
            jax.ShapeDtypeStruct(far.shape, f32),
        ]
    operands = [asked, own, lower, upper, far, band] + ([] if first else [start])
    vmem = pl.BlockSpec(memory_space=pltpu.VMEM)
    return pl.pallas_call(
        functools.partial(apply_kernel, size, first),
        out_shape=out_shape,
        in_specs=[pl.BlockSpec(memory_space=pltpu.SMEM)] + [vmem] * (len(operands) - 1),
        out_specs=[vmem] * len(out_shape),
        scratch_shapes=[pltpu.VMEM((2 * width, total), jnp.bfloat16)],
        compiler_params=pltpu.CompilerParams(vmem_limit_bytes=16 * 2**20),
        cost_estimate=pl.CostEstimate(
            flops=2 * 2 * width * band.size, bytes_accessed=2 * band.size, transcendentals=0
        ),
        name="apply",
    )(*operands)


def far_kernel(size, asked, own, out):
    for slot in range(out.shape[0] // size):
        row = pl.multiple_of(asked[slot] * size, size)
        out[slot * size : (slot + 1) * size, :] = own[pl.ds(row, size), :]


def gather_far(asked, own, size):
    return pl.pallas_call(
        functools.partial(far_kernel, size),
        out_shape=jax.ShapeDtypeStruct((asked.shape[0] * size, own.shape[1]), own.dtype),
        in_specs=[
            pl.BlockSpec(memory_space=pltpu.SMEM),
            pl.BlockSpec(memory_space=pltpu.VMEM),
        ],
        out_specs=pl.BlockSpec(memory_space=pltpu.VMEM),
        compiler_params=pltpu.CompilerParams(vmem_limit_bytes=4 * 2**20),
        name="far",
    )(asked, own)


def per_device(hamiltonian, subspace, block_cols, far_list):
    block_rows, entries = block_cols.shape
    size = hamiltonian.shape[1] // entries
    slot_total = far_list.shape[1]
    device_count = lax.axis_size("rows")
    first_row = lax.axis_index("rows") * block_rows
    block_total = block_rows * device_count
    swap_level = (device_count // 8).bit_length() - 1
    near = REACH * size
    rows = block_rows * size

    asked_list = partner(far_list, "rows", swap_level)
    lower, upper = halo(subspace[rows - near :], subspace[:near], "rows")
    asked = jnp.clip(asked_list[0] - first_row, 0, block_rows - 1)
    outgoing = gather_far(asked, subspace, size)

    pair_row = first_row + 2 * (jnp.arange(block_rows, dtype=jnp.int32)[:, None] // 2)
    reach = 2 + 2 * REACH
    places = jnp.where(
        block_cols < block_total,
        (block_cols - pair_row + REACH + block_total) % block_total,
        reach + block_cols - block_total,
    )
    slots = jnp.arange(reach + slot_total, dtype=jnp.int32)
    entry = jnp.arange(entries, dtype=jnp.int32)[None, :, None]
    hit = places[:, :, None] == slots[None, None, :]
    inverse = entries + jnp.sum(jnp.where(hit, entry - entries, 0), axis=1)

    far = partner(outgoing, "rows", swap_level)
    inverse, _ = lax.optimization_barrier((inverse, outgoing))
    band = make_band(inverse, hamiltonian.T, size)

    value, to_lower, to_upper, to_far = run_apply(
        size, asked, subspace, lower, upper, far, band
    )
    far = partner(to_far, "rows", swap_level)
    lower, upper = halo(to_upper, to_lower, "rows")
    return run_apply(size, asked, value, lower, upper, far, band, subspace)[0]


def solution(mesh):
    placed = (P("rows", None), P("rows", None), P("rows", None), P("rows", None))
    return jax.shard_map(
        per_device, mesh=mesh, in_specs=placed, out_specs=P("rows", None), check_vma=False
    )
```

```python
import functools

import jax
import jax.numpy as jnp
from jax import lax
from jax.experimental import pallas as pl
from jax.experimental.pallas import tpu as pltpu
from jax.sharding import PartitionSpec as P

CENTER = 0.25
HALF_WIDTH = 1.5
REACH = 13
PARTS = 2
F32 = jnp.float32
VMEM = pl.BlockSpec(memory_space=pltpu.VMEM)
SMEM = pl.BlockSpec(memory_space=pltpu.SMEM)


def partner(value, axis, bit):
    mask = 2**bit
    pairs = [(source, source ^ mask) for source in range(lax.axis_size(axis))]
    return lax.ppermute(value, axis, pairs)


def halo(above, below, axis):
    devices = lax.axis_size(axis)
    up = [(i, (i + 1) % devices) for i in range(devices)]
    down = [(j, i) for i, j in up]
    return lax.ppermute(above, axis, up), lax.ppermute(below, axis, down)


def split(value):
    high = value.astype(jnp.bfloat16)
    return high, (value - high.astype(F32)).astype(jnp.bfloat16)


def fold(sums):
    width, tile = sums.shape[0] // 2, sums.shape[1] // 2
    small = sums[width:, tile:] + sums[width:, :tile] + sums[:width, tile:]
    return small + sums[:width, :tile]


def params(limit):
    return pltpu.CompilerParams(vmem_limit_bytes=limit * 2**20)


def cost(flops, moved):
    return pl.CostEstimate(flops=flops, bytes_accessed=moved, transcendentals=0)


class Plan:
    def __init__(self, size, rows, width, slots):
        self.size, self.rows, self.width = size, rows, width
        self.tile = 2 * size
        self.pairs = rows // self.tile
        self.near = (REACH + 1) // 2
        self.far = slots * size // self.tile
        self.edge = self.near * self.tile
        self.part = width // PARTS
        self.outer = 2 * self.near + self.far
        self.places = 2 * (self.outer + self.pairs)

    def outer_range(self, p):
        extra = p + self.near - self.pairs + 1
        if isinstance(p, int):
            return min(p, self.near), self.near + self.far + max(0, extra)
        return jnp.minimum(p, self.near), self.near + self.far + jnp.maximum(0, extra)

    def own_range(self, p):
        return max(0, p - self.near), min(self.pairs, p + self.near + 1)


def write_far(plan, asked, source, write):
    tile, size = plan.tile, plan.size
    lane = lax.broadcasted_iota(jnp.int32, (source.shape[0], tile), 1)

    def block(slot, want):
        index = asked[slot]
        at = pl.multiple_of((index // 2) * tile, tile)
        value = source[:, pl.ds(at, tile)]
        return jnp.where(index % 2 == want, value, pltpu.roll(value, size, 1))

    for t in range(plan.far):
        value = jnp.where(lane < size, block(2 * t, 0), block(2 * t + 1, 1))
        write(t * tile, value)


def pack_kernel(plan, natural, turned, *sends):
    tile, edge, part = plan.tile, plan.edge, plan.part
    for p in range(plan.pairs):
        turned[:, p * tile : (p + 1) * tile] = natural[p * tile : (p + 1) * tile, :].T
    for h in range(PARTS):
        rows = slice(h * part, (h + 1) * part)
        sends[2 * h][...] = turned[rows, plan.rows - edge :]
        sends[2 * h + 1][...] = turned[rows, :edge]


def pack(plan, natural):
    edge = jax.ShapeDtypeStruct((plan.part, plan.edge), F32)
    return pl.pallas_call(
        functools.partial(pack_kernel, plan),
        out_shape=[pltpu.VMEM((plan.width, plan.rows), F32)] + [edge] * (2 * PARTS),
        in_specs=[VMEM],
        out_specs=[VMEM] * (1 + 2 * PARTS),
        compiler_params=params(8),
        name="pack",
    )(natural)


def far_kernel(plan, asked, turned, out):
    def write(at, value):
        out[:, at : at + plan.tile] = value

    write_far(plan, asked, turned, write)


def gather_far(plan, asked, turned):
    return pl.pallas_call(
        functools.partial(far_kernel, plan),
        out_shape=jax.ShapeDtypeStruct((plan.width, plan.far * plan.tile), F32),
        in_specs=[SMEM, VMEM],
        out_specs=VMEM,
        compiler_params=params(8),
        name="far",
    )(asked, turned)


def band_kernel(plan, depth, inverse, ham_t, vectors, band, inner, staged, halves, sems):
    size, tile, width = plan.size, plan.tile, plan.width
    lane = lax.broadcasted_iota(jnp.int32, (size, tile), 1)

    def fetch(p):
        return pltpu.make_async_copy(
            ham_t.at[:, pl.ds(pl.multiple_of(p * tile, tile), tile)],
            staged.at[p, pl.ds(0, depth), :],
            sems.at[p],
        )

    for p in range(plan.pairs):
        fetch(p).start()
    for p in range(plan.pairs):
        staged[p, depth:, :] = jnp.zeros((size, tile), F32)
    for p in range(plan.pairs):
        at = p * tile
        high, low = split(vectors[:, at : at + tile])
        halves[:width, at : at + tile] = high
        halves[width:, at : at + tile] = low

    def place(p, q, at):
        even = pl.multiple_of(inverse[2 * p, q] * size, size)
        odd = pl.multiple_of(inverse[2 * p + 1, q] * size, size)
        first = staged[p, pl.ds(even, size), :]
        second = staged[p, pl.ds(odd, size), :]
        high, low = split(jnp.where(lane < size, first, second))
        band[p, pl.ds(at, size), :tile] = high
        band[p, pl.ds(at, size), tile:] = low

    def one_pair(p, carry):
        fetch(p).wait()
        for q in range(2 * plan.outer, plan.places):
            place(p, q, q * size)
        sums = jnp.dot(
            halves[...], band[p, plan.outer * tile :, :], preferred_element_type=F32
        )
        inner[:, pl.ds(pl.multiple_of(p * tile, tile), tile)] = fold(sums)

        def outer_tile(t, carry):
            for q in range(2):
                at = pl.multiple_of(t * tile + q * size, size)
                place(p, 2 * t + q, at)
            return carry

        lax.fori_loop(*plan.outer_range(p), outer_tile, 0)
        return carry

    lax.fori_loop(0, plan.pairs, one_pair, 0)


def make_band(plan, inverse, ham_t, vectors):
    depth, rows = ham_t.shape
    size, tile = plan.size, plan.tile
    return pl.pallas_call(
        functools.partial(band_kernel, plan, depth),
        out_shape=[
            pltpu.VMEM((plan.pairs, plan.places * size, 2 * tile), jnp.bfloat16),
            pltpu.VMEM((plan.width, rows), F32),
        ],
        in_specs=[SMEM, pl.BlockSpec(memory_space=pltpu.HBM), VMEM],
        out_specs=[VMEM, VMEM],
        scratch_shapes=[
            pltpu.VMEM((plan.pairs, depth + size, tile), F32),
            pltpu.VMEM((2 * plan.width, rows), jnp.bfloat16),
            pltpu.SemaphoreType.DMA((plan.pairs,)),
        ],
        compiler_params=params(16),
        cost_estimate=cost(8 * plan.width * rows * rows, 2 * 4 * depth * rows),
        name="band",
    )(inverse, pltpu.with_memory_space_constraint(ham_t, pltpu.HBM), vectors)


def inner_kernel(plan, *refs):
    vectors, band, inner, halves = refs[:PARTS], *refs[PARTS:]
    tile, width, part = plan.tile, plan.width, plan.part
    for p in range(plan.pairs):
        at = p * tile
        for h, ref in enumerate(vectors):
            high, low = split(ref[:, at : at + tile])
            halves[h * part : (h + 1) * part, at : at + tile] = high
            halves[width + h * part : width + (h + 1) * part, at : at + tile] = low
    base = plan.outer * tile
    for p in range(plan.pairs):
        begin, end = (tile * bound for bound in plan.own_range(p))
        sums = jnp.dot(
            halves[:, begin:end],
            band[p, base + begin : base + end, :],
            preferred_element_type=F32,
        )
        inner[:, p * tile : (p + 1) * tile] = fold(sums)


def run_inner(plan, vectors, band):
    return pl.pallas_call(
        functools.partial(inner_kernel, plan),
        out_shape=pltpu.VMEM((plan.width, plan.rows), F32),
        in_specs=[VMEM] * (PARTS + 1),
        out_specs=VMEM,
        scratch_shapes=[pltpu.VMEM((2 * plan.width, plan.rows), jnp.bfloat16)],
        compiler_params=params(8),
        cost_estimate=cost(8 * plan.width * plan.rows**2, 0),
        name="inner",
    )(*vectors, band)


def outer_products(plan, h, lower, far, upper, band, halves):
    tile, part = plan.tile, plan.part
    at = 0
    for ref in (lower, far, upper):
        rows = slice(h * part, (h + 1) * part) if ref.shape[0] > part else slice(None)
        for begin in range(0, ref.shape[1], tile):
            high, low = split(ref[rows, begin : begin + tile])
            halves[:part, at : at + tile] = high
            halves[part:, at : at + tile] = low
            at += tile
    for p in range(plan.pairs):
        begin, end = (tile * bound for bound in plan.outer_range(p))
        sums = jnp.dot(
            halves[:, begin:end], band[p, begin:end, :], preferred_element_type=F32
        )
        yield p * tile, fold(sums)


def first_kernel(
    plan, h, asked, lower, far, upper, band, inner, own, value, to_upper, to_lower, to_far, halves
):
    tile, edge, part = plan.tile, plan.edge, plan.part
    rows = slice(h * part, (h + 1) * part)
    for at, product in outer_products(plan, h, lower, far, upper, band, halves):
        lanes = slice(at, at + tile)
        shifted = product + inner[rows, lanes] - CENTER * own[rows, lanes]
        term = shifted * (1.0 / HALF_WIDTH)
        value[:, lanes] = term
        if at < edge:
            to_lower[:, lanes] = term
        skip = plan.rows - edge
        if at >= skip:
            to_upper[:, at - skip : at - skip + tile] = term

    def write(at, term):
        to_far[:, at : at + tile] = term

    write_far(plan, asked, value, write)


def run_first(plan, h, asked, arrived, band, inner, own):
    edge = jax.ShapeDtypeStruct((plan.part, plan.edge), F32)
    far = jax.ShapeDtypeStruct((plan.part, plan.far * plan.tile), F32)
    return pl.pallas_call(
        functools.partial(first_kernel, plan, h),
        out_shape=[pltpu.VMEM((plan.part, plan.rows), F32), edge, edge, far],
        in_specs=[SMEM] + [VMEM] * 6,
        out_specs=[VMEM] * 4,
        scratch_shapes=[pltpu.VMEM((2 * plan.part, plan.outer * plan.tile), jnp.bfloat16)],
        compiler_params=params(8),
        cost_estimate=cost(8 * plan.part * plan.rows**2, 0),
        name="first",
    )(asked, *arrived, band, inner, own)


def second_kernel(plan, h, lower, far, upper, band, inner, own, start, *rest):
    earlier, out, halves = rest[:-2], *rest[-2:]
    tile, part = plan.tile, plan.part
    rows = slice(h * part, (h + 1) * part)
    for at, product in outer_products(plan, h, lower, far, upper, band, halves):
        lanes = slice(at, at + tile)
        shifted = product + inner[rows, lanes] - CENTER * own[:, lanes]
        term = 2.0 / HALF_WIDTH * shifted - start[rows, lanes]
        if h < PARTS - 1:
            out[:, lanes] = term
        else:
            whole = [ref[:, lanes] for ref in earlier] + [term]
            out[lanes, :] = jnp.concatenate(whole, axis=0).T


def run_second(plan, h, arrived, band, inner, own, start, earlier):
    if h < PARTS - 1:
        out, earlier = pltpu.VMEM((plan.part, plan.rows), F32), []
    else:
        out = jax.ShapeDtypeStruct((plan.rows, plan.width), F32)
    return pl.pallas_call(
        functools.partial(second_kernel, plan, h),
        out_shape=out,
        in_specs=[VMEM] * (7 + len(earlier)),
        out_specs=VMEM,
        scratch_shapes=[pltpu.VMEM((2 * plan.part, plan.outer * plan.tile), jnp.bfloat16)],
        compiler_params=params(8),
        cost_estimate=cost(8 * plan.part * plan.rows**2, 0),
        name="second",
    )(*arrived, band, inner, own, start, *earlier)


def after(value, *others):
    return lax.optimization_barrier((value, *others))[0]


def per_device(hamiltonian, subspace, block_cols, far_list):
    block_rows, entries = block_cols.shape
    size = hamiltonian.shape[1] // entries
    device_count = lax.axis_size("rows")
    first_row = lax.axis_index("rows") * block_rows
    block_total = block_rows * device_count
    swap_level = (device_count // 8).bit_length() - 1
    plan = Plan(size, block_rows * size, subspace.shape[1], far_list.shape[1])

    asked_list = partner(far_list, "rows", swap_level)
    start, *sends = pack(plan, subspace)
    asked = jnp.clip(asked_list[0] - first_row, 0, block_rows - 1)

    listed = gather_far(plan, asked, start)
    far = partner(listed, "rows", swap_level)
    arrived = []
    for h in range(PARTS):
        above, below = sends[2 * h : 2 * h + 2]
        if h > 0:
            above, below = lax.optimization_barrier((above, below, listed))[:2]
        lower, upper = halo(above, below, "rows")
        arrived.append((lower, far, upper))

    near, far_slots = 2 * plan.near, 2 * plan.far
    shift = (block_cols - first_row + near + block_total) % block_total
    places = jnp.where(
        block_cols >= block_total,
        near + block_cols - block_total,
        jnp.where(
            shift < near,
            shift,
            jnp.where(
                shift < near + block_rows,
                shift - near + 2 * plan.outer,
                shift - block_rows + far_slots,
            ),
        ),
    )
    every = jnp.arange(plan.places, dtype=jnp.int32)[None, None, :]
    entry = jnp.arange(entries, dtype=jnp.int32)[None, :, None]
    hit = places[:, :, None] == every
    inverse = entries + jnp.sum(jnp.where(hit, entry - entries, 0), axis=1)

    band, inner = make_band(plan, after(inverse, listed), hamiltonian.T, start)

    values, later = [], []
    for h in range(PARTS):
        if values:
            inner = after(inner, values[-1])
        value, above, below, listed = run_first(
            plan, h, asked, arrived[h], band, inner, start
        )
        values.append(value)
        far = partner(listed, "rows", swap_level)
        lower, upper = halo(above, below, "rows")
        later.append((lower, far, upper))
    inner = run_inner(plan, values, band)
    result = []
    for h in range(PARTS):
        if result:
            inner = after(inner, result[-1])
        out = run_second(plan, h, later[h], band, inner, values[h], start, result)
        result.append(out)
    return result[-1]


def solution(mesh):
    placed = (P("rows", None), P("rows", None), P("rows", None), P("rows", None))
    return jax.shard_map(
        per_device, mesh=mesh, in_specs=placed, out_specs=P("rows", None), check_vma=False
    )
```

```python
import functools

import jax
import jax.numpy as jnp
from jax import lax
from jax.experimental import pallas as pl
from jax.experimental.pallas import tpu as pltpu
from jax.sharding import PartitionSpec as P

CENTER = 0.25
HALF_WIDTH = 1.5
REACH = 13
PARTS = 1
F32 = jnp.float32
VMEM = pl.BlockSpec(memory_space=pltpu.VMEM)
SMEM = pl.BlockSpec(memory_space=pltpu.SMEM)


def partner(value, axis, bit):
    mask = 2**bit
    pairs = [(source, source ^ mask) for source in range(lax.axis_size(axis))]
    return lax.ppermute(value, axis, pairs)


def swap_chips(value, axis):
    devices = lax.axis_size(axis)
    pairs = [(i, (i + (1 if i % 2 else -1)) % devices) for i in range(devices)]
    return lax.ppermute(value, axis, pairs)


def split(value):
    high = value.astype(jnp.bfloat16)
    return high, (value - high.astype(F32)).astype(jnp.bfloat16)


def fold(sums):
    width, tile = sums.shape[0] // 2, sums.shape[1] // 2
    small = sums[width:, tile:] + sums[width:, :tile] + sums[:width, tile:]
    return small + sums[:width, :tile]


def params(limit):
    return pltpu.CompilerParams(vmem_limit_bytes=limit * 2**20)


def cost(flops, moved):
    return pl.CostEstimate(flops=flops, bytes_accessed=moved, transcendentals=0)


class Plan:
    def __init__(self, size, rows, width, slots):
        self.size, self.rows, self.width = size, rows, width
        self.tile = 2 * size
        self.pairs = rows // self.tile
        self.near = (REACH + 1) // 2
        self.far = slots * size // self.tile
        self.edge = self.near * self.tile
        self.part = width // PARTS
        self.outer = 2 * self.near + self.far
        self.places = 2 * (self.outer + self.pairs)

    def outer_range(self, p):
        extra = p + self.near - self.pairs + 1
        if isinstance(p, int):
            return min(p, self.near), self.near + self.far + max(0, extra)
        return jnp.minimum(p, self.near), self.near + self.far + jnp.maximum(0, extra)

    def own_range(self, p):
        begin, end = p - self.near, p + self.near + 1
        if isinstance(p, int):
            return max(0, begin), min(self.pairs, end)
        return jnp.maximum(0, begin), jnp.minimum(self.pairs, end)


def write_far(plan, asked, source, write):
    tile, size = plan.tile, plan.size
    lane = lax.broadcasted_iota(jnp.int32, (source.shape[0], tile), 1)

    def block(slot, want):
        index = lax.rem(asked[0, slot] + 2 * plan.pairs, 2 * plan.pairs)
        at = pl.multiple_of((index // 2) * tile, tile)
        value = source[:, pl.ds(at, tile)]
        return jnp.where(index % 2 == want, value, pltpu.roll(value, size, 1))

    for t in range(plan.far):
        value = jnp.where(lane < size, block(2 * t, 0), block(2 * t + 1, 1))
        write(t * tile, value)


def write_sends(plan, side, source, rows, away, near):
    skip = plan.rows - plan.edge
    odd = side[0]
    for ref, at in ((away, odd * skip), (near, (1 - odd) * skip)):
        ref[...] = source[rows, pl.ds(pl.multiple_of(at, plan.tile), plan.edge)]


def pack_kernel(plan, chunks, side, natural, turned, *rest):
    sends, staged, sems = rest[:-2], *rest[-2:]
    tile, part, step = plan.tile, plan.part, plan.rows // chunks

    def fetch(c):
        return pltpu.make_async_copy(
            natural.at[pl.ds(c * step, step), :],
            staged.at[pl.ds(c * step, step), :],
            sems.at[c],
        )

    for c in range(chunks):
        fetch(c).start()
    for c in range(chunks):
        fetch(c).wait()
        for at in range(c * step, (c + 1) * step, tile):
            turned[:, at : at + tile] = staged[at : at + tile, :].T
    for h in range(PARTS):
        rows = slice(h * part, (h + 1) * part)
        write_sends(plan, side, turned, rows, *sends[2 * h : 2 * h + 2])


def pack(plan, side, natural):
    edge = jax.ShapeDtypeStruct((plan.part, plan.edge), F32)
    chunks = 4 if plan.pairs % 4 == 0 else 1
    return pl.pallas_call(
        functools.partial(pack_kernel, plan, chunks),
        out_shape=[pltpu.VMEM((plan.width, plan.rows), F32)] + [edge] * (2 * PARTS),
        in_specs=[SMEM, pl.BlockSpec(memory_space=pltpu.HBM)],
        out_specs=[VMEM] * (1 + 2 * PARTS),
        scratch_shapes=[
            pltpu.VMEM((plan.rows, plan.width), F32),
            pltpu.SemaphoreType.DMA((chunks,)),
        ],
        compiler_params=params(8),
        name="pack",
    )(side, pltpu.with_memory_space_constraint(natural, pltpu.HBM))


def far_kernel(plan, asked, turned, out):
    def write(at, value):
        out[:, at : at + plan.tile] = value

    write_far(plan, asked, turned, write)


def gather_far(plan, asked, turned):
    return pl.pallas_call(
        functools.partial(far_kernel, plan),
        out_shape=jax.ShapeDtypeStruct((plan.width, plan.far * plan.tile), F32),
        in_specs=[SMEM, VMEM],
        out_specs=VMEM,
        compiler_params=params(8),
        name="far",
    )(asked, turned)


def band_kernel(plan, depth, inverse, ham_t, band, staged, sems):
    size, tile = plan.size, plan.tile
    lane = lax.broadcasted_iota(jnp.int32, (size, tile), 1)

    def fetch(p):
        return pltpu.make_async_copy(
            ham_t.at[:, pl.ds(pl.multiple_of(p * tile, tile), tile)],
            staged.at[p, pl.ds(0, depth), :],
            sems.at[p],
        )

    for p in range(plan.pairs):
        fetch(p).start()
    for p in range(plan.pairs):
        staged[p, depth:, :] = jnp.zeros((size, tile), F32)

    def one_pair(p, carry):
        fetch(p).wait()

        def block(q):
            even = pl.multiple_of(inverse[2 * p, q] * size, size)
            odd = pl.multiple_of(inverse[2 * p + 1, q] * size, size)
            first = staged[p, pl.ds(even, size), :]
            second = staged[p, pl.ds(odd, size), :]
            return jnp.where(lane < size, first, second)

        def group(g, carry):
            halves = [split(block(4 * g + q)) for q in range(4)]
            for q, (high, low) in enumerate(halves):
                at = pl.multiple_of((4 * g + q) * size, size)
                band[p, pl.ds(at, size), :tile] = high
                band[p, pl.ds(at, size), tile:] = low
            return carry

        begin, end = plan.outer_range(p)
        lax.fori_loop(begin // 2, (end + 1) // 2, group, 0)
        begin, end = (plan.outer + bound for bound in plan.own_range(p))
        lax.fori_loop(begin // 2, (end + 1) // 2, group, 0)
        return carry

    lax.fori_loop(0, plan.pairs, one_pair, 0)


def make_band(plan, inverse, ham_t):
    depth, rows = ham_t.shape
    size, tile = plan.size, plan.tile
    return pl.pallas_call(
        functools.partial(band_kernel, plan, depth),
        out_shape=pltpu.VMEM((plan.pairs, plan.places * size, 2 * tile), jnp.bfloat16),
        in_specs=[SMEM, pl.BlockSpec(memory_space=pltpu.HBM)],
        out_specs=VMEM,
        scratch_shapes=[
            pltpu.VMEM((plan.pairs, depth + size, tile), F32),
            pltpu.SemaphoreType.DMA((plan.pairs,)),
        ],
        compiler_params=params(16),
        cost_estimate=cost(0, 2 * 4 * depth * rows),
        name="band",
    )(inverse, pltpu.with_memory_space_constraint(ham_t, pltpu.HBM))


def inner_kernel(plan, *refs):
    vectors, band, inner, halves = refs[:PARTS], *refs[PARTS:]
    tile, width, part = plan.tile, plan.width, plan.part
    for p in range(plan.pairs):
        at = p * tile
        for h, ref in enumerate(vectors):
            high, low = split(ref[:, at : at + tile])
            halves[h * part : (h + 1) * part, at : at + tile] = high
            halves[width + h * part : width + (h + 1) * part, at : at + tile] = low
    base = plan.outer * tile
    for p in range(plan.pairs):
        begin, end = (tile * bound for bound in plan.own_range(p))
        sums = jnp.dot(
            halves[:, begin:end],
            band[p, base + begin : base + end, :],
            preferred_element_type=F32,
        )
        inner[:, p * tile : (p + 1) * tile] = fold(sums)


def run_inner(plan, vectors, band):
    return pl.pallas_call(
        functools.partial(inner_kernel, plan),
        out_shape=pltpu.VMEM((plan.width, plan.rows), F32),
        in_specs=[VMEM] * (PARTS + 1),
        out_specs=VMEM,
        scratch_shapes=[pltpu.VMEM((2 * plan.width, plan.rows), jnp.bfloat16)],
        compiler_params=params(8),
        cost_estimate=cost(8 * plan.width * plan.rows**2, 0),
        name="inner",
    )(*vectors, band)


def outer_products(plan, h, side, away, far, near, band, halves):
    tile, part = plan.tile, plan.part
    upper = (plan.near + plan.far) * tile
    odd = side[0]
    for ref, base in ((away, odd * upper), (near, (1 - odd) * upper), (far, plan.edge)):
        rows = slice(h * part, (h + 1) * part) if ref.shape[0] > part else slice(None)
        for begin in range(0, ref.shape[1], tile):
            at = pl.ds(pl.multiple_of(base + begin, tile), tile)
            high, low = split(ref[rows, begin : begin + tile])
            halves[:part, at] = high
            halves[part:, at] = low
    for p in range(plan.pairs):
        begin, end = (tile * bound for bound in plan.outer_range(p))
        sums = jnp.dot(
            halves[:, begin:end], band[p, begin:end, :], preferred_element_type=F32
        )
        yield p * tile, fold(sums)


def first_kernel(
    plan, h, side, asked, away, far, near, band, inner, own, value, to_away, to_near, to_far, halves
):
    tile, part = plan.tile, plan.part
    rows = slice(h * part, (h + 1) * part)
    for at, product in outer_products(plan, h, side, away, far, near, band, halves):
        lanes = slice(at, at + tile)
        shifted = product + inner[rows, lanes] - CENTER * own[rows, lanes]
        value[:, lanes] = shifted * (1.0 / HALF_WIDTH)
    write_sends(plan, side, value, slice(None), to_away, to_near)

    def write(at, term):
        to_far[:, at : at + tile] = term

    write_far(plan, asked, value, write)


def run_first(plan, h, side, asked, arrived, band, inner, own):
    edge = jax.ShapeDtypeStruct((plan.part, plan.edge), F32)
    far = jax.ShapeDtypeStruct((plan.part, plan.far * plan.tile), F32)
    return pl.pallas_call(
        functools.partial(first_kernel, plan, h),
        out_shape=[pltpu.VMEM((plan.part, plan.rows), F32), edge, edge, far],
        in_specs=[SMEM] * 2 + [VMEM] * 6,
        out_specs=[VMEM] * 4,
        scratch_shapes=[pltpu.VMEM((2 * plan.part, plan.outer * plan.tile), jnp.bfloat16)],
        compiler_params=params(8),
        cost_estimate=cost(8 * plan.part * plan.rows**2, 0),
        name="first",
    )(side, asked, *arrived, band, inner, own)


def second_kernel(plan, h, side, away, far, near, band, inner, own, start, *rest):
    earlier, out, halves = rest[:-2], *rest[-2:]
    tile, part = plan.tile, plan.part
    rows = slice(h * part, (h + 1) * part)
    for at, product in outer_products(plan, h, side, away, far, near, band, halves):
        lanes = slice(at, at + tile)
        shifted = product + inner[rows, lanes] - CENTER * own[:, lanes]
        term = 2.0 / HALF_WIDTH * shifted - start[rows, lanes]
        if h < PARTS - 1:
            out[:, lanes] = term
        else:
            whole = [ref[:, lanes] for ref in earlier] + [term]
            out[lanes, :] = jnp.concatenate(whole, axis=0).T


def run_second(plan, h, side, arrived, band, inner, own, start, earlier):
    if h < PARTS - 1:
        out, earlier = pltpu.VMEM((plan.part, plan.rows), F32), []
    else:
        out = jax.ShapeDtypeStruct((plan.rows, plan.width), F32)
    return pl.pallas_call(
        functools.partial(second_kernel, plan, h),
        out_shape=out,
        in_specs=[SMEM] + [VMEM] * (7 + len(earlier)),
        out_specs=VMEM,
        scratch_shapes=[pltpu.VMEM((2 * plan.part, plan.outer * plan.tile), jnp.bfloat16)],
        compiler_params=params(8),
        cost_estimate=cost(8 * plan.part * plan.rows**2, 0),
        name="second",
    )(side, *arrived, band, inner, own, start, *earlier)


def after(value, *others):
    return lax.optimization_barrier((value, *others))[0]


def per_device(hamiltonian, subspace, block_cols, far_list):
    block_rows, entries = block_cols.shape
    size = hamiltonian.shape[1] // entries
    device_count = lax.axis_size("rows")
    first_row = lax.axis_index("rows") * block_rows
    block_total = block_rows * device_count
    swap_level = (device_count // 8).bit_length() - 1
    plan = Plan(size, block_rows * size, subspace.shape[1], far_list.shape[1])

    side = (lax.axis_index("rows") % 2).astype(jnp.int32).reshape(1)

    def exchange(to_away, to_near):
        return swap_chips(to_away, "rows"), partner(to_near, "rows", 0)

    asked = partner(far_list, "rows", swap_level)
    start, *sends = pack(plan, side, subspace)
    listed = gather_far(plan, asked, start)
    far = partner(listed, "rows", swap_level)
    arrived = []
    for h in range(PARTS):
        to_away, to_near = sends[2 * h : 2 * h + 2]
        if h > 0:
            to_away, to_near = lax.optimization_barrier((to_away, to_near, listed))[:2]
        away, near = exchange(to_away, to_near)
        arrived.append((away, far, near))

    block_cols = after(block_cols, listed)
    near, far_slots = 2 * plan.near, 2 * plan.far
    shift = (block_cols - first_row + near + block_total) % block_total
    places = jnp.where(
        block_cols >= block_total,
        near + block_cols - block_total,
        jnp.where(
            shift < near,
            shift,
            jnp.where(
                shift < near + block_rows,
                shift - near + 2 * plan.outer,
                shift - block_rows + far_slots,
            ),
        ),
    )
    every = jnp.arange(plan.places, dtype=jnp.int32)[None, None, :]
    entry = jnp.arange(entries, dtype=jnp.int32)[None, :, None]
    hit = places[:, :, None] == every
    inverse = entries + jnp.sum(jnp.where(hit, entry - entries, 0), axis=1)

    band = make_band(plan, inverse, hamiltonian.T)
    inner = run_inner(plan, [start[h * plan.part : (h + 1) * plan.part] for h in range(PARTS)], band)

    values, later = [], []
    for h in range(PARTS):
        if values:
            inner = after(inner, values[-1])
        value, to_away, to_near, listed = run_first(
            plan, h, side, asked, arrived[h], band, inner, start
        )
        values.append(value)
        far = partner(listed, "rows", swap_level)
        away, near = exchange(to_away, to_near)
        later.append((away, far, near))
    inner = run_inner(plan, values, band)
    result = []
    for h in range(PARTS):
        if result:
            inner = after(inner, result[-1])
        out = run_second(plan, h, side, later[h], band, inner, values[h], start, result)
        result.append(out)
    return result[-1]


def solution(mesh):
    placed = (P("rows", None), P("rows", None), P("rows", None), P("rows", None))
    return jax.shard_map(
        per_device, mesh=mesh, in_specs=placed, out_specs=P("rows", None), check_vma=False
    )
```

```python
import functools

import jax
import jax.numpy as jnp
from jax import lax
from jax.experimental import pallas as pl
from jax.experimental.pallas import tpu as pltpu
from jax.sharding import PartitionSpec as P

CENTER = 0.25
HALF_WIDTH = 1.5
REACH = 13
PARTS = 1
F32 = jnp.float32
VMEM = pl.BlockSpec(memory_space=pltpu.VMEM)
SMEM = pl.BlockSpec(memory_space=pltpu.SMEM)


def partner(value, axis, bit):
    mask = 2**bit
    pairs = [(source, source ^ mask) for source in range(lax.axis_size(axis))]
    return lax.ppermute(value, axis, pairs)


def swap_chips(value, axis):
    devices = lax.axis_size(axis)
    pairs = [(i, (i + (1 if i % 2 else -1)) % devices) for i in range(devices)]
    return lax.ppermute(value, axis, pairs)


def split(value):
    high = value.astype(jnp.bfloat16)
    return high, (value - high.astype(F32)).astype(jnp.bfloat16)


def fold(sums):
    width, tile = sums.shape[0] // 2, sums.shape[1] // 2
    small = sums[width:, tile:] + sums[width:, :tile] + sums[:width, tile:]
    return small + sums[:width, :tile]


def params(limit):
    return pltpu.CompilerParams(vmem_limit_bytes=limit * 2**20)


def cost(flops, moved):
    return pl.CostEstimate(flops=flops, bytes_accessed=moved, transcendentals=0)


class Plan:
    def __init__(self, size, rows, width, slots):
        self.size, self.rows, self.width = size, rows, width
        self.tile = 2 * size
        self.pairs = rows // self.tile
        self.near = (REACH + 1) // 2
        self.far = slots * size // self.tile
        self.edge = self.near * self.tile
        self.part = width // PARTS
        self.outer = 2 * self.near + self.far
        self.places = 2 * (self.outer + self.pairs)
        self.depth = max(sum(run[2] for run in self.runs(p)) for p in range(self.pairs))

    def outer_range(self, p):
        extra = p + self.near - self.pairs + 1
        return min(p, self.near), self.near + self.far + max(0, extra)

    def own_range(self, p):
        return max(0, p - self.near), min(self.pairs, p + self.near + 1)

    def runs(self, p):
        begin, end = self.outer_range(p)
        rows = (end - begin) * self.tile
        outer = (2 * begin, 0, rows)
        begin, end = self.own_range(p)
        return outer, (2 * (self.outer + begin), rows, (end - begin) * self.tile)

    def mirrored(self, t, side):
        return t + side[0] * (self.pairs - 1 - 2 * t)


def write_far(plan, side, asked, source, write):
    tile, size = plan.tile, plan.size
    lane = lax.broadcasted_iota(jnp.int32, (source.shape[0], tile), 1)

    def block(slot, want):
        index = lax.rem(asked[0, slot] + 2 * plan.pairs, 2 * plan.pairs)
        at = plan.mirrored(lax.div(index, 2), side) * tile
        value = source[:, pl.ds(pl.multiple_of(at, tile), tile)]
        return jnp.where(lax.rem(index, 2) == want, value, pltpu.roll(value, size, 1))

    for t in range(plan.far):
        value = jnp.where(lane < size, block(2 * t, 0), block(2 * t + 1, 1))
        write(t * tile, value)


def write_sends(plan, at, value, to_away, to_near):
    skip = plan.rows - plan.edge
    if at < plan.edge:
        to_away[:, at : at + plan.tile] = value
    if at >= skip:
        to_near[:, at - skip : at - skip + plan.tile] = value


def pack_kernel(plan, chunks, side, natural, turned, *rest):
    sends, staged, sems = rest[:-2], *rest[-2:]
    tile, part, count = plan.tile, plan.part, plan.pairs // chunks
    step = count * tile

    def fetch(c):
        return pltpu.make_async_copy(
            natural.at[pl.ds(c * step, step), :],
            staged.at[pl.ds(c * step, step), :],
            sems.at[c],
        )

    for c in range(chunks):
        fetch(c).start()
    for c in range(chunks):
        fetch(c).wait()
    for t in range(plan.pairs):
        at = pl.multiple_of(plan.mirrored(t, side) * tile, tile)
        value = staged[pl.ds(at, tile), :].T
        at = t * tile
        turned[:, at : at + tile] = value
        for h in range(PARTS):
            rows = slice(h * part, (h + 1) * part)
            write_sends(plan, at, value[rows], *sends[2 * h : 2 * h + 2])


def pack(plan, side, natural):
    edge = jax.ShapeDtypeStruct((plan.part, plan.edge), F32)
    chunks = 4 if plan.pairs % 4 == 0 else 1
    return pl.pallas_call(
        functools.partial(pack_kernel, plan, chunks),
        out_shape=[pltpu.VMEM((plan.width, plan.rows), F32)] + [edge] * (2 * PARTS),
        in_specs=[SMEM, pl.BlockSpec(memory_space=pltpu.HBM)],
        out_specs=[VMEM] * (1 + 2 * PARTS),
        scratch_shapes=[
            pltpu.VMEM((plan.rows, plan.width), F32),
            pltpu.SemaphoreType.DMA((chunks,)),
        ],
        compiler_params=params(8),
        name="pack",
    )(side, pltpu.with_memory_space_constraint(natural, pltpu.HBM))


def far_kernel(plan, side, asked, turned, out):
    def write(at, value):
        out[:, at : at + plan.tile] = value

    write_far(plan, side, asked, turned, write)


def gather_far(plan, side, asked, turned):
    return pl.pallas_call(
        functools.partial(far_kernel, plan),
        out_shape=jax.ShapeDtypeStruct((plan.width, plan.far * plan.tile), F32),
        in_specs=[SMEM, SMEM, VMEM],
        out_specs=VMEM,
        compiler_params=params(8),
        name="far",
    )(side, asked, turned)


def own_halves(plan, vectors, halves):
    tile, width, part = plan.tile, plan.width, plan.part
    for at in range(0, plan.rows, tile):
        for h, ref in enumerate(vectors):
            high, low = split(ref[:, at : at + tile])
            rows = slice(h * ref.shape[0], (h + 1) * ref.shape[0])
            halves[rows, at : at + tile] = high
            halves[width + rows.start : width + rows.stop, at : at + tile] = low


def own_product(plan, p, halves, band, inner):
    begin, end = (plan.tile * bound for bound in plan.own_range(p))
    _, (_, row, rows) = plan.runs(p)
    sums = jnp.dot(
        halves[:, begin:end], band[p, row : row + rows, :], preferred_element_type=F32
    )
    inner[:, p * plan.tile : (p + 1) * plan.tile] = fold(sums)


def band_kernel(plan, depth, side, inverse, ham_t, vectors, band, inner, staged, halves, sems):
    size, tile = plan.size, plan.tile
    lane = lax.broadcasted_iota(jnp.int32, (size, tile), 1)

    def fetch(p):
        at = pl.multiple_of(plan.mirrored(p, side) * tile, tile)
        return pltpu.make_async_copy(
            ham_t.at[:, pl.ds(at, tile)], staged.at[p, pl.ds(0, depth), :], sems.at[p]
        )

    for p in range(plan.pairs):
        fetch(p).start()
    for p in range(plan.pairs):
        staged[p, depth:, :] = jnp.zeros((size, tile), F32)
    own_halves(plan, [vectors], halves)

    for p in range(plan.pairs):
        fetch(p).wait()
        row = 2 * plan.mirrored(p, side)

        def block(q):
            even = pl.multiple_of(inverse[row, q] * size, size)
            odd = pl.multiple_of(inverse[row + 1, q] * size, size)
            first = staged[p, pl.ds(even, size), :]
            second = staged[p, pl.ds(odd, size), :]
            return jnp.where(lane < size, first, second)

        if p > 0:
            own_product(plan, p - 1, halves, band, inner)
        for place, at, rows in plan.runs(p):
            for q in range(rows // size):
                high, low = split(block(place + q))
                lines = slice(at + q * size, at + (q + 1) * size)
                band[p, lines, :tile] = high
                band[p, lines, tile:] = low
    own_product(plan, plan.pairs - 1, halves, band, inner)


def make_band(plan, side, inverse, ham_t, vectors):
    depth, rows = ham_t.shape
    size, tile = plan.size, plan.tile
    return pl.pallas_call(
        functools.partial(band_kernel, plan, depth),
        out_shape=[
            pltpu.VMEM((plan.pairs, plan.depth, 2 * tile), jnp.bfloat16),
            pltpu.VMEM((plan.width, rows), F32),
        ],
        in_specs=[SMEM, SMEM, pl.BlockSpec(memory_space=pltpu.HBM), VMEM],
        out_specs=[VMEM, VMEM],
        scratch_shapes=[
            pltpu.VMEM((plan.pairs, depth + size, tile), F32),
            pltpu.VMEM((2 * plan.width, rows), jnp.bfloat16),
            pltpu.SemaphoreType.DMA((plan.pairs,)),
        ],
        compiler_params=params(14),
        cost_estimate=cost(0, 2 * 4 * depth * rows),
        name="band",
    )(side, inverse, pltpu.with_memory_space_constraint(ham_t, pltpu.HBM), vectors)


def inner_kernel(plan, *refs):
    vectors, band, inner, halves = refs[:PARTS], *refs[PARTS:]
    own_halves(plan, vectors, halves)
    for p in range(plan.pairs):
        own_product(plan, p, halves, band, inner)


def run_inner(plan, vectors, band):
    return pl.pallas_call(
        functools.partial(inner_kernel, plan),
        out_shape=pltpu.VMEM((plan.width, plan.rows), F32),
        in_specs=[VMEM] * (PARTS + 1),
        out_specs=VMEM,
        scratch_shapes=[pltpu.VMEM((2 * plan.width, plan.rows), jnp.bfloat16)],
        compiler_params=params(8),
        cost_estimate=cost(8 * plan.width * plan.rows**2, 0),
        name="inner",
    )(*vectors, band)


def outer_products(plan, h, away, far, near, band, halves):
    tile, part = plan.tile, plan.part
    tiles = [(away, plan.near - 1 - t) for t in range(plan.near)]
    tiles += [(far, t) for t in range(plan.far)]
    tiles += [(near, plan.near - 1 - t) for t in range(plan.near)]
    for t, (ref, source) in enumerate(tiles):
        rows = slice(h * part, (h + 1) * part) if ref.shape[0] > part else slice(None)
        high, low = split(ref[rows, source * tile : (source + 1) * tile])
        halves[:part, t * tile : (t + 1) * tile] = high
        halves[part:, t * tile : (t + 1) * tile] = low
    for p in range(plan.pairs):
        begin, end = (tile * bound for bound in plan.outer_range(p))
        sums = jnp.dot(
            halves[:, begin:end], band[p, : end - begin, :], preferred_element_type=F32
        )
        yield p * tile, fold(sums)


def first_kernel(
    plan, h, side, asked, away, far, near, band, inner, own, value, to_away, to_near, to_far, halves
):
    tile, part = plan.tile, plan.part
    rows = slice(h * part, (h + 1) * part)
    for at, product in outer_products(plan, h, away, far, near, band, halves):
        lanes = slice(at, at + tile)
        shifted = product + inner[rows, lanes] - CENTER * own[rows, lanes]
        term = shifted * (1.0 / HALF_WIDTH)
        value[:, lanes] = term
        write_sends(plan, at, term, to_away, to_near)

    def write(at, term):
        to_far[:, at : at + tile] = term

    write_far(plan, side, asked, value, write)


def run_first(plan, h, side, asked, arrived, band, inner, own):
    edge = jax.ShapeDtypeStruct((plan.part, plan.edge), F32)
    far = jax.ShapeDtypeStruct((plan.part, plan.far * plan.tile), F32)
    return pl.pallas_call(
        functools.partial(first_kernel, plan, h),
        out_shape=[pltpu.VMEM((plan.part, plan.rows), F32), edge, edge, far],
        in_specs=[SMEM] * 2 + [VMEM] * 6,
        out_specs=[VMEM] * 4,
        scratch_shapes=[pltpu.VMEM((2 * plan.part, plan.outer * plan.tile), jnp.bfloat16)],
        compiler_params=params(8),
        cost_estimate=cost(8 * plan.part * plan.rows**2, 0),
        name="first",
    )(side, asked, *arrived, band, inner, own)


def second_kernel(plan, h, side, away, far, near, band, inner, own, start, *rest):
    earlier, out, halves = rest[:-2], *rest[-2:]
    tile, part = plan.tile, plan.part
    rows = slice(h * part, (h + 1) * part)
    for at, product in outer_products(plan, h, away, far, near, band, halves):
        lanes = slice(at, at + tile)
        shifted = product + inner[rows, lanes] - CENTER * own[:, lanes]
        term = 2.0 / HALF_WIDTH * shifted - start[rows, lanes]
        if h < PARTS - 1:
            out[:, lanes] = term
        else:
            whole = [ref[:, lanes] for ref in earlier] + [term]
            place = pl.multiple_of(plan.mirrored(at // tile, side) * tile, tile)
            out[pl.ds(place, tile), :] = jnp.concatenate(whole, axis=0).T


def run_second(plan, h, side, arrived, band, inner, own, start, earlier):
    if h < PARTS - 1:
        out, earlier = pltpu.VMEM((plan.part, plan.rows), F32), []
    else:
        out = jax.ShapeDtypeStruct((plan.rows, plan.width), F32)
    return pl.pallas_call(
        functools.partial(second_kernel, plan, h),
        out_shape=out,
        in_specs=[SMEM] + [VMEM] * (7 + len(earlier)),
        out_specs=VMEM,
        scratch_shapes=[pltpu.VMEM((2 * plan.part, plan.outer * plan.tile), jnp.bfloat16)],
        compiler_params=params(8),
        cost_estimate=cost(8 * plan.part * plan.rows**2, 0),
        name="second",
    )(side, *arrived, band, inner, own, start, *earlier)


def after(value, *others):
    return lax.optimization_barrier((value, *others))[0]


def per_device(hamiltonian, subspace, block_cols, far_list):
    block_rows, entries = block_cols.shape
    size = hamiltonian.shape[1] // entries
    device_count = lax.axis_size("rows")
    first_row = lax.axis_index("rows") * block_rows
    block_total = block_rows * device_count
    swap_level = (device_count // 8).bit_length() - 1
    plan = Plan(size, block_rows * size, subspace.shape[1], far_list.shape[1])

    side = (lax.axis_index("rows") % 2).astype(jnp.int32).reshape(1)

    def exchange(to_away, to_near):
        return swap_chips(to_away, "rows"), partner(to_near, "rows", 0)

    asked = partner(far_list, "rows", swap_level)
    start, *sends = pack(plan, side, subspace)
    listed = gather_far(plan, side, asked, start)
    far = partner(listed, "rows", swap_level)
    arrived = []
    for h in range(PARTS):
        to_away, to_near = sends[2 * h : 2 * h + 2]
        if h > 0:
            to_away, to_near = lax.optimization_barrier((to_away, to_near, listed))[:2]
        away, near = exchange(to_away, to_near)
        arrived.append((away, far, near))

    block_cols = after(block_cols, listed)
    near, far_slots = 2 * plan.near, 2 * plan.far
    shift = (block_cols - first_row + near + block_total) % block_total
    last = block_rows + 2 * near - 2
    shift = shift + side[0] * (last - 4 * (shift // 2))
    places = jnp.where(
        block_cols >= block_total,
        near + block_cols - block_total,
        jnp.where(
            shift < near,
            shift,
            jnp.where(
                shift < near + block_rows,
                shift - near + 2 * plan.outer,
                shift - block_rows + far_slots,
            ),
        ),
    )
    every = jnp.arange(plan.places, dtype=jnp.int32)[None, None, :]
    entry = jnp.arange(entries, dtype=jnp.int32)[None, :, None]
    hit = places[:, :, None] == every
    inverse = entries + jnp.sum(jnp.where(hit, entry - entries, 0), axis=1)

    band, inner = make_band(plan, side, inverse, hamiltonian.T, start)

    values, later = [], []
    for h in range(PARTS):
        if values:
            inner = after(inner, values[-1])
        value, to_away, to_near, listed = run_first(
            plan, h, side, asked, arrived[h], band, inner, start
        )
        values.append(value)
        far = partner(listed, "rows", swap_level)
        away, near = exchange(to_away, to_near)
        later.append((away, far, near))
    inner = run_inner(plan, values, band)
    result = []
    for h in range(PARTS):
        if result:
            inner = after(inner, result[-1])
        out = run_second(plan, h, side, later[h], band, inner, values[h], start, result)
        result.append(out)
    return result[-1]


def solution(mesh):
    placed = (P("rows", None), P("rows", None), P("rows", None), P("rows", None))
    return jax.shard_map(
        per_device, mesh=mesh, in_specs=placed, out_specs=P("rows", None), check_vma=False
    )
```

```python
import functools

import jax
import jax.numpy as jnp
from jax import lax
from jax.experimental import pallas as pl
from jax.experimental.pallas import tpu as pltpu
from jax.sharding import PartitionSpec as P

CENTER = 0.25
HALF_WIDTH = 1.5
REACH = 13
F32 = jnp.float32
VMEM = pl.BlockSpec(memory_space=pltpu.VMEM)
SMEM = pl.BlockSpec(memory_space=pltpu.SMEM)


def partner(value, axis, bit):
    mask = 2**bit
    pairs = [(source, source ^ mask) for source in range(lax.axis_size(axis))]
    return lax.ppermute(value, axis, pairs)


def swap_chips(value, axis):
    devices = lax.axis_size(axis)
    pairs = [(i, (i + (1 if i % 2 else -1)) % devices) for i in range(devices)]
    return lax.ppermute(value, axis, pairs)


def split(value):
    high = value.astype(jnp.bfloat16)
    return high, (value - high.astype(F32)).astype(jnp.bfloat16)


def fold(sums):
    width, tile = sums.shape[0] // 2, sums.shape[1] // 2
    small = sums[width:, tile:] + sums[width:, :tile] + sums[:width, tile:]
    return small + sums[:width, :tile]


def params(limit):
    return pltpu.CompilerParams(vmem_limit_bytes=limit * 2**20)


def cost(flops, moved):
    return pl.CostEstimate(flops=flops, bytes_accessed=moved, transcendentals=0)


class Plan:
    def __init__(self, size, rows, width, slots):
        self.size, self.rows, self.width = size, rows, width
        self.tile = 2 * size
        self.pairs = rows // self.tile
        self.near = (REACH + 1) // 2
        self.far = slots * size // self.tile
        self.edge = self.near * self.tile
        self.half = width // 2
        self.whole = self.edge - self.tile
        self.outer = 2 * self.near + self.far
        self.places = 2 * (self.outer + self.pairs)
        self.depth = max(sum(run[2] for run in self.runs(p)) for p in range(self.pairs))

    def outer_range(self, p):
        extra = p + self.near - self.pairs + 1
        return min(p, self.near), self.near + self.far + max(0, extra)

    def own_range(self, p):
        return max(0, p - self.near), min(self.pairs, p + self.near + 1)

    def runs(self, p):
        begin, end = self.outer_range(p)
        rows = (end - begin) * self.tile
        outer = (2 * begin, 0, rows)
        begin, end = self.own_range(p)
        return outer, (2 * (self.outer + begin), rows, (end - begin) * self.tile)

    def mirrored(self, t, side):
        return t + side[0] * (self.pairs - 1 - 2 * t)


def write_far(plan, side, asked, source, write):
    tile, size = plan.tile, plan.size
    lane = lax.broadcasted_iota(jnp.int32, (source.shape[0], tile), 1)

    def block(slot, want):
        index = lax.rem(asked[0, slot] + 2 * plan.pairs, 2 * plan.pairs)
        at = plan.mirrored(lax.div(index, 2), side) * tile
        value = source[:, pl.ds(pl.multiple_of(at, tile), tile)]
        return jnp.where(lax.rem(index, 2) == want, value, pltpu.roll(value, size, 1))

    for t in range(plan.far):
        value = jnp.where(lane < size, block(2 * t, 0), block(2 * t + 1, 1))
        write(t * tile, value)


def write_sends(plan, side, at, value, sends):
    tile, half, skip = plan.tile, plan.half, plan.rows - plan.edge
    first, second, to_near = sends
    if at < plan.whole:
        first[:, at : at + tile] = value[:half]
        second[:, at : at + tile] = value[half:]
    elif at == plan.whole:
        lane = lax.broadcasted_iota(jnp.int32, (half, tile), 1)
        turned = pltpu.roll(value, plan.size, 1)
        even = jnp.where(lane < plan.size, value[:half], turned[half:])
        odd = jnp.where(lane < plan.size, turned[:half], value[half:])
        first[:, at : at + tile] = jnp.where(side[0] == 0, even, odd)
    if at >= skip:
        to_near[:, at - skip : at - skip + tile] = value


def away_tile(plan, side, first, second, t):
    at = t * plan.tile
    lanes = slice(at, at + plan.tile)
    if at < plan.whole:
        return jnp.concatenate([first[:, lanes], second[:, lanes]], axis=0)
    packed = first[:, lanes]
    turned = pltpu.roll(packed, plan.size, 1)
    even = jnp.concatenate([turned, packed], axis=0)
    odd = jnp.concatenate([packed, turned], axis=0)
    return jnp.where(side[0] == 0, even, odd)


def send_shapes(plan):
    lanes = ((plan.half, plan.edge), (plan.half, plan.whole), (plan.width, plan.edge))
    return [jax.ShapeDtypeStruct(shape, F32) for shape in lanes]


def pack_kernel(plan, chunks, side, natural, turned, *rest):
    sends, staged, sems = rest[:-2], *rest[-2:]
    tile, count = plan.tile, plan.pairs // chunks
    step = count * tile

    def fetch(c):
        return pltpu.make_async_copy(
            natural.at[pl.ds(c * step, step), :],
            staged.at[pl.ds(c * step, step), :],
            sems.at[c],
        )

    for c in range(chunks):
        fetch(c).start()
    for c in range(chunks):
        fetch(c).wait()
    for t in range(plan.pairs):
        at = pl.multiple_of(plan.mirrored(t, side) * tile, tile)
        value = staged[pl.ds(at, tile), :].T
        turned[:, t * tile : (t + 1) * tile] = value
        write_sends(plan, side, t * tile, value, sends)


def pack(plan, side, natural):
    chunks = 4 if plan.pairs % 4 == 0 else 1
    return pl.pallas_call(
        functools.partial(pack_kernel, plan, chunks),
        out_shape=[pltpu.VMEM((plan.width, plan.rows), F32)] + send_shapes(plan),
        in_specs=[SMEM, pl.BlockSpec(memory_space=pltpu.HBM)],
        out_specs=[VMEM] * 4,
        scratch_shapes=[
            pltpu.VMEM((plan.rows, plan.width), F32),
            pltpu.SemaphoreType.DMA((chunks,)),
        ],
        compiler_params=params(8),
        name="pack",
    )(side, pltpu.with_memory_space_constraint(natural, pltpu.HBM))


def far_kernel(plan, side, asked, turned, out):
    def write(at, value):
        out[:, at : at + plan.tile] = value

    write_far(plan, side, asked, turned, write)


def gather_far(plan, side, asked, turned):
    return pl.pallas_call(
        functools.partial(far_kernel, plan),
        out_shape=jax.ShapeDtypeStruct((plan.width, plan.far * plan.tile), F32),
        in_specs=[SMEM, SMEM, VMEM],
        out_specs=VMEM,
        compiler_params=params(8),
        name="far",
    )(side, asked, turned)


def own_halves(plan, vectors, halves):
    for at in range(0, plan.rows, plan.tile):
        high, low = split(vectors[:, at : at + plan.tile])
        halves[: plan.width, at : at + plan.tile] = high
        halves[plan.width :, at : at + plan.tile] = low


def own_product(plan, p, halves, band, inner):
    begin, end = (plan.tile * bound for bound in plan.own_range(p))
    _, (_, row, rows) = plan.runs(p)
    sums = jnp.dot(
        halves[:, begin:end], band[p, row : row + rows, :], preferred_element_type=F32
    )
    inner[:, p * plan.tile : (p + 1) * plan.tile] = fold(sums)


def band_kernel(plan, depth, side, inverse, ham_t, vectors, band, inner, staged, halves, sems):
    size, tile = plan.size, plan.tile
    lane = lax.broadcasted_iota(jnp.int32, (size, tile), 1)

    def fetch(p):
        at = pl.multiple_of(plan.mirrored(p, side) * tile, tile)
        return pltpu.make_async_copy(
            ham_t.at[:, pl.ds(at, tile)], staged.at[p, pl.ds(0, depth), :], sems.at[p]
        )

    for p in range(plan.pairs):
        fetch(p).start()
    for p in range(plan.pairs):
        staged[p, depth:, :] = jnp.zeros((size, tile), F32)
    own_halves(plan, vectors, halves)

    for p in range(plan.pairs):
        fetch(p).wait()
        row = 2 * plan.mirrored(p, side)

        def block(q):
            even = pl.multiple_of(inverse[row, q] * size, size)
            odd = pl.multiple_of(inverse[row + 1, q] * size, size)
            first = staged[p, pl.ds(even, size), :]
            second = staged[p, pl.ds(odd, size), :]
            return jnp.where(lane < size, first, second)

        if p > 0:
            own_product(plan, p - 1, halves, band, inner)
        for place, at, rows in plan.runs(p):
            for q in range(rows // size):
                high, low = split(block(place + q))
                lines = slice(at + q * size, at + (q + 1) * size)
                band[p, lines, :tile] = high
                band[p, lines, tile:] = low
    own_product(plan, plan.pairs - 1, halves, band, inner)


def make_band(plan, side, inverse, ham_t, vectors):
    depth, rows = ham_t.shape
    size, tile = plan.size, plan.tile
    return pl.pallas_call(
        functools.partial(band_kernel, plan, depth),
        out_shape=[
            pltpu.VMEM((plan.pairs, plan.depth, 2 * tile), jnp.bfloat16),
            pltpu.VMEM((plan.width, rows), F32),
        ],
        in_specs=[SMEM, SMEM, pl.BlockSpec(memory_space=pltpu.HBM), VMEM],
        out_specs=[VMEM, VMEM],
        scratch_shapes=[
            pltpu.VMEM((plan.pairs, depth + size, tile), F32),
            pltpu.VMEM((2 * plan.width, rows), jnp.bfloat16),
            pltpu.SemaphoreType.DMA((plan.pairs,)),
        ],
        compiler_params=params(14),
        cost_estimate=cost(0, 2 * 4 * depth * rows),
        name="band",
    )(side, inverse, pltpu.with_memory_space_constraint(ham_t, pltpu.HBM), vectors)


def inner_kernel(plan, vectors, band, inner, halves):
    own_halves(plan, vectors, halves)
    for p in range(plan.pairs):
        own_product(plan, p, halves, band, inner)


def run_inner(plan, vectors, band):
    return pl.pallas_call(
        functools.partial(inner_kernel, plan),
        out_shape=pltpu.VMEM((plan.width, plan.rows), F32),
        in_specs=[VMEM] * 2,
        out_specs=VMEM,
        scratch_shapes=[pltpu.VMEM((2 * plan.width, plan.rows), jnp.bfloat16)],
        compiler_params=params(8),
        cost_estimate=cost(8 * plan.width * plan.rows**2, 0),
        name="inner",
    )(vectors, band)


def outer_products(plan, side, first, second, far, near, band, halves):
    tile, width = plan.tile, plan.width
    tiles = [lambda t=t: away_tile(plan, side, first, second, t) for t in range(plan.near)][::-1]
    tiles += [lambda t=t: far[:, t * tile : (t + 1) * tile] for t in range(plan.far)]
    tiles += [lambda t=t: near[:, t * tile : (t + 1) * tile] for t in range(plan.near)][::-1]
    for t, read in enumerate(tiles):
        high, low = split(read())
        halves[:width, t * tile : (t + 1) * tile] = high
        halves[width:, t * tile : (t + 1) * tile] = low
    for p in range(plan.pairs):
        begin, end = (tile * bound for bound in plan.outer_range(p))
        sums = jnp.dot(
            halves[:, begin:end], band[p, : end - begin, :], preferred_element_type=F32
        )
        yield p * tile, fold(sums)


def first_kernel(
    plan, side, asked, first, second, far, near, band, inner, own, value, to_far, *rest
):
    sends, halves = rest[:-1], rest[-1]
    tile = plan.tile
    for at, product in outer_products(plan, side, first, second, far, near, band, halves):
        lanes = slice(at, at + tile)
        shifted = product + inner[:, lanes] - CENTER * own[:, lanes]
        term = shifted * (1.0 / HALF_WIDTH)
        value[:, lanes] = term
        write_sends(plan, side, at, term, sends)

    def write(at, term):
        to_far[:, at : at + tile] = term

    write_far(plan, side, asked, value, write)


def run_first(plan, side, asked, arrived, band, inner, own):
    far = jax.ShapeDtypeStruct((plan.width, plan.far * plan.tile), F32)
    return pl.pallas_call(
        functools.partial(first_kernel, plan),
        out_shape=[pltpu.VMEM((plan.width, plan.rows), F32), far] + send_shapes(plan),
        in_specs=[SMEM] * 2 + [VMEM] * 7,
        out_specs=[VMEM] * 5,
        scratch_shapes=[pltpu.VMEM((2 * plan.width, plan.outer * plan.tile), jnp.bfloat16)],
        compiler_params=params(8),
        cost_estimate=cost(8 * plan.width * plan.rows**2, 0),
        name="first",
    )(side, asked, *arrived, band, inner, own)


def second_kernel(plan, side, first, second, far, near, band, inner, own, start, out, halves):
    tile = plan.tile
    for at, product in outer_products(plan, side, first, second, far, near, band, halves):
        lanes = slice(at, at + tile)
        shifted = product + inner[:, lanes] - CENTER * own[:, lanes]
        term = 2.0 / HALF_WIDTH * shifted - start[:, lanes]
        place = pl.multiple_of(plan.mirrored(at // tile, side) * tile, tile)
        out[pl.ds(place, tile), :] = term.T


def run_second(plan, side, arrived, band, inner, own, start):
    return pl.pallas_call(
        functools.partial(second_kernel, plan),
        out_shape=jax.ShapeDtypeStruct((plan.rows, plan.width), F32),
        in_specs=[SMEM] + [VMEM] * 8,
        out_specs=VMEM,
        scratch_shapes=[pltpu.VMEM((2 * plan.width, plan.outer * plan.tile), jnp.bfloat16)],
        compiler_params=params(8),
        cost_estimate=cost(8 * plan.width * plan.rows**2, 0),
        name="second",
    )(side, *arrived, band, inner, own, start)


def after(value, *others):
    return lax.optimization_barrier((value, *others))[0]


def per_device(hamiltonian, subspace, block_cols, far_list):
    block_rows, entries = block_cols.shape
    size = hamiltonian.shape[1] // entries
    device_count = lax.axis_size("rows")
    first_row = lax.axis_index("rows") * block_rows
    block_total = block_rows * device_count
    swap_level = (device_count // 8).bit_length() - 1
    plan = Plan(size, block_rows * size, subspace.shape[1], far_list.shape[1])

    side = (lax.axis_index("rows") % 2).astype(jnp.int32).reshape(1)

    def exchange(listed, sends):
        far = partner(listed, "rows", swap_level)
        first, second = (swap_chips(value, "rows") for value in sends[:2])
        return first, second, far, partner(sends[2], "rows", 0)

    asked = partner(far_list, "rows", swap_level)
    start, *sends = pack(plan, side, subspace)
    listed = gather_far(plan, side, asked, start)
    arrived = exchange(listed, sends)

    block_cols = after(block_cols, listed)
    near, far_slots = 2 * plan.near, 2 * plan.far
    shift = (block_cols - first_row + near + block_total) % block_total
    last = block_rows + 2 * near - 2
    shift = shift + side[0] * (last - 4 * (shift // 2))
    places = jnp.where(
        block_cols >= block_total,
        near + block_cols - block_total,
        jnp.where(
            shift < near,
            shift,
            jnp.where(
                shift < near + block_rows,
                shift - near + 2 * plan.outer,
                shift - block_rows + far_slots,
            ),
        ),
    )
    every = jnp.arange(plan.places, dtype=jnp.int32)[None, None, :]
    entry = jnp.arange(entries, dtype=jnp.int32)[None, :, None]
    hit = places[:, :, None] == every
    inverse = entries + jnp.sum(jnp.where(hit, entry - entries, 0), axis=1)

    band, inner = make_band(plan, side, inverse, hamiltonian.T, start)

    value, listed, *sends = run_first(plan, side, asked, arrived, band, inner, start)
    arrived = exchange(listed, sends)
    inner = run_inner(plan, value, band)
    return run_second(plan, side, arrived, band, inner, value, start)


def solution(mesh):
    placed = (P("rows", None), P("rows", None), P("rows", None), P("rows", None))
    return jax.shard_map(
        per_device, mesh=mesh, in_specs=placed, out_specs=P("rows", None), check_vma=False
    )
```

```python
import functools

import jax
import jax.numpy as jnp
from jax import lax
from jax.experimental import pallas as pl
from jax.experimental.pallas import tpu as pltpu
from jax.sharding import PartitionSpec as P

CENTER = 0.25
HALF_WIDTH = 1.5
REACH = 13
F32 = jnp.float32
VMEM = pl.BlockSpec(memory_space=pltpu.VMEM)
HBM = pl.BlockSpec(memory_space=pltpu.HBM)
SMEM = pl.BlockSpec(memory_space=pltpu.SMEM)


def partner(value, axis, bit):
    mask = 2**bit
    pairs = [(source, source ^ mask) for source in range(lax.axis_size(axis))]
    return lax.ppermute(value, axis, pairs)


def swap_chips(value, axis):
    devices = lax.axis_size(axis)
    pairs = [(i, (i + (1 if i % 2 else -1)) % devices) for i in range(devices)]
    return lax.ppermute(value, axis, pairs)


def split(value):
    high = value.astype(jnp.bfloat16)
    return high, (value - high.astype(F32)).astype(jnp.bfloat16)


def fold(sums):
    width, tile = sums.shape[0] // 2, sums.shape[1] // 2
    small = sums[width:, tile:] + sums[width:, :tile] + sums[:width, tile:]
    return small + sums[:width, :tile]


def params(limit):
    return pltpu.CompilerParams(vmem_limit_bytes=limit * 2**20)


def cost(flops, moved):
    return pl.CostEstimate(flops=flops, bytes_accessed=moved, transcendentals=0)


class Plan:
    def __init__(self, size, rows, width, slots):
        self.size, self.rows, self.width = size, rows, width
        self.tile = 2 * size
        self.pairs = rows // self.tile
        self.near = (REACH + 1) // 2
        self.far = slots * size // self.tile
        self.edge = self.near * self.tile
        self.half = width // 2
        self.whole = self.edge - self.tile
        self.outer = 2 * self.near + self.far
        self.places = 2 * (self.outer + self.pairs)
        self.depth = max(sum(run[2] for run in self.runs(p)) for p in range(self.pairs))

    def outer_range(self, p):
        extra = p + self.near - self.pairs + 1
        return min(p, self.near), self.near + self.far + max(0, extra)

    def own_range(self, p):
        return max(0, p - self.near), min(self.pairs, p + self.near + 1)

    def runs(self, p):
        begin, end = self.outer_range(p)
        rows = (end - begin) * self.tile
        outer = (2 * begin, 0, rows)
        begin, end = self.own_range(p)
        return outer, (2 * (self.outer + begin), rows, (end - begin) * self.tile)

    def mirrored(self, t, side):
        return t + side[0] * (self.pairs - 1 - 2 * t)


def write_far(plan, side, asked, source, write):
    tile, size = plan.tile, plan.size
    lane = lax.broadcasted_iota(jnp.int32, (source.shape[0], tile), 1)

    def block(slot, want):
        index = lax.rem(asked[0, slot] + 2 * plan.pairs, 2 * plan.pairs)
        at = plan.mirrored(lax.div(index, 2), side) * tile
        value = source[:, pl.ds(pl.multiple_of(at, tile), tile)]
        return jnp.where(lax.rem(index, 2) == want, value, pltpu.roll(value, size, 1))

    for t in range(plan.far):
        value = jnp.where(lane < size, block(2 * t, 0), block(2 * t + 1, 1))
        write(t * tile, value)


def write_sends(plan, side, at, value, sends):
    tile, half, skip = plan.tile, plan.half, plan.rows - plan.edge
    to_away, to_near = sends
    if at < plan.whole:
        to_away[:, at : at + tile] = value[:half]
        to_away[:, plan.edge + at : plan.edge + at + tile] = value[half:]
    elif at == plan.whole:
        lane = lax.broadcasted_iota(jnp.int32, (half, tile), 1)
        turned = pltpu.roll(value, plan.size, 1)
        even = jnp.where(lane < plan.size, value[:half], turned[half:])
        odd = jnp.where(lane < plan.size, turned[:half], value[half:])
        to_away[:, at : at + tile] = jnp.where(side[0] == 0, even, odd)
    if at >= skip:
        to_near[:, at - skip : at - skip + tile] = value


def away_tile(plan, side, away, t):
    at, tile = t * plan.tile, plan.tile
    packed = away[:, at : at + tile]
    if at < plan.whole:
        rest = away[:, plan.edge + at : plan.edge + at + tile]
        return jnp.concatenate([packed, rest], axis=0)
    turned = pltpu.roll(packed, plan.size, 1)
    even = jnp.concatenate([turned, packed], axis=0)
    odd = jnp.concatenate([packed, turned], axis=0)
    return jnp.where(side[0] == 0, even, odd)


def send_shapes(plan):
    lanes = ((plan.half, plan.edge + plan.whole), (plan.width, plan.edge))
    return [jax.ShapeDtypeStruct(shape, F32) for shape in lanes]


def pack_kernel(plan, chunks, side, natural, turned, *rest):
    sends, staged, sems = rest[:-2], *rest[-2:]
    tile, count = plan.tile, plan.pairs // chunks
    step = count * tile

    def fetch(c):
        return pltpu.make_async_copy(
            natural.at[pl.ds(c * step, step), :],
            staged.at[pl.ds(c * step, step), :],
            sems.at[c],
        )

    for c in range(chunks):
        fetch(c).start()
    for c in range(chunks):
        fetch(c).wait()
    for t in range(plan.pairs):
        at = pl.multiple_of(plan.mirrored(t, side) * tile, tile)
        value = staged[pl.ds(at, tile), :].T
        turned[:, t * tile : (t + 1) * tile] = value
        write_sends(plan, side, t * tile, value, sends)


def pack(plan, side, natural):
    chunks = 4 if plan.pairs % 4 == 0 else 1
    return pl.pallas_call(
        functools.partial(pack_kernel, plan, chunks),
        out_shape=[pltpu.VMEM((plan.width, plan.rows), F32)] + send_shapes(plan),
        in_specs=[SMEM, HBM],
        out_specs=[VMEM] * 3,
        scratch_shapes=[
            pltpu.VMEM((plan.rows, plan.width), F32),
            pltpu.SemaphoreType.DMA((chunks,)),
        ],
        compiler_params=params(8),
        name="pack",
    )(side, pltpu.with_memory_space_constraint(natural, pltpu.HBM))


def far_kernel(plan, side, asked, turned, out):
    def write(at, value):
        out[:, at : at + plan.tile] = value

    write_far(plan, side, asked, turned, write)


def gather_far(plan, side, asked, turned):
    return pl.pallas_call(
        functools.partial(far_kernel, plan),
        out_shape=jax.ShapeDtypeStruct((plan.width, plan.far * plan.tile), F32),
        in_specs=[SMEM, SMEM, VMEM],
        out_specs=VMEM,
        compiler_params=params(8),
        name="far",
    )(side, asked, turned)


def own_halves(plan, vectors, halves):
    for at in range(0, plan.rows, plan.tile):
        high, low = split(vectors[:, at : at + plan.tile])
        halves[: plan.width, at : at + plan.tile] = high
        halves[plan.width :, at : at + plan.tile] = low


def own_product(plan, p, halves, band, inner):
    begin, end = (plan.tile * bound for bound in plan.own_range(p))
    _, (_, row, rows) = plan.runs(p)
    sums = jnp.dot(
        halves[:, begin:end], band[p, row : row + rows, :], preferred_element_type=F32
    )
    inner[:, p * plan.tile : (p + 1) * plan.tile] = fold(sums)


def band_kernel(plan, depth, side, inverse, ham_t, vectors, band, inner, staged, halves, sems):
    size, tile = plan.size, plan.tile
    lane = lax.broadcasted_iota(jnp.int32, (size, tile), 1)

    def fetch(p):
        at = pl.multiple_of(plan.mirrored(p, side) * tile, tile)
        return pltpu.make_async_copy(
            ham_t.at[:, pl.ds(at, tile)], staged.at[p, pl.ds(0, depth), :], sems.at[p]
        )

    for p in range(plan.pairs):
        fetch(p).start()
    for p in range(plan.pairs):
        staged[p, depth:, :] = jnp.zeros((size, tile), F32)
    own_halves(plan, vectors, halves)

    for p in range(plan.pairs):
        fetch(p).wait()
        row = 2 * plan.mirrored(p, side)

        def block(q):
            even = pl.multiple_of(inverse[row, q] * size, size)
            odd = pl.multiple_of(inverse[row + 1, q] * size, size)
            first = staged[p, pl.ds(even, size), :]
            second = staged[p, pl.ds(odd, size), :]
            return jnp.where(lane < size, first, second)

        if p > 0:
            own_product(plan, p - 1, halves, band, inner)
        for place, at, rows in plan.runs(p):
            for q in range(rows // size):
                high, low = split(block(place + q))
                lines = slice(at + q * size, at + (q + 1) * size)
                band[p, lines, :tile] = high
                band[p, lines, tile:] = low
    own_product(plan, plan.pairs - 1, halves, band, inner)


def make_band(plan, side, inverse, ham_t, vectors):
    depth, rows = ham_t.shape
    size, tile = plan.size, plan.tile
    return pl.pallas_call(
        functools.partial(band_kernel, plan, depth),
        out_shape=[
            pltpu.VMEM((plan.pairs, plan.depth, 2 * tile), jnp.bfloat16),
            pltpu.VMEM((plan.width, rows), F32),
        ],
        in_specs=[SMEM, SMEM, HBM, VMEM],
        out_specs=[VMEM, VMEM],
        scratch_shapes=[
            pltpu.VMEM((plan.pairs, depth + size, tile), F32),
            pltpu.VMEM((2 * plan.width, rows), jnp.bfloat16),
            pltpu.SemaphoreType.DMA((plan.pairs,)),
        ],
        compiler_params=params(14),
        cost_estimate=cost(0, 2 * 4 * depth * rows),
        name="band",
    )(side, inverse, pltpu.with_memory_space_constraint(ham_t, pltpu.HBM), vectors)


def inner_kernel(plan, vectors, band, inner, halves):
    own_halves(plan, vectors, halves)
    for p in range(plan.pairs):
        own_product(plan, p, halves, band, inner)


def run_inner(plan, vectors, band):
    return pl.pallas_call(
        functools.partial(inner_kernel, plan),
        out_shape=pltpu.VMEM((plan.width, plan.rows), F32),
        in_specs=[VMEM] * 2,
        out_specs=VMEM,
        scratch_shapes=[pltpu.VMEM((2 * plan.width, plan.rows), jnp.bfloat16)],
        compiler_params=params(8),
        cost_estimate=cost(8 * plan.width * plan.rows**2, 0),
        name="inner",
    )(vectors, band)


def outer_products(plan, side, away, far, near, band, halves, near_held, sem):
    tile, width, edge = plan.tile, plan.width, plan.near
    copy = pltpu.make_async_copy(near.at[1 - side[0]], near_held, sem)
    copy.start()

    def put(t, value):
        high, low = split(value)
        halves[:width, t * tile : (t + 1) * tile] = high
        halves[width:, t * tile : (t + 1) * tile] = low

    for t in range(edge):
        put(edge - 1 - t, away_tile(plan, side, away, t))
    for t in range(plan.far):
        put(edge + t, far[:, t * tile : (t + 1) * tile])
    waited = False
    for p in range(plan.pairs):
        begin, end = plan.outer_range(p)
        if end > edge + plan.far and not waited:
            copy.wait()
            for t in range(edge):
                put(plan.outer - 1 - t, near_held[:, t * tile : (t + 1) * tile])
            waited = True
        begin, end = begin * tile, end * tile
        sums = jnp.dot(
            halves[:, begin:end], band[p, : end - begin, :], preferred_element_type=F32
        )
        yield p * tile, fold(sums)


def outer_scratch(plan):
    return [
        pltpu.VMEM((2 * plan.width, plan.outer * plan.tile), jnp.bfloat16),
        pltpu.VMEM((plan.width, plan.edge), F32),
        pltpu.SemaphoreType.DMA,
    ]


def in_hbm(arrived):
    away, far, near = arrived
    return away, far, pltpu.with_memory_space_constraint(near, pltpu.HBM)


def first_kernel(
    plan, side, asked, away, far, near, band, inner, own, value, to_far, *rest
):
    sends, held = rest[:2], rest[2:]
    tile = plan.tile
    for at, product in outer_products(plan, side, away, far, near, band, *held):
        lanes = slice(at, at + tile)
        shifted = product + inner[:, lanes] - CENTER * own[:, lanes]
        term = shifted * (1.0 / HALF_WIDTH)
        value[:, lanes] = term
        write_sends(plan, side, at, term, sends)

    def write(at, term):
        to_far[:, at : at + tile] = term

    write_far(plan, side, asked, value, write)


def run_first(plan, side, asked, arrived, band, inner, own):
    far = jax.ShapeDtypeStruct((plan.width, plan.far * plan.tile), F32)
    return pl.pallas_call(
        functools.partial(first_kernel, plan),
        out_shape=[pltpu.VMEM((plan.width, plan.rows), F32), far] + send_shapes(plan),
        in_specs=[SMEM] * 2 + [VMEM] * 2 + [HBM] + [VMEM] * 3,
        out_specs=[VMEM] * 4,
        scratch_shapes=outer_scratch(plan),
        compiler_params=params(8),
        cost_estimate=cost(8 * plan.width * plan.rows**2, 0),
        name="first",
    )(side, asked, *in_hbm(arrived), band, inner, own)


def second_kernel(plan, side, away, far, near, band, inner, own, start, out, *held):
    tile = plan.tile
    for at, product in outer_products(plan, side, away, far, near, band, *held):
        lanes = slice(at, at + tile)
        shifted = product + inner[:, lanes] - CENTER * own[:, lanes]
        term = 2.0 / HALF_WIDTH * shifted - start[:, lanes]
        place = pl.multiple_of(plan.mirrored(at // tile, side) * tile, tile)
        out[pl.ds(place, tile), :] = term.T


def run_second(plan, side, arrived, band, inner, own, start):
    return pl.pallas_call(
        functools.partial(second_kernel, plan),
        out_shape=jax.ShapeDtypeStruct((plan.rows, plan.width), F32),
        in_specs=[SMEM] + [VMEM] * 2 + [HBM] + [VMEM] * 4,
        out_specs=VMEM,
        scratch_shapes=outer_scratch(plan),
        compiler_params=params(8),
        cost_estimate=cost(8 * plan.width * plan.rows**2, 0),
        name="second",
    )(side, *in_hbm(arrived), band, inner, own, start)


def after(value, *others):
    return lax.optimization_barrier((value, *others))[0]


def per_device(hamiltonian, subspace, block_cols, far_list):
    block_rows, entries = block_cols.shape
    size = hamiltonian.shape[1] // entries
    device_count = lax.axis_size("rows")
    first_row = lax.axis_index("rows") * block_rows
    block_total = block_rows * device_count
    swap_level = (device_count // 8).bit_length() - 1
    plan = Plan(size, block_rows * size, subspace.shape[1], far_list.shape[1])

    side = (lax.axis_index("rows") % 2).astype(jnp.int32).reshape(1)

    def exchange(listed, sends):
        far = partner(listed, "rows", swap_level)
        to_away, to_near = sends
        pairs = [[i, i + 1] for i in range(0, device_count, 2)]
        near = lax.all_gather(to_near, "rows", axis_index_groups=pairs)
        return swap_chips(to_away, "rows"), far, near

    asked = partner(far_list, "rows", swap_level)
    start, *sends = pack(plan, side, subspace)
    listed = gather_far(plan, side, asked, start)
    arrived = exchange(listed, sends)

    block_cols = after(block_cols, listed)
    near, far_slots = 2 * plan.near, 2 * plan.far
    shift = (block_cols - first_row + near + block_total) % block_total
    last = block_rows + 2 * near - 2
    shift = shift + side[0] * (last - 4 * (shift // 2))
    places = jnp.where(
        block_cols >= block_total,
        near + block_cols - block_total,
        jnp.where(
            shift < near,
            shift,
            jnp.where(
                shift < near + block_rows,
                shift - near + 2 * plan.outer,
                shift - block_rows + far_slots,
            ),
        ),
    )
    every = jnp.arange(plan.places, dtype=jnp.int32)[None, None, :]
    entry = jnp.arange(entries, dtype=jnp.int32)[None, :, None]
    hit = places[:, :, None] == every
    inverse = entries + jnp.sum(jnp.where(hit, entry - entries, 0), axis=1)

    band, inner = make_band(plan, side, inverse, hamiltonian.T, start)

    value, listed, *sends = run_first(plan, side, asked, arrived, band, inner, start)
    arrived = exchange(listed, sends)
    inner = run_inner(plan, value, band)
    return run_second(plan, side, arrived, band, inner, value, start)


def solution(mesh):
    placed = (P("rows", None), P("rows", None), P("rows", None), P("rows", None))
    return jax.shard_map(
        per_device, mesh=mesh, in_specs=placed, out_specs=P("rows", None), check_vma=False
    )
```

```python
import functools

import jax
import jax.numpy as jnp
from jax import lax
from jax.experimental import pallas as pl
from jax.experimental.pallas import tpu as pltpu
from jax.sharding import PartitionSpec as P

CENTER = 0.25
HALF_WIDTH = 1.5
REACH = 13
F32 = jnp.float32
VMEM = pl.BlockSpec(memory_space=pltpu.VMEM)
SMEM = pl.BlockSpec(memory_space=pltpu.SMEM)


def partner(value, axis, bit):
    mask = 2**bit
    pairs = [(source, source ^ mask) for source in range(lax.axis_size(axis))]
    return lax.ppermute(value, axis, pairs)


def swap_chips(value, axis):
    devices = lax.axis_size(axis)
    pairs = [(i, (i + (1 if i % 2 else -1)) % devices) for i in range(devices)]
    return lax.ppermute(value, axis, pairs)


def split(value):
    high = value.astype(jnp.bfloat16)
    return high, (value - high.astype(F32)).astype(jnp.bfloat16)


def fold(sums):
    width, tile = sums.shape[0] // 2, sums.shape[1] // 2
    small = sums[width:, tile:] + sums[width:, :tile] + sums[:width, tile:]
    return small + sums[:width, :tile]


def params(limit):
    return pltpu.CompilerParams(vmem_limit_bytes=limit * 2**20)


def cost(flops, moved):
    return pl.CostEstimate(flops=flops, bytes_accessed=moved, transcendentals=0)


class Plan:
    def __init__(self, size, rows, width, slots):
        self.size, self.rows, self.width = size, rows, width
        self.tile = 2 * size
        self.pairs = rows // self.tile
        self.near = (REACH + 1) // 2
        self.far = slots * size // self.tile
        self.edge = self.near * self.tile
        self.half = width // 2
        self.whole = self.edge - self.tile
        self.outer = 2 * self.near + self.far
        self.places = 2 * (self.outer + self.pairs)
        self.depth = max(sum(run[2] for run in self.runs(p)) for p in range(self.pairs))

    def outer_range(self, p):
        extra = p + self.near - self.pairs + 1
        return min(p, self.near), self.near + self.far + max(0, extra)

    def spans(self, p):
        begin, end = self.outer_range(p)
        row = self.near - begin
        return {
            "away": (begin, self.near, 0),
            "far": (0, self.far, row),
            "near": (0, end - self.near - self.far, row + self.far),
        }

    def own_range(self, p):
        return max(0, p - self.near), min(self.pairs, p + self.near + 1)

    def runs(self, p):
        begin, end = self.outer_range(p)
        rows = (end - begin) * self.tile
        outer = (2 * begin, 0, rows)
        begin, end = self.own_range(p)
        return outer, (2 * (self.outer + begin), rows, (end - begin) * self.tile)

    def mirrored(self, t, side):
        return t + side[0] * (self.pairs - 1 - 2 * t)


def write_far(plan, side, asked, source, write):
    tile, size = plan.tile, plan.size
    lane = lax.broadcasted_iota(jnp.int32, (source.shape[0], tile), 1)

    def block(slot, want):
        index = lax.rem(asked[0, slot] + 2 * plan.pairs, 2 * plan.pairs)
        at = plan.mirrored(lax.div(index, 2), side) * tile
        value = source[:, pl.ds(pl.multiple_of(at, tile), tile)]
        return jnp.where(lax.rem(index, 2) == want, value, pltpu.roll(value, size, 1))

    for t in range(plan.far):
        value = jnp.where(lane < size, block(2 * t, 0), block(2 * t + 1, 1))
        write(t * tile, value)


def write_sends(plan, side, at, value, to_away, to_near):
    tile, half, skip = plan.tile, plan.half, plan.rows - plan.edge
    if at < plan.whole:
        to_away[:, at : at + tile] = value[:half]
        to_away[:, plan.edge + at : plan.edge + at + tile] = value[half:]
    elif at == plan.whole:
        lane = lax.broadcasted_iota(jnp.int32, (half, tile), 1)
        turned = pltpu.roll(value, plan.size, 1)
        even = jnp.where(lane < plan.size, value[:half], turned[half:])
        odd = jnp.where(lane < plan.size, turned[:half], value[half:])
        to_away[:, at : at + tile] = jnp.where(side[0] == 0, even, odd)
    if at >= skip:
        to_near[:, at - skip : at - skip + tile] = value


def away_tile(plan, side, away, t):
    at, tile = t * plan.tile, plan.tile
    packed = away[:, at : at + tile]
    if at < plan.whole:
        rest = away[:, plan.edge + at : plan.edge + at + tile]
        return jnp.concatenate([packed, rest], axis=0)
    turned = pltpu.roll(packed, plan.size, 1)
    even = jnp.concatenate([turned, packed], axis=0)
    odd = jnp.concatenate([packed, turned], axis=0)
    return jnp.where(side[0] == 0, even, odd)


def send_shapes(plan):
    shapes = ((plan.half, plan.edge + plan.whole), (plan.width, plan.edge))
    return [jax.ShapeDtypeStruct(shape, F32) for shape in shapes]


def pack_kernel(plan, chunks, side, natural, turned, *rest):
    sends, staged, sems = rest[:-2], *rest[-2:]
    tile, count = plan.tile, plan.pairs // chunks
    step = count * tile

    def fetch(c):
        return pltpu.make_async_copy(
            natural.at[pl.ds(c * step, step), :],
            staged.at[pl.ds(c * step, step), :],
            sems.at[c],
        )

    for c in range(chunks):
        fetch(c).start()
    for c in range(chunks):
        fetch(c).wait()
    for t in range(plan.pairs):
        at = pl.multiple_of(plan.mirrored(t, side) * tile, tile)
        value = staged[pl.ds(at, tile), :].T
        turned[:, t * tile : (t + 1) * tile] = value
        write_sends(plan, side, t * tile, value, *sends)


def pack(plan, side, natural):
    chunks = 4 if plan.pairs % 4 == 0 else 1
    return pl.pallas_call(
        functools.partial(pack_kernel, plan, chunks),
        out_shape=[pltpu.VMEM((plan.width, plan.rows), F32)] + send_shapes(plan),
        in_specs=[SMEM, pl.BlockSpec(memory_space=pltpu.HBM)],
        out_specs=[VMEM] * 3,
        scratch_shapes=[
            pltpu.VMEM((plan.rows, plan.width), F32),
            pltpu.SemaphoreType.DMA((chunks,)),
        ],
        compiler_params=params(8),
        name="pack",
    )(side, pltpu.with_memory_space_constraint(natural, pltpu.HBM))


def far_kernel(plan, side, asked, turned, out):
    def write(at, value):
        out[:, at : at + plan.tile] = value

    write_far(plan, side, asked, turned, write)


def gather_far(plan, side, asked, turned):
    return pl.pallas_call(
        functools.partial(far_kernel, plan),
        out_shape=jax.ShapeDtypeStruct((plan.width, plan.far * plan.tile), F32),
        in_specs=[SMEM, SMEM, VMEM],
        out_specs=VMEM,
        compiler_params=params(8),
        name="far",
    )(side, asked, turned)


def own_halves(plan, vectors, halves):
    for at in range(0, plan.rows, plan.tile):
        high, low = split(vectors[:, at : at + plan.tile])
        halves[: plan.width, at : at + plan.tile] = high
        halves[plan.width :, at : at + plan.tile] = low


def own_product(plan, p, halves, band, inner):
    begin, end = (plan.tile * bound for bound in plan.own_range(p))
    _, (_, row, rows) = plan.runs(p)
    sums = jnp.dot(
        halves[:, begin:end], band[p, row : row + rows, :], preferred_element_type=F32
    )
    inner[:, p * plan.tile : (p + 1) * plan.tile] = fold(sums)


def band_kernel(plan, depth, side, inverse, ham_t, vectors, band, inner, staged, halves, sems):
    size, tile = plan.size, plan.tile
    slots = staged.shape[0]
    ahead = slots - 1
    lane = lax.broadcasted_iota(jnp.int32, (size, tile), 1)

    def fetch(p):
        at = pl.multiple_of(plan.mirrored(p, side) * tile, tile)
        held = staged.at[p % slots, pl.ds(0, depth), :]
        return pltpu.make_async_copy(ham_t.at[:, pl.ds(at, tile)], held, sems.at[p % slots])

    for p in range(min(ahead, plan.pairs)):
        fetch(p).start()
    for slot in range(slots):
        staged[slot, depth:, :] = jnp.zeros((size, tile), F32)
    own_halves(plan, vectors, halves)

    for p in range(plan.pairs):
        fetch(p).wait()
        if p + ahead < plan.pairs:
            fetch(p + ahead).start()
        row = 2 * plan.mirrored(p, side)

        def block(q):
            even = pl.multiple_of(inverse[row, q] * size, size)
            odd = pl.multiple_of(inverse[row + 1, q] * size, size)
            first = staged[p % slots, pl.ds(even, size), :]
            second = staged[p % slots, pl.ds(odd, size), :]
            return jnp.where(lane < size, first, second)

        if p > 0:
            own_product(plan, p - 1, halves, band, inner)
        for place, at, rows in plan.runs(p):
            for q in range(rows // size):
                high, low = split(block(place + q))
                lines = slice(at + q * size, at + (q + 1) * size)
                band[p, lines, :tile] = high
                band[p, lines, tile:] = low
    own_product(plan, plan.pairs - 1, halves, band, inner)


def make_band(plan, side, inverse, ham_t, vectors):
    depth, rows = ham_t.shape
    size, tile = plan.size, plan.tile
    return pl.pallas_call(
        functools.partial(band_kernel, plan, depth),
        out_shape=[
            pltpu.VMEM((plan.pairs, plan.depth, 2 * tile), jnp.bfloat16),
            pltpu.VMEM((plan.width, rows), F32),
        ],
        in_specs=[SMEM, SMEM, pl.BlockSpec(memory_space=pltpu.HBM), VMEM],
        out_specs=[VMEM, VMEM],
        scratch_shapes=[
            pltpu.VMEM((4, depth + size, tile), F32),
            pltpu.VMEM((2 * plan.width, rows), jnp.bfloat16),
            pltpu.SemaphoreType.DMA((4,)),
        ],
        compiler_params=params(10),
        cost_estimate=cost(0, 2 * 4 * depth * rows),
        name="band",
    )(side, inverse, pltpu.with_memory_space_constraint(ham_t, pltpu.HBM), vectors)


def inner_kernel(plan, vectors, band, inner, halves):
    own_halves(plan, vectors, halves)
    for p in range(plan.pairs):
        own_product(plan, p, halves, band, inner)


def run_inner(plan, vectors, band):
    return pl.pallas_call(
        functools.partial(inner_kernel, plan),
        out_shape=pltpu.VMEM((plan.width, plan.rows), F32),
        in_specs=[VMEM] * 2,
        out_specs=VMEM,
        scratch_shapes=[pltpu.VMEM((2 * plan.width, plan.rows), jnp.bfloat16)],
        compiler_params=params(8),
        cost_estimate=cost(8 * plan.width * plan.rows**2, 0),
        name="inner",
    )(vectors, band)


class Outer:
    def __init__(self, plan, side, halves, away=None, far=None, near=None):
        self.plan, self.halves, self.bases, tile = plan, halves, {}, plan.tile
        tiles = []
        if away is not None:
            self.bases["away"] = len(tiles)
            tiles += [away_tile(plan, side, away, t) for t in reversed(range(plan.near))]
        if far is not None:
            self.bases["far"] = len(tiles)
            tiles += [far[:, t * tile : (t + 1) * tile] for t in range(plan.far)]
        if near is not None:
            self.bases["near"] = len(tiles)
            order = reversed(range(plan.near))
            tiles += [near[:, t * tile : (t + 1) * tile] for t in order]
        for t, value in enumerate(tiles):
            high, low = split(value)
            halves[: plan.width, t * tile : (t + 1) * tile] = high
            halves[plan.width :, t * tile : (t + 1) * tile] = low

    def add(self, p, total, band):
        plan, runs = self.plan, []
        for name, (first, last, row) in plan.spans(p).items():
            if name in self.bases and first < last:
                first, last = first + self.bases[name], last + self.bases[name]
                if runs and runs[-1][1] == first and sum(runs[-1][1:]) - runs[-1][0] == row:
                    runs[-1][1] = last
                else:
                    runs.append([first, last, row])
        for first, last, row in runs:
            rows = slice(row * plan.tile, (row + last - first) * plan.tile)
            vectors = self.halves[:, first * plan.tile : last * plan.tile]
            total += fold(jnp.dot(vectors, band[p, rows, :], preferred_element_type=F32))
        return total


def outer_scratch(plan, tiles):
    return [pltpu.VMEM((2 * plan.width, tiles * plan.tile), jnp.bfloat16)]


def middle_kernel(plan, kind, side, other, near, band, inner, out, halves):
    outer = Outer(plan, side, halves, near=near, **{kind: other})
    for p in range(plan.pairs):
        lanes = slice(p * plan.tile, (p + 1) * plan.tile)
        out[:, lanes] = outer.add(p, inner[:, lanes], band)


def run_middle(plan, kind, side, other, near, band, inner):
    return pl.pallas_call(
        functools.partial(middle_kernel, plan, kind),
        out_shape=pltpu.VMEM((plan.width, plan.rows), F32),
        in_specs=[SMEM] + [VMEM] * 4,
        out_specs=VMEM,
        scratch_shapes=outer_scratch(plan, 2 * plan.near),
        compiler_params=params(8),
        cost_estimate=cost(8 * plan.width * plan.rows**2, 0),
        name="middle",
    )(side, other, near, band, inner)


def first_kernel(
    plan, side, asked, far, band, inner, own, value, to_far, to_away, to_near, halves
):
    outer = Outer(plan, side, halves, far=far)
    for p in range(plan.pairs):
        lanes = slice(p * plan.tile, (p + 1) * plan.tile)
        product = outer.add(p, inner[:, lanes] - CENTER * own[:, lanes], band)
        term = product * (1.0 / HALF_WIDTH)
        value[:, lanes] = term
        write_sends(plan, side, lanes.start, term, to_away, to_near)

    def write(at, term):
        to_far[:, at : at + plan.tile] = term

    write_far(plan, side, asked, value, write)


def run_first(plan, side, asked, far, band, inner, own):
    shapes = [jax.ShapeDtypeStruct(far.shape, F32)] + send_shapes(plan)
    return pl.pallas_call(
        functools.partial(first_kernel, plan),
        out_shape=[pltpu.VMEM((plan.width, plan.rows), F32)] + shapes,
        in_specs=[SMEM] * 2 + [VMEM] * 4,
        out_specs=[VMEM] * (1 + len(shapes)),
        scratch_shapes=outer_scratch(plan, plan.far),
        compiler_params=params(8),
        cost_estimate=cost(2 * plan.width * plan.rows**2, 0),
        name="first",
    )(side, asked, far, band, inner, own)


def second_kernel(plan, side, away, band, inner, own, start, out, halves):
    outer = Outer(plan, side, halves, away=away)
    for p in range(plan.pairs):
        lanes = slice(p * plan.tile, (p + 1) * plan.tile)
        product = outer.add(p, inner[:, lanes] - CENTER * own[:, lanes], band)
        term = 2.0 / HALF_WIDTH * product - start[:, lanes]
        place = pl.multiple_of(plan.mirrored(p, side) * plan.tile, plan.tile)
        out[pl.ds(place, plan.tile), :] = term.T


def run_second(plan, side, away, band, inner, own, start):
    return pl.pallas_call(
        functools.partial(second_kernel, plan),
        out_shape=jax.ShapeDtypeStruct((plan.rows, plan.width), F32),
        in_specs=[SMEM] + [VMEM] * 5,
        out_specs=VMEM,
        scratch_shapes=outer_scratch(plan, plan.near),
        compiler_params=params(8),
        cost_estimate=cost(2 * plan.width * plan.rows**2, 0),
        name="second",
    )(side, away, band, inner, own, start)


def after(value, *others):
    return lax.optimization_barrier((value, *others))[0]


def per_device(hamiltonian, subspace, block_cols, far_list):
    block_rows, entries = block_cols.shape
    size = hamiltonian.shape[1] // entries
    device_count = lax.axis_size("rows")
    first_row = lax.axis_index("rows") * block_rows
    block_total = block_rows * device_count
    swap_level = (device_count // 8).bit_length() - 1
    plan = Plan(size, block_rows * size, subspace.shape[1], far_list.shape[1])

    side = (lax.axis_index("rows") % 2).astype(jnp.int32).reshape(1)

    def exchange(listed, sends):
        to_away, to_near = sends
        far = partner(listed, "rows", swap_level)
        return swap_chips(to_away, "rows"), far, partner(to_near, "rows", 0)

    asked = partner(far_list, "rows", swap_level)
    start, *sends = pack(plan, side, subspace)
    listed = gather_far(plan, side, asked, start)
    away, far, near = exchange(listed, sends)

    block_cols = after(block_cols, listed)
    edge, far_slots = 2 * plan.near, 2 * plan.far
    shift = block_cols - first_row + edge
    shift = jnp.where(shift < 0, shift + block_total, shift)
    shift = jnp.where(shift >= block_total, shift - block_total, shift)
    last = block_rows + 2 * edge - 2
    shift = shift + side[0] * (last - 4 * (shift >> 1))
    places = jnp.where(
        block_cols >= block_total,
        edge + block_cols - block_total,
        jnp.where(
            shift < edge,
            shift,
            jnp.where(
                shift < edge + block_rows,
                shift - edge + 2 * plan.outer,
                shift - block_rows + far_slots,
            ),
        ),
    )
    every = jnp.arange(plan.places, dtype=jnp.int32)[None, None, :]
    entry = jnp.arange(entries, dtype=jnp.int32)[None, :, None]
    hit = places[:, :, None] == every
    inverse = entries + jnp.sum(jnp.where(hit, entry - entries, 0), axis=1)

    band, inner = make_band(plan, side, inverse, hamiltonian.T, start)

    inner = run_middle(plan, "away", side, away, near, band, inner)
    value, listed, *sends = run_first(plan, side, asked, far, band, inner, start)
    away, far, near = exchange(listed, sends)
    inner = run_inner(plan, value, band)
    inner = run_middle(plan, "far", side, far, near, band, inner)
    return run_second(plan, side, away, band, inner, value, start)


def solution(mesh):
    placed = (P("rows", None), P("rows", None), P("rows", None), P("rows", None))
    return jax.shard_map(
        per_device, mesh=mesh, in_specs=placed, out_specs=P("rows", None), check_vma=False
    )
```

```python
import functools

import jax
import jax.numpy as jnp
from jax import lax
from jax.experimental import pallas as pl
from jax.experimental.pallas import tpu as pltpu
from jax.sharding import PartitionSpec as P

CENTER = 0.25
HALF_WIDTH = 1.5
REACH = 13
F32 = jnp.float32
VMEM = pl.BlockSpec(memory_space=pltpu.VMEM)
SMEM = pl.BlockSpec(memory_space=pltpu.SMEM)


def partner(value, axis, bit):
    mask = 2**bit
    pairs = [(source, source ^ mask) for source in range(lax.axis_size(axis))]
    return lax.ppermute(value, axis, pairs)


def swap_chips(value, axis):
    devices = lax.axis_size(axis)
    pairs = [(i, (i + (1 if i % 2 else -1)) % devices) for i in range(devices)]
    return lax.ppermute(value, axis, pairs)


def split(value):
    high = value.astype(jnp.bfloat16)
    return high, (value - high.astype(F32)).astype(jnp.bfloat16)


def fold(sums):
    width, tile = sums.shape[0] // 2, sums.shape[1] // 2
    small = sums[width:, tile:] + sums[width:, :tile] + sums[:width, tile:]
    return small + sums[:width, :tile]


def params(limit):
    return pltpu.CompilerParams(vmem_limit_bytes=limit * 2**20)


def cost(flops, moved):
    return pl.CostEstimate(flops=flops, bytes_accessed=moved, transcendentals=0)


class Plan:
    def __init__(self, size, rows, width, slots):
        self.size, self.rows, self.width = size, rows, width
        self.tile = 2 * size
        self.pairs = rows // self.tile
        self.near = (REACH + 1) // 2
        self.far = slots * size // self.tile
        self.edge = self.near * self.tile
        self.half = width // 2
        self.whole = self.edge - self.tile
        self.outer = 2 * self.near + self.far
        self.places = 2 * (self.outer + self.pairs)
        self.depth = max(sum(run[2] for run in self.runs(p)) for p in range(self.pairs))

    def outer_range(self, p):
        extra = p + self.near - self.pairs + 1
        return min(p, self.near), self.near + self.far + max(0, extra)

    def spans(self, p):
        begin, end = self.outer_range(p)
        row = self.near - begin
        return {
            "away": (begin, self.near, 0),
            "far": (0, self.far, row),
            "near": (0, end - self.near - self.far, row + self.far),
        }

    def own_range(self, p):
        return max(0, p - self.near), min(self.pairs, p + self.near + 1)

    def runs(self, p):
        begin, end = self.outer_range(p)
        rows = (end - begin) * self.tile
        outer = (2 * begin, 0, rows)
        begin, end = self.own_range(p)
        return outer, (2 * (self.outer + begin), rows, (end - begin) * self.tile)

    def mirrored(self, t, side):
        return t + side[0] * (self.pairs - 1 - 2 * t)


def write_far(plan, side, asked, source, write):
    tile, size = plan.tile, plan.size
    lane = lax.broadcasted_iota(jnp.int32, (source.shape[0], tile), 1)

    def block(slot, want):
        index = lax.rem(asked[0, slot] + 2 * plan.pairs, 2 * plan.pairs)
        at = plan.mirrored(lax.div(index, 2), side) * tile
        value = source[:, pl.ds(pl.multiple_of(at, tile), tile)]
        return jnp.where(lax.rem(index, 2) == want, value, pltpu.roll(value, size, 1))

    for t in range(plan.far):
        value = jnp.where(lane < size, block(2 * t, 0), block(2 * t + 1, 1))
        write(t * tile, value)


def write_sends(plan, side, at, value, to_away, to_near):
    tile, half, skip = plan.tile, plan.half, plan.rows - plan.edge
    if at < plan.whole:
        to_away[:, at : at + tile] = value[:half]
        to_away[:, plan.edge + at : plan.edge + at + tile] = value[half:]
    elif at == plan.whole:
        lane = lax.broadcasted_iota(jnp.int32, (half, tile), 1)
        turned = pltpu.roll(value, plan.size, 1)
        even = jnp.where(lane < plan.size, value[:half], turned[half:])
        odd = jnp.where(lane < plan.size, turned[:half], value[half:])
        to_away[:, at : at + tile] = jnp.where(side[0] == 0, even, odd)
    if at >= skip:
        to_near[:, at - skip : at - skip + tile] = value


def away_tile(plan, side, away, t):
    at, tile = t * plan.tile, plan.tile
    packed = away[:, at : at + tile]
    if at < plan.whole:
        rest = away[:, plan.edge + at : plan.edge + at + tile]
        return jnp.concatenate([packed, rest], axis=0)
    turned = pltpu.roll(packed, plan.size, 1)
    even = jnp.concatenate([turned, packed], axis=0)
    odd = jnp.concatenate([packed, turned], axis=0)
    return jnp.where(side[0] == 0, even, odd)


def send_shapes(plan):
    shapes = ((plan.half, plan.edge + plan.whole), (plan.width, plan.edge))
    return [jax.ShapeDtypeStruct(shape, F32) for shape in shapes]


def pack_kernel(plan, chunks, side, natural, turned, *rest):
    sends, staged, sems = rest[:-2], *rest[-2:]
    tile, count = plan.tile, plan.pairs // chunks
    step = count * tile

    def fetch(c):
        return pltpu.make_async_copy(
            natural.at[pl.ds(c * step, step), :],
            staged.at[pl.ds(c * step, step), :],
            sems.at[c],
        )

    for c in range(chunks):
        fetch(c).start()
    for c in range(chunks):
        fetch(c).wait()
    for t in range(plan.pairs):
        at = pl.multiple_of(plan.mirrored(t, side) * tile, tile)
        value = staged[pl.ds(at, tile), :].T
        turned[:, t * tile : (t + 1) * tile] = value
        write_sends(plan, side, t * tile, value, *sends)


def pack(plan, side, natural):
    chunks = 4 if plan.pairs % 4 == 0 else 1
    return pl.pallas_call(
        functools.partial(pack_kernel, plan, chunks),
        out_shape=[pltpu.VMEM((plan.width, plan.rows), F32)] + send_shapes(plan),
        in_specs=[SMEM, pl.BlockSpec(memory_space=pltpu.HBM)],
        out_specs=[VMEM] * 3,
        scratch_shapes=[
            pltpu.VMEM((plan.rows, plan.width), F32),
            pltpu.SemaphoreType.DMA((chunks,)),
        ],
        compiler_params=params(8),
        name="pack",
    )(side, pltpu.with_memory_space_constraint(natural, pltpu.HBM))


def far_kernel(plan, side, asked, turned, out):
    def write(at, value):
        out[:, at : at + plan.tile] = value

    write_far(plan, side, asked, turned, write)


def gather_far(plan, side, asked, turned):
    return pl.pallas_call(
        functools.partial(far_kernel, plan),
        out_shape=jax.ShapeDtypeStruct((plan.width, plan.far * plan.tile), F32),
        in_specs=[SMEM, SMEM, VMEM],
        out_specs=VMEM,
        compiler_params=params(8),
        name="far",
    )(side, asked, turned)


def own_halves(plan, vectors, halves):
    for at in range(0, plan.rows, plan.tile):
        high, low = split(vectors[:, at : at + plan.tile])
        halves[: plan.width, at : at + plan.tile] = high
        halves[plan.width :, at : at + plan.tile] = low


def own_product(plan, p, halves, band):
    begin, end = (plan.tile * bound for bound in plan.own_range(p))
    _, (_, row, rows) = plan.runs(p)
    vectors = halves[:, begin:end]
    return fold(jnp.dot(vectors, band[p, row : row + rows, :], preferred_element_type=F32))


def band_kernel(plan, depth, side, inverse, ham_t, vectors, band, inner, staged, halves, sems):
    size, tile = plan.size, plan.tile
    slots = staged.shape[0]
    ahead = slots - 1
    lane = lax.broadcasted_iota(jnp.int32, (size, tile), 1)

    def fetch(p):
        at = pl.multiple_of(plan.mirrored(p, side) * tile, tile)
        held = staged.at[p % slots, pl.ds(0, depth), :]
        return pltpu.make_async_copy(ham_t.at[:, pl.ds(at, tile)], held, sems.at[p % slots])

    def store(p, at, high, low):
        band[p, at : at + size, :tile] = high
        band[p, at : at + size, tile:] = low

    for p in range(min(ahead, plan.pairs)):
        fetch(p).start()
    for slot in range(slots):
        staged[slot, depth:, :] = jnp.zeros((size, tile), F32)
    own_halves(plan, vectors, halves)

    for p in range(plan.pairs):
        fetch(p).wait()
        if p + ahead < plan.pairs:
            fetch(p + ahead).start()
        row = 2 * plan.mirrored(p, side)

        def block(q):
            even = pl.multiple_of(inverse[row, q] * size, size)
            odd = pl.multiple_of(inverse[row + 1, q] * size, size)
            first = staged[p % slots, pl.ds(even, size), :]
            second = staged[p % slots, pl.ds(odd, size), :]
            return jnp.where(lane < size, first, second)

        ready = None if p == 0 else own_product(plan, p - 1, halves, band)
        places = [(place + q, at + q * size) for place, at, rows in plan.runs(p) for q in range(rows // size)]
        waiting = []
        for begin in range(0, len(places), 2):
            batch = [(at, *split(block(q))) for q, at in places[begin : begin + 2]]
            for entry in waiting:
                store(p, *entry)
            waiting = batch
        for entry in waiting:
            store(p, *entry)
        if p > 0:
            inner[:, (p - 1) * tile : p * tile] = ready
    p = plan.pairs - 1
    inner[:, p * tile : (p + 1) * tile] = own_product(plan, p, halves, band)


def make_band(plan, side, inverse, ham_t, vectors):
    depth, rows = ham_t.shape
    size, tile = plan.size, plan.tile
    return pl.pallas_call(
        functools.partial(band_kernel, plan, depth),
        out_shape=[
            pltpu.VMEM((plan.pairs, plan.depth, 2 * tile), jnp.bfloat16),
            pltpu.VMEM((plan.width, rows), F32),
        ],
        in_specs=[SMEM, SMEM, pl.BlockSpec(memory_space=pltpu.HBM), VMEM],
        out_specs=[VMEM, VMEM],
        scratch_shapes=[
            pltpu.VMEM((4, depth + size, tile), F32),
            pltpu.VMEM((2 * plan.width, rows), jnp.bfloat16),
            pltpu.SemaphoreType.DMA((4,)),
        ],
        compiler_params=params(10),
        cost_estimate=cost(0, 2 * 4 * depth * rows),
        name="band",
    )(side, inverse, pltpu.with_memory_space_constraint(ham_t, pltpu.HBM), vectors)


def put_halves(plan, halves, tiles):
    for t, value in enumerate(tiles):
        high, low = split(value)
        halves[: plan.width, t * plan.tile : (t + 1) * plan.tile] = high
        halves[plan.width :, t * plan.tile : (t + 1) * plan.tile] = low


def message_product(plan, name, p, halves, band):
    first, last, row = plan.spans(p)[name]
    if first == last:
        return 0.0
    rows = slice(row * plan.tile, (row + last - first) * plan.tile)
    vectors = halves[:, first * plan.tile : last * plan.tile]
    return fold(jnp.dot(vectors, band[p, rows, :], preferred_element_type=F32))


def halves_scratch(plan, tiles):
    return pltpu.VMEM((2 * plan.width, tiles * plan.tile), jnp.bfloat16)


def near_tiles(plan, near):
    tile = plan.tile
    return [near[:, t * tile : (t + 1) * tile] for t in reversed(range(plan.near))]


def away_tiles(plan, side, away):
    return [away_tile(plan, side, away, t) for t in reversed(range(plan.near))]


def near_kernel(plan, near, band, inner, out, halves):
    put_halves(plan, halves, near_tiles(plan, near))
    for p in range(plan.pairs):
        lanes = slice(p * plan.tile, (p + 1) * plan.tile)
        out[:, lanes] = inner[:, lanes] + message_product(plan, "near", p, halves, band)


def add_near(plan, near, band, inner):
    return pl.pallas_call(
        functools.partial(near_kernel, plan),
        out_shape=pltpu.VMEM((plan.width, plan.rows), F32),
        in_specs=[VMEM] * 3,
        out_specs=VMEM,
        scratch_shapes=[halves_scratch(plan, plan.near)],
        compiler_params=params(8),
        cost_estimate=cost(2 * plan.width * plan.rows**2, 0),
        name="near",
    )(near, band, inner)


def inner_kernel(plan, vectors, near, band, out, halves, near_halves):
    own_halves(plan, vectors, halves)
    put_halves(plan, near_halves, near_tiles(plan, near))
    for p in range(plan.pairs):
        total = own_product(plan, p, halves, band)
        total += message_product(plan, "near", p, near_halves, band)
        out[:, p * plan.tile : (p + 1) * plan.tile] = total


def run_inner(plan, vectors, near, band):
    return pl.pallas_call(
        functools.partial(inner_kernel, plan),
        out_shape=pltpu.VMEM((plan.width, plan.rows), F32),
        in_specs=[VMEM] * 3,
        out_specs=VMEM,
        scratch_shapes=[halves_scratch(plan, plan.pairs), halves_scratch(plan, plan.near)],
        compiler_params=params(8),
        cost_estimate=cost(8 * plan.width * plan.rows**2, 0),
        name="inner",
    )(vectors, near, band)


def far_split_kernel(plan, far, halves):
    tile = plan.tile
    put_halves(plan, halves, [far[:, t * tile : (t + 1) * tile] for t in range(plan.far)])


def split_far(plan, far):
    return pl.pallas_call(
        functools.partial(far_split_kernel, plan),
        out_shape=halves_scratch(plan, plan.far),
        in_specs=[VMEM],
        out_specs=VMEM,
        compiler_params=params(8),
        cost_estimate=cost(16 * plan.width * plan.rows**2, 0),
        name="split",
    )(far)


def first_kernel(
    plan, side, asked, away, far, band, inner, own, value, to_far, to_away, to_near, halves
):
    put_halves(plan, halves, away_tiles(plan, side, away))
    for p in range(plan.pairs):
        lanes = slice(p * plan.tile, (p + 1) * plan.tile)
        product = inner[:, lanes] - CENTER * own[:, lanes]
        product += message_product(plan, "far", p, far, band)
        product += message_product(plan, "away", p, halves, band)
        term = product * (1.0 / HALF_WIDTH)
        value[:, lanes] = term
        write_sends(plan, side, lanes.start, term, to_away, to_near)

    def write(at, term):
        to_far[:, at : at + plan.tile] = term

    write_far(plan, side, asked, value, write)


def run_first(plan, side, asked, away, far, band, inner, own):
    to_far = jax.ShapeDtypeStruct((plan.width, plan.far * plan.tile), F32)
    shapes = [to_far] + send_shapes(plan)
    return pl.pallas_call(
        functools.partial(first_kernel, plan),
        out_shape=[pltpu.VMEM((plan.width, plan.rows), F32)] + shapes,
        in_specs=[SMEM] * 2 + [VMEM] * 5,
        out_specs=[VMEM] * (1 + len(shapes)),
        scratch_shapes=[halves_scratch(plan, plan.near)],
        compiler_params=params(8),
        cost_estimate=cost(2 * plan.width * plan.rows**2, 0),
        name="first",
    )(side, asked, away, far, band, inner, own)


def second_kernel(plan, side, away, far, band, inner, own, start, out, halves):
    put_halves(plan, halves, away_tiles(plan, side, away))
    for p in range(plan.pairs):
        lanes = slice(p * plan.tile, (p + 1) * plan.tile)
        product = inner[:, lanes] - CENTER * own[:, lanes]
        product += message_product(plan, "far", p, far, band)
        product += message_product(plan, "away", p, halves, band)
        term = 2.0 / HALF_WIDTH * product - start[:, lanes]
        place = pl.multiple_of(plan.mirrored(p, side) * plan.tile, plan.tile)
        out[pl.ds(place, plan.tile), :] = term.T


def run_second(plan, side, away, far, band, inner, own, start):
    return pl.pallas_call(
        functools.partial(second_kernel, plan),
        out_shape=jax.ShapeDtypeStruct((plan.rows, plan.width), F32),
        in_specs=[SMEM] + [VMEM] * 6,
        out_specs=VMEM,
        scratch_shapes=[halves_scratch(plan, plan.near)],
        compiler_params=params(8),
        cost_estimate=cost(2 * plan.width * plan.rows**2, 0),
        name="second",
    )(side, away, far, band, inner, own, start)


def after(value, *others):
    return lax.optimization_barrier((value, *others))[0]


def per_device(hamiltonian, subspace, block_cols, far_list):
    block_rows, entries = block_cols.shape
    size = hamiltonian.shape[1] // entries
    device_count = lax.axis_size("rows")
    first_row = lax.axis_index("rows") * block_rows
    block_total = block_rows * device_count
    swap_level = (device_count // 8).bit_length() - 1
    plan = Plan(size, block_rows * size, subspace.shape[1], far_list.shape[1])

    side = (lax.axis_index("rows") % 2).astype(jnp.int32).reshape(1)

    def exchange(listed, sends):
        to_away, to_near = sends
        far = partner(listed, "rows", swap_level)
        return swap_chips(to_away, "rows"), far, partner(to_near, "rows", 0)

    asked = partner(far_list, "rows", swap_level)
    start, *sends = pack(plan, side, subspace)
    listed = gather_far(plan, side, asked, start)
    to_away, to_near, _ = lax.optimization_barrier((*sends, listed))
    away, far, near = exchange(listed, (to_away, to_near))

    block_cols = after(block_cols, listed)
    edge, far_slots = 2 * plan.near, 2 * plan.far
    shift = block_cols - first_row + edge
    shift = jnp.where(shift < 0, shift + block_total, shift)
    shift = jnp.where(shift >= block_total, shift - block_total, shift)
    last = block_rows + 2 * edge - 2
    shift = shift + side[0] * (last - 4 * (shift >> 1))
    places = jnp.where(
        block_cols >= block_total,
        edge + block_cols - block_total,
        jnp.where(
            shift < edge,
            shift,
            jnp.where(
                shift < edge + block_rows,
                shift - edge + 2 * plan.outer,
                shift - block_rows + far_slots,
            ),
        ),
    )
    every = jnp.arange(plan.places, dtype=jnp.int32)[None, None, :]
    entry = jnp.arange(entries, dtype=jnp.int32)[None, :, None]
    hit = places[:, :, None] == every
    inverse = entries + jnp.sum(jnp.where(hit, entry - entries, 0), axis=1)

    band, inner = make_band(plan, side, inverse, hamiltonian.T, start)

    inner = add_near(plan, near, band, inner)
    value, listed, *sends = run_first(
        plan, side, asked, away, split_far(plan, after(far, inner)), band, inner, start
    )
    away, far, near = exchange(listed, sends)
    inner = run_inner(plan, value, near, band)
    far = split_far(plan, after(far, inner))
    return run_second(plan, side, away, far, band, inner, value, start)


def solution(mesh):
    placed = (P("rows", None), P("rows", None), P("rows", None), P("rows", None))
    return jax.shard_map(
        per_device, mesh=mesh, in_specs=placed, out_specs=P("rows", None), check_vma=False
    )
```

```python
import functools

import jax
import jax.numpy as jnp
from jax import lax
from jax.experimental import pallas as pl
from jax.experimental.pallas import tpu as pltpu
from jax.sharding import PartitionSpec as P

CENTER = 0.25
HALF_WIDTH = 1.5
REACH = 13
F32 = jnp.float32
VMEM = pl.BlockSpec(memory_space=pltpu.VMEM)
HBM = pl.BlockSpec(memory_space=pltpu.HBM)
SMEM = pl.BlockSpec(memory_space=pltpu.SMEM)


def partner(value, axis, bit):
    mask = 2**bit
    pairs = [(source, source ^ mask) for source in range(lax.axis_size(axis))]
    return lax.ppermute(value, axis, pairs)


def swap_chips(value, axis):
    devices = lax.axis_size(axis)
    pairs = [(i, (i + (1 if i % 2 else -1)) % devices) for i in range(devices)]
    return lax.ppermute(value, axis, pairs)


def split(value):
    high = value.astype(jnp.bfloat16)
    return high, (value - high.astype(F32)).astype(jnp.bfloat16)


def fold(sums):
    width, tile = sums.shape[0] // 2, sums.shape[1] // 2
    small = sums[width:, tile:] + sums[width:, :tile] + sums[:width, tile:]
    return small + sums[:width, :tile]


def params(limit):
    return pltpu.CompilerParams(vmem_limit_bytes=limit * 2**20)


def cost(flops, moved):
    return pl.CostEstimate(flops=flops, bytes_accessed=moved, transcendentals=0)


class Plan:
    def __init__(self, size, rows, width, slots):
        self.size, self.rows, self.width = size, rows, width
        self.tile = 2 * size
        self.pairs = rows // self.tile
        self.near = (REACH + 1) // 2
        self.far = slots * size // self.tile
        self.edge = self.near * self.tile
        self.half = width // 2
        self.whole = self.edge - self.tile
        self.outer = 2 * self.near + self.far
        self.places = 2 * (self.outer + self.pairs)
        self.depth = max(sum(run[2] for run in self.runs(p)) for p in range(self.pairs))

    def outer_range(self, p):
        extra = p + self.near - self.pairs + 1
        return min(p, self.near), self.near + self.far + max(0, extra)

    def spans(self, p):
        begin, end = self.outer_range(p)
        row = self.near - begin
        return {
            "away": (begin, self.near, 0),
            "far": (0, self.far, row),
            "near": (0, end - self.near - self.far, row + self.far),
        }

    def own_range(self, p):
        return max(0, p - self.near), min(self.pairs, p + self.near + 1)

    def runs(self, p):
        begin, end = self.outer_range(p)
        rows = (end - begin) * self.tile
        outer = (2 * begin, 0, rows)
        begin, end = self.own_range(p)
        return outer, (2 * (self.outer + begin), rows, (end - begin) * self.tile)

    def mirrored(self, t, side):
        return t + side[0] * (self.pairs - 1 - 2 * t)


def write_far(plan, side, asked, source, write):
    tile, size = plan.tile, plan.size
    lane = lax.broadcasted_iota(jnp.int32, (source.shape[0], tile), 1)

    def block(slot, want):
        index = lax.rem(asked[0, slot] + 2 * plan.pairs, 2 * plan.pairs)
        at = plan.mirrored(lax.div(index, 2), side) * tile
        value = source[:, pl.ds(pl.multiple_of(at, tile), tile)]
        return jnp.where(lax.rem(index, 2) == want, value, pltpu.roll(value, size, 1))

    for t in range(plan.far):
        value = jnp.where(lane < size, block(2 * t, 0), block(2 * t + 1, 1))
        write(t * tile, value)


def write_sends(plan, side, at, value, to_away, to_near):
    tile, half, skip = plan.tile, plan.half, plan.rows - plan.edge
    if at < plan.whole:
        to_away[:, at : at + tile] = value[:half]
        to_away[:, plan.edge + at : plan.edge + at + tile] = value[half:]
    elif at == plan.whole:
        lane = lax.broadcasted_iota(jnp.int32, (half, tile), 1)
        turned = pltpu.roll(value, plan.size, 1)
        even = jnp.where(lane < plan.size, value[:half], turned[half:])
        odd = jnp.where(lane < plan.size, turned[:half], value[half:])
        to_away[:, at : at + tile] = jnp.where(side[0] == 0, even, odd)
    if at >= skip:
        to_near[:, at - skip : at - skip + tile] = value


def away_tile(plan, side, away, t):
    at, tile = t * plan.tile, plan.tile
    packed = away[:, at : at + tile]
    if at < plan.whole:
        rest = away[:, plan.edge + at : plan.edge + at + tile]
        return jnp.concatenate([packed, rest], axis=0)
    turned = pltpu.roll(packed, plan.size, 1)
    even = jnp.concatenate([turned, packed], axis=0)
    odd = jnp.concatenate([packed, turned], axis=0)
    return jnp.where(side[0] == 0, even, odd)


def send_shapes(plan):
    shapes = ((plan.half, plan.edge + plan.whole), (plan.width, plan.edge))
    return [jax.ShapeDtypeStruct(shape, F32) for shape in shapes]


def pack_kernel(plan, chunks, side, natural, codes, turned, held, *rest):
    sends, staged, sems = rest[:-2], *rest[-2:]
    tile, count = plan.tile, plan.pairs // chunks
    step = count * tile

    def fetch(c):
        return pltpu.make_async_copy(
            natural.at[pl.ds(c * step, step), :],
            staged.at[pl.ds(c * step, step), :],
            sems.at[c],
        )

    for c in range(chunks):
        fetch(c).start()
    copy = pltpu.make_async_copy(codes, held, sems.at[chunks])
    copy.start()
    for c in range(chunks):
        fetch(c).wait()
    for t in range(plan.pairs):
        at = pl.multiple_of(plan.mirrored(t, side) * tile, tile)
        value = staged[pl.ds(at, tile), :].T
        turned[:, t * tile : (t + 1) * tile] = value
        write_sends(plan, side, t * tile, value, *sends)
    copy.wait()


def pack(plan, side, natural, codes):
    chunks = 4 if plan.pairs % 4 == 0 else 1
    return pl.pallas_call(
        functools.partial(pack_kernel, plan, chunks),
        out_shape=[
            pltpu.VMEM((plan.width, plan.rows), F32),
            pltpu.VMEM(codes.shape, codes.dtype),
        ]
        + send_shapes(plan),
        in_specs=[SMEM, HBM, HBM],
        out_specs=[VMEM] * 4,
        scratch_shapes=[
            pltpu.VMEM((plan.rows, plan.width), F32),
            pltpu.SemaphoreType.DMA((chunks + 1,)),
        ],
        compiler_params=params(8),
        name="pack",
    )(side, *(pltpu.with_memory_space_constraint(x, pltpu.HBM) for x in (natural, codes)))


def far_kernel(plan, side, asked, turned, out):
    def write(at, value):
        out[:, at : at + plan.tile] = value

    write_far(plan, side, asked, turned, write)


def gather_far(plan, side, asked, turned):
    return pl.pallas_call(
        functools.partial(far_kernel, plan),
        out_shape=jax.ShapeDtypeStruct((plan.width, plan.far * plan.tile), F32),
        in_specs=[SMEM, SMEM, VMEM],
        out_specs=VMEM,
        compiler_params=params(8),
        name="far",
    )(side, asked, turned)


def own_halves(plan, vectors, halves):
    for at in range(0, plan.rows, plan.tile):
        high, low = split(vectors[:, at : at + plan.tile])
        halves[: plan.width, at : at + plan.tile] = high
        halves[plan.width :, at : at + plan.tile] = low


def own_product(plan, p, halves, band):
    begin, end = (plan.tile * bound for bound in plan.own_range(p))
    _, (_, row, rows) = plan.runs(p)
    vectors = halves[:, begin:end]
    return fold(jnp.dot(vectors, band[p, row : row + rows, :], preferred_element_type=F32))


def band_kernel(plan, depth, side, inverse, ham_t, vectors, band, inner, staged, halves, sems):
    size, tile = plan.size, plan.tile
    group = staged.shape[2] // tile
    units = plan.pairs // group
    lane = lax.broadcasted_iota(jnp.int32, (size, tile), 1)

    def fetch(u):
        natural = u + side[0] * (units - 1 - 2 * u)
        at = pl.multiple_of(natural * group * tile, group * tile)
        held = staged.at[u, pl.ds(0, depth), :]
        return pltpu.make_async_copy(ham_t.at[:, pl.ds(at, group * tile)], held, sems.at[u])

    def store(p, at, high, low):
        band[p, at : at + size, :tile] = high
        band[p, at : at + size, tile:] = low

    for u in range(units):
        fetch(u).start()
    for u in range(units):
        staged[u, depth:, :] = jnp.zeros((size, group * tile), F32)
    own_halves(plan, vectors, halves)

    for p in range(plan.pairs):
        u, t = p // group, p % group
        if t == 0:
            fetch(u).wait()
        lanes = pl.multiple_of((t + side[0] * (group - 1 - 2 * t)) * tile, tile)
        row = 2 * plan.mirrored(p, side)

        def block(q):
            even = pl.multiple_of(inverse[row, q] * size, size)
            odd = pl.multiple_of(inverse[row + 1, q] * size, size)
            first = staged[u, pl.ds(even, size), pl.ds(lanes, tile)]
            second = staged[u, pl.ds(odd, size), pl.ds(lanes, tile)]
            return jnp.where(lane < size, first, second)

        ready = None if p == 0 else own_product(plan, p - 1, halves, band)
        places = [(place + q, at + q * size) for place, at, rows in plan.runs(p) for q in range(rows // size)]
        waiting = []
        for begin in range(0, len(places), 2):
            batch = [(at, *split(block(q))) for q, at in places[begin : begin + 2]]
            for entry in waiting:
                store(p, *entry)
            waiting = batch
        for entry in waiting:
            store(p, *entry)
        if p > 0:
            inner[:, (p - 1) * tile : p * tile] = ready
    p = plan.pairs - 1
    inner[:, p * tile : (p + 1) * tile] = own_product(plan, p, halves, band)


def make_band(plan, side, inverse, ham_t, vectors):
    depth, rows = ham_t.shape
    size, tile = plan.size, plan.tile
    group = 2 if plan.pairs % 2 == 0 else 1
    return pl.pallas_call(
        functools.partial(band_kernel, plan, depth),
        out_shape=[
            pltpu.VMEM((plan.pairs, plan.depth, 2 * tile), jnp.bfloat16),
            pltpu.VMEM((plan.width, rows), F32),
        ],
        in_specs=[SMEM, SMEM, HBM, VMEM],
        out_specs=[VMEM, VMEM],
        scratch_shapes=[
            pltpu.VMEM((plan.pairs // group, depth + size, group * tile), F32),
            pltpu.VMEM((2 * plan.width, rows), jnp.bfloat16),
            pltpu.SemaphoreType.DMA((plan.pairs // group,)),
        ],
        compiler_params=params(14),
        cost_estimate=cost(0, 2 * 4 * depth * rows),
        name="band",
    )(side, inverse, pltpu.with_memory_space_constraint(ham_t, pltpu.HBM), vectors)


def put_halves(plan, halves, tiles):
    for t, value in enumerate(tiles):
        high, low = split(value)
        halves[: plan.width, t * plan.tile : (t + 1) * plan.tile] = high
        halves[plan.width :, t * plan.tile : (t + 1) * plan.tile] = low


def message_product(plan, name, p, halves, band):
    first, last, row = plan.spans(p)[name]
    if first == last:
        return 0.0
    rows = slice(row * plan.tile, (row + last - first) * plan.tile)
    vectors = halves[:, first * plan.tile : last * plan.tile]
    return fold(jnp.dot(vectors, band[p, rows, :], preferred_element_type=F32))


def halves_scratch(plan, tiles):
    return pltpu.VMEM((2 * plan.width, tiles * plan.tile), jnp.bfloat16)


def near_tiles(plan, near):
    tile = plan.tile
    return [near[:, t * tile : (t + 1) * tile] for t in reversed(range(plan.near))]


def away_tiles(plan, side, away):
    return [away_tile(plan, side, away, t) for t in reversed(range(plan.near))]


def middle_kernel(plan, side, away, near, band, inner, out, away_halves, near_halves):
    put_halves(plan, away_halves, away_tiles(plan, side, away))
    put_halves(plan, near_halves, near_tiles(plan, near))
    for p in range(plan.pairs):
        lanes = slice(p * plan.tile, (p + 1) * plan.tile)
        total = inner[:, lanes] + message_product(plan, "away", p, away_halves, band)
        out[:, lanes] = total + message_product(plan, "near", p, near_halves, band)


def run_middle(plan, side, away, near, band, inner):
    return pl.pallas_call(
        functools.partial(middle_kernel, plan),
        out_shape=pltpu.VMEM((plan.width, plan.rows), F32),
        in_specs=[SMEM] + [VMEM] * 4,
        out_specs=VMEM,
        scratch_shapes=[halves_scratch(plan, plan.near)] * 2,
        compiler_params=params(8),
        cost_estimate=cost(8 * plan.width * plan.rows**2, 0),
        name="middle",
    )(side, away, near, band, inner)


def inner_kernel(plan, vectors, near, band, out, halves, near_halves):
    own_halves(plan, vectors, halves)
    put_halves(plan, near_halves, near_tiles(plan, near))
    for p in range(plan.pairs):
        total = own_product(plan, p, halves, band)
        total += message_product(plan, "near", p, near_halves, band)
        out[:, p * plan.tile : (p + 1) * plan.tile] = total


def run_inner(plan, vectors, near, band):
    return pl.pallas_call(
        functools.partial(inner_kernel, plan),
        out_shape=pltpu.VMEM((plan.width, plan.rows), F32),
        in_specs=[VMEM] * 3,
        out_specs=VMEM,
        scratch_shapes=[halves_scratch(plan, plan.pairs), halves_scratch(plan, plan.near)],
        compiler_params=params(8),
        cost_estimate=cost(8 * plan.width * plan.rows**2, 0),
        name="inner",
    )(vectors, near, band)


def far_tiles(plan, far):
    return [far[:, t * plan.tile : (t + 1) * plan.tile] for t in range(plan.far)]


def far_split_kernel(plan, far, halves):
    put_halves(plan, halves, far_tiles(plan, far))


def split_far(plan, far):
    return pl.pallas_call(
        functools.partial(far_split_kernel, plan),
        out_shape=halves_scratch(plan, plan.far),
        in_specs=[VMEM],
        out_specs=VMEM,
        compiler_params=params(8),
        cost_estimate=cost(16 * plan.width * plan.rows**2, 0),
        name="split",
    )(far)


def first_kernel(
    plan, side, asked, far, band, inner, own, value, to_far, to_away, to_near, halves
):
    put_halves(plan, halves, far_tiles(plan, far))
    for p in range(plan.pairs):
        lanes = slice(p * plan.tile, (p + 1) * plan.tile)
        product = inner[:, lanes] - CENTER * own[:, lanes]
        product += message_product(plan, "far", p, halves, band)
        term = product * (1.0 / HALF_WIDTH)
        value[:, lanes] = term
        write_sends(plan, side, lanes.start, term, to_away, to_near)

    def write(at, term):
        to_far[:, at : at + plan.tile] = term

    write_far(plan, side, asked, value, write)


def run_first(plan, side, asked, far, band, inner, own):
    shapes = [jax.ShapeDtypeStruct(far.shape, F32)] + send_shapes(plan)
    return pl.pallas_call(
        functools.partial(first_kernel, plan),
        out_shape=[pltpu.VMEM((plan.width, plan.rows), F32)] + shapes,
        in_specs=[SMEM] * 2 + [VMEM] * 4,
        out_specs=[VMEM] * (1 + len(shapes)),
        scratch_shapes=[halves_scratch(plan, plan.far)],
        compiler_params=params(8),
        cost_estimate=cost(2 * plan.width * plan.rows**2, 0),
        name="first",
    )(side, asked, far, band, inner, own)


def second_kernel(plan, side, away, far, band, inner, own, start, out, halves, held, sems):
    put_halves(plan, halves, away_tiles(plan, side, away))
    copies = []
    for p in range(plan.pairs):
        lanes = slice(p * plan.tile, (p + 1) * plan.tile)
        product = inner[:, lanes] - CENTER * own[:, lanes]
        product += message_product(plan, "far", p, far, band)
        product += message_product(plan, "away", p, halves, band)
        term = 2.0 / HALF_WIDTH * product - start[:, lanes]
        place = pl.multiple_of(plan.mirrored(p, side) * plan.tile, plan.tile)
        held[p] = term.T
        copies.append(
            pltpu.make_async_copy(held.at[p], out.at[pl.ds(place, plan.tile), :], sems.at[p])
        )
        copies[-1].start()
    for copy in copies:
        copy.wait()


def run_second(plan, side, away, far, band, inner, own, start):
    return pl.pallas_call(
        functools.partial(second_kernel, plan),
        out_shape=jax.ShapeDtypeStruct((plan.rows, plan.width), F32),
        in_specs=[SMEM] + [VMEM] * 6,
        out_specs=HBM,
        scratch_shapes=[
            halves_scratch(plan, plan.near),
            pltpu.VMEM((plan.pairs, plan.tile, plan.width), F32),
            pltpu.SemaphoreType.DMA((plan.pairs,)),
        ],
        compiler_params=params(8),
        cost_estimate=cost(2 * plan.width * plan.rows**2, 0),
        name="second",
    )(side, away, far, band, inner, own, start)


def after(value, *others):
    return lax.optimization_barrier((value, *others))[0]


def per_device(hamiltonian, subspace, block_cols, far_list):
    block_rows, entries = block_cols.shape
    size = hamiltonian.shape[1] // entries
    device_count = lax.axis_size("rows")
    first_row = lax.axis_index("rows") * block_rows
    block_total = block_rows * device_count
    swap_level = (device_count // 8).bit_length() - 1
    plan = Plan(size, block_rows * size, subspace.shape[1], far_list.shape[1])

    side = (lax.axis_index("rows") % 2).astype(jnp.int32).reshape(1)

    def exchange(listed, sends):
        to_away, to_near = sends
        far = partner(listed, "rows", swap_level)
        return swap_chips(to_away, "rows"), far, partner(to_near, "rows", 0)

    asked = partner(far_list, "rows", swap_level)
    start, block_cols, *sends = pack(plan, side, subspace, block_cols)
    listed = gather_far(plan, side, asked, start)
    away, far, near = exchange(listed, sends)

    block_cols = after(block_cols, listed)
    edge, far_slots = 2 * plan.near, 2 * plan.far
    shift = block_cols - first_row + edge
    shift = jnp.where(shift < 0, shift + block_total, shift)
    shift = jnp.where(shift >= block_total, shift - block_total, shift)
    last = block_rows + 2 * edge - 2
    shift = shift + side[0] * (last - 4 * (shift >> 1))
    places = jnp.where(
        block_cols >= block_total,
        edge + block_cols - block_total,
        jnp.where(
            shift < edge,
            shift,
            jnp.where(
                shift < edge + block_rows,
                shift - edge + 2 * plan.outer,
                shift - block_rows + far_slots,
            ),
        ),
    )
    every = jnp.arange(plan.places, dtype=jnp.int32)[None, None, :]
    entry = jnp.arange(entries, dtype=jnp.int32)[None, :, None]
    hit = places[:, :, None] == every
    inverse = entries + jnp.sum(jnp.where(hit, entry - entries, 0), axis=1)

    band, inner = make_band(plan, side, inverse, hamiltonian.T, start)

    inner = run_middle(plan, side, away, near, band, inner)
    value, listed, *sends = run_first(plan, side, asked, far, band, inner, start)
    away, far, near = exchange(listed, sends)
    inner = run_inner(plan, value, near, band)
    far = split_far(plan, after(far, inner))
    return run_second(plan, side, away, far, band, inner, value, start)


def solution(mesh):
    placed = (P("rows", None), P("rows", None), P("rows", None), P("rows", None))
    return jax.shard_map(
        per_device, mesh=mesh, in_specs=placed, out_specs=P("rows", None), check_vma=False
    )
```

```python
import functools

import jax
import jax.numpy as jnp
from jax import lax
from jax.experimental import pallas as pl
from jax.experimental.pallas import tpu as pltpu
from jax.sharding import PartitionSpec as P

CENTER = 0.25
HALF_WIDTH = 1.5
REACH = 13
F32 = jnp.float32
VMEM = pl.BlockSpec(memory_space=pltpu.VMEM)
HBM = pl.BlockSpec(memory_space=pltpu.HBM)
SMEM = pl.BlockSpec(memory_space=pltpu.SMEM)


def partner(value, axis, bit):
    mask = 2**bit
    pairs = [(source, source ^ mask) for source in range(lax.axis_size(axis))]
    return lax.ppermute(value, axis, pairs)


def swap_chips(value, axis):
    devices = lax.axis_size(axis)
    pairs = [(i, (i + (1 if i % 2 else -1)) % devices) for i in range(devices)]
    return lax.ppermute(value, axis, pairs)


def split(value):
    high = value.astype(jnp.bfloat16)
    return high, (value - high.astype(F32)).astype(jnp.bfloat16)


def fold(sums):
    width, tile = sums.shape[0] // 2, sums.shape[1] // 2
    small = sums[width:, tile:] + sums[width:, :tile] + sums[:width, tile:]
    return small + sums[:width, :tile]


def params(limit):
    return pltpu.CompilerParams(vmem_limit_bytes=limit * 2**20)


def cost(flops, moved):
    return pl.CostEstimate(flops=flops, bytes_accessed=moved, transcendentals=0)


class Plan:
    def __init__(self, size, rows, width, slots):
        self.size, self.rows, self.width = size, rows, width
        self.tile = 2 * size
        self.pairs = rows // self.tile
        self.near = (REACH + 1) // 2
        self.far = slots * size // self.tile
        self.edge = self.near * self.tile
        self.half = width // 2
        self.whole = self.edge - self.tile
        self.outer = 2 * self.near + self.far
        self.places = 2 * (self.outer + self.pairs)
        self.depth = max(sum(run[2] for run in self.runs(p)) for p in range(self.pairs))

    def outer_range(self, p):
        extra = p + self.near - self.pairs + 1
        return min(p, self.near), self.near + self.far + max(0, extra)

    def spans(self, p):
        begin, end = self.outer_range(p)
        row = self.near - begin
        return {
            "away": (begin, self.near, 0),
            "far": (0, self.far, row),
            "near": (0, end - self.near - self.far, row + self.far),
        }

    def own_range(self, p):
        return max(0, p - self.near), min(self.pairs, p + self.near + 1)

    def runs(self, p):
        begin, end = self.outer_range(p)
        rows = (end - begin) * self.tile
        outer = (2 * begin, 0, rows)
        begin, end = self.own_range(p)
        return outer, (2 * (self.outer + begin), rows, (end - begin) * self.tile)

    def mirrored(self, t, side):
        return t + side[0] * (self.pairs - 1 - 2 * t)


def write_far(plan, side, asked, source, write):
    tile, size = plan.tile, plan.size
    lane = lax.broadcasted_iota(jnp.int32, (source.shape[0], tile), 1)

    def block(slot, want):
        index = lax.rem(asked[0, slot] + 2 * plan.pairs, 2 * plan.pairs)
        at = plan.mirrored(lax.div(index, 2), side) * tile
        value = source[:, pl.ds(pl.multiple_of(at, tile), tile)]
        return jnp.where(lax.rem(index, 2) == want, value, pltpu.roll(value, size, 1))

    for t in range(plan.far):
        value = jnp.where(lane < size, block(2 * t, 0), block(2 * t + 1, 1))
        write(t * tile, value)


def write_sends(plan, side, at, value, to_away, to_near):
    tile, half, skip = plan.tile, plan.half, plan.rows - plan.edge
    if at < plan.whole:
        to_away[:, at : at + tile] = value[:half]
        to_away[:, plan.edge + at : plan.edge + at + tile] = value[half:]
    elif at == plan.whole:
        lane = lax.broadcasted_iota(jnp.int32, (half, tile), 1)
        turned = pltpu.roll(value, plan.size, 1)
        even = jnp.where(lane < plan.size, value[:half], turned[half:])
        odd = jnp.where(lane < plan.size, turned[:half], value[half:])
        to_away[:, at : at + tile] = jnp.where(side[0] == 0, even, odd)
    if at >= skip:
        to_near[:, at - skip : at - skip + tile] = value


def away_tile(plan, side, away, t):
    at, tile = t * plan.tile, plan.tile
    packed = away[:, at : at + tile]
    if at < plan.whole:
        rest = away[:, plan.edge + at : plan.edge + at + tile]
        return jnp.concatenate([packed, rest], axis=0)
    turned = pltpu.roll(packed, plan.size, 1)
    even = jnp.concatenate([turned, packed], axis=0)
    odd = jnp.concatenate([packed, turned], axis=0)
    return jnp.where(side[0] == 0, even, odd)


def send_shapes(plan):
    shapes = ((plan.half, plan.edge + plan.whole), (plan.width, plan.edge))
    return [jax.ShapeDtypeStruct(shape, F32) for shape in shapes]


def pack_kernel(plan, chunks, side, natural, codes, turned, held, *rest):
    sends, staged, sems = rest[:-2], *rest[-2:]
    tile, count = plan.tile, plan.pairs // chunks
    step = count * tile

    def fetch(c):
        return pltpu.make_async_copy(
            natural.at[pl.ds(c * step, step), :],
            staged.at[pl.ds(c * step, step), :],
            sems.at[c],
        )

    for c in range(chunks):
        fetch(c).start()
    copy = pltpu.make_async_copy(codes, held, sems.at[chunks])
    copy.start()
    for c in range(chunks):
        fetch(c).wait()
    for t in range(plan.pairs):
        at = pl.multiple_of(plan.mirrored(t, side) * tile, tile)
        value = staged[pl.ds(at, tile), :].T
        turned[:, t * tile : (t + 1) * tile] = value
        write_sends(plan, side, t * tile, value, *sends)
    copy.wait()


def pack(plan, side, natural, codes):
    chunks = 4 if plan.pairs % 4 == 0 else 1
    return pl.pallas_call(
        functools.partial(pack_kernel, plan, chunks),
        out_shape=[
            pltpu.VMEM((plan.width, plan.rows), F32),
            pltpu.VMEM(codes.shape, codes.dtype),
        ]
        + send_shapes(plan),
        in_specs=[SMEM, HBM, HBM],
        out_specs=[VMEM] * 4,
        scratch_shapes=[
            pltpu.VMEM((plan.rows, plan.width), F32),
            pltpu.SemaphoreType.DMA((chunks + 1,)),
        ],
        compiler_params=params(8),
        name="pack",
    )(side, *(pltpu.with_memory_space_constraint(x, pltpu.HBM) for x in (natural, codes)))


def far_kernel(plan, side, asked, turned, out):
    def write(at, value):
        out[:, at : at + plan.tile] = value

    write_far(plan, side, asked, turned, write)


def gather_far(plan, side, asked, turned):
    return pl.pallas_call(
        functools.partial(far_kernel, plan),
        out_shape=jax.ShapeDtypeStruct((plan.width, plan.far * plan.tile), F32),
        in_specs=[SMEM, SMEM, VMEM],
        out_specs=VMEM,
        compiler_params=params(8),
        name="far",
    )(side, asked, turned)


def own_halves(plan, vectors, halves):
    for at in range(0, plan.rows, plan.tile):
        high, low = split(vectors[:, at : at + plan.tile])
        halves[: plan.width, at : at + plan.tile] = high
        halves[plan.width :, at : at + plan.tile] = low


def own_product(plan, p, halves, band):
    begin, end = (plan.tile * bound for bound in plan.own_range(p))
    _, (_, row, rows) = plan.runs(p)
    vectors = halves[:, begin:end]
    return fold(jnp.dot(vectors, band[p, row : row + rows, :], preferred_element_type=F32))


def band_kernel(plan, depth, side, inverse, ham_t, vectors, band, inner, staged, halves, sems):
    size, tile = plan.size, plan.tile
    group = staged.shape[2] // tile
    units = plan.pairs // group
    lane = lax.broadcasted_iota(jnp.int32, (size, tile), 1)

    def fetch(u):
        natural = u + side[0] * (units - 1 - 2 * u)
        at = pl.multiple_of(natural * group * tile, group * tile)
        held = staged.at[u, pl.ds(0, depth), :]
        return pltpu.make_async_copy(ham_t.at[:, pl.ds(at, group * tile)], held, sems.at[u])

    def store(p, at, high, low):
        band[p, at : at + size, :tile] = high
        band[p, at : at + size, tile:] = low

    for u in range(units):
        fetch(u).start()
    for u in range(units):
        staged[u, depth:, :] = jnp.zeros((size, group * tile), F32)
    own_halves(plan, vectors, halves)

    for p in range(plan.pairs):
        u, t = p // group, p % group
        if t == 0:
            fetch(u).wait()
        lanes = pl.multiple_of((t + side[0] * (group - 1 - 2 * t)) * tile, tile)
        row = 2 * plan.mirrored(p, side)

        def block(q):
            even = pl.multiple_of(inverse[row, q] * size, size)
            odd = pl.multiple_of(inverse[row + 1, q] * size, size)
            first = staged[u, pl.ds(even, size), pl.ds(lanes, tile)]
            second = staged[u, pl.ds(odd, size), pl.ds(lanes, tile)]
            return jnp.where(lane < size, first, second)

        ready = None if p == 0 else own_product(plan, p - 1, halves, band)
        places = [(place + q, at + q * size) for place, at, rows in plan.runs(p) for q in range(rows // size)]
        waiting = []
        for begin in range(0, len(places), 2):
            batch = [(at, *split(block(q))) for q, at in places[begin : begin + 2]]
            for entry in waiting:
                store(p, *entry)
            waiting = batch
        for entry in waiting:
            store(p, *entry)
        if p > 0:
            inner[:, (p - 1) * tile : p * tile] = ready
    p = plan.pairs - 1
    inner[:, p * tile : (p + 1) * tile] = own_product(plan, p, halves, band)


def make_band(plan, side, inverse, ham_t, vectors):
    depth, rows = ham_t.shape
    size, tile = plan.size, plan.tile
    group = 2 if plan.pairs % 2 == 0 else 1
    return pl.pallas_call(
        functools.partial(band_kernel, plan, depth),
        out_shape=[
            pltpu.VMEM((plan.pairs, plan.depth, 2 * tile), jnp.bfloat16),
            pltpu.VMEM((plan.width, rows), F32),
        ],
        in_specs=[SMEM, SMEM, HBM, VMEM],
        out_specs=[VMEM, VMEM],
        scratch_shapes=[
            pltpu.VMEM((plan.pairs // group, depth + size, group * tile), F32),
            pltpu.VMEM((2 * plan.width, rows), jnp.bfloat16),
            pltpu.SemaphoreType.DMA((plan.pairs // group,)),
        ],
        compiler_params=params(14),
        cost_estimate=cost(0, 2 * 4 * depth * rows),
        name="band",
    )(side, inverse, pltpu.with_memory_space_constraint(ham_t, pltpu.HBM), vectors)


def put_halves(plan, halves, tiles):
    for t, value in enumerate(tiles):
        high, low = split(value)
        halves[: plan.width, t * plan.tile : (t + 1) * plan.tile] = high
        halves[plan.width :, t * plan.tile : (t + 1) * plan.tile] = low


def message_product(plan, name, p, halves, band):
    first, last, row = plan.spans(p)[name]
    if first == last:
        return 0.0
    rows = slice(row * plan.tile, (row + last - first) * plan.tile)
    vectors = halves[:, first * plan.tile : last * plan.tile]
    return fold(jnp.dot(vectors, band[p, rows, :], preferred_element_type=F32))


def halves_scratch(plan, tiles):
    return pltpu.VMEM((2 * plan.width, tiles * plan.tile), jnp.bfloat16)


def near_tiles(plan, near):
    tile = plan.tile
    return [near[:, t * tile : (t + 1) * tile] for t in reversed(range(plan.near))]


def away_tiles(plan, side, away):
    return [away_tile(plan, side, away, t) for t in reversed(range(plan.near))]


def middle_kernel(plan, side, away, near, band, inner, out, away_halves, near_halves):
    put_halves(plan, away_halves, away_tiles(plan, side, away))
    put_halves(plan, near_halves, near_tiles(plan, near))
    for p in range(plan.pairs):
        lanes = slice(p * plan.tile, (p + 1) * plan.tile)
        total = inner[:, lanes] + message_product(plan, "away", p, away_halves, band)
        out[:, lanes] = total + message_product(plan, "near", p, near_halves, band)


def run_middle(plan, side, away, near, band, inner):
    return pl.pallas_call(
        functools.partial(middle_kernel, plan),
        out_shape=pltpu.VMEM((plan.width, plan.rows), F32),
        in_specs=[SMEM] + [VMEM] * 4,
        out_specs=VMEM,
        scratch_shapes=[halves_scratch(plan, plan.near)] * 2,
        compiler_params=params(8),
        cost_estimate=cost(8 * plan.width * plan.rows**2, 0),
        name="middle",
    )(side, away, near, band, inner)


def inner_kernel(plan, vectors, near, band, out, halves, near_halves):
    own_halves(plan, vectors, halves)
    put_halves(plan, near_halves, near_tiles(plan, near))
    for p in range(plan.pairs):
        total = own_product(plan, p, halves, band)
        total += message_product(plan, "near", p, near_halves, band)
        out[:, p * plan.tile : (p + 1) * plan.tile] = total


def run_inner(plan, vectors, near, band):
    return pl.pallas_call(
        functools.partial(inner_kernel, plan),
        out_shape=pltpu.VMEM((plan.width, plan.rows), F32),
        in_specs=[VMEM] * 3,
        out_specs=VMEM,
        scratch_shapes=[halves_scratch(plan, plan.pairs), halves_scratch(plan, plan.near)],
        compiler_params=params(8),
        cost_estimate=cost(8 * plan.width * plan.rows**2, 0),
        name="inner",
    )(vectors, near, band)


def far_tiles(plan, far):
    return [far[:, t * plan.tile : (t + 1) * plan.tile] for t in range(plan.far)]


def far_split_kernel(plan, far, halves):
    put_halves(plan, halves, far_tiles(plan, far))


def split_far(plan, far):
    return pl.pallas_call(
        functools.partial(far_split_kernel, plan),
        out_shape=halves_scratch(plan, plan.far),
        in_specs=[VMEM],
        out_specs=VMEM,
        compiler_params=params(8),
        cost_estimate=cost(16 * plan.width * plan.rows**2, 0),
        name="split",
    )(far)


def first_kernel(
    plan, side, asked, far, band, inner, own, value, to_far, to_away, to_near, halves
):
    put_halves(plan, halves, far_tiles(plan, far))
    for p in range(plan.pairs):
        lanes = slice(p * plan.tile, (p + 1) * plan.tile)
        product = inner[:, lanes] - CENTER * own[:, lanes]
        product += message_product(plan, "far", p, halves, band)
        term = product * (1.0 / HALF_WIDTH)
        value[:, lanes] = term
        write_sends(plan, side, lanes.start, term, to_away, to_near)

    def write(at, term):
        to_far[:, at : at + plan.tile] = term

    write_far(plan, side, asked, value, write)


def run_first(plan, side, asked, far, band, inner, own):
    shapes = [jax.ShapeDtypeStruct(far.shape, F32)] + send_shapes(plan)
    return pl.pallas_call(
        functools.partial(first_kernel, plan),
        out_shape=[pltpu.VMEM((plan.width, plan.rows), F32)] + shapes,
        in_specs=[SMEM] * 2 + [VMEM] * 4,
        out_specs=[VMEM] * (1 + len(shapes)),
        scratch_shapes=[halves_scratch(plan, plan.far)],
        compiler_params=params(8),
        cost_estimate=cost(2 * plan.width * plan.rows**2, 0),
        name="first",
    )(side, asked, far, band, inner, own)


def second_kernel(plan, side, away, far, band, inner, own, start, out, halves, held, sems):
    put_halves(plan, halves, away_tiles(plan, side, away))
    copies = []
    for p in range(plan.pairs):
        lanes = slice(p * plan.tile, (p + 1) * plan.tile)
        product = inner[:, lanes] - CENTER * own[:, lanes]
        product += message_product(plan, "far", p, far, band)
        product += message_product(plan, "away", p, halves, band)
        term = 2.0 / HALF_WIDTH * product - start[:, lanes]
        place = pl.multiple_of(plan.mirrored(p, side) * plan.tile, plan.tile)
        held[p] = term.T
        copies.append(
            pltpu.make_async_copy(held.at[p], out.at[pl.ds(place, plan.tile), :], sems.at[p])
        )
        copies[-1].start()
    for copy in copies:
        copy.wait()


def run_second(plan, side, away, far, band, inner, own, start):
    return pl.pallas_call(
        functools.partial(second_kernel, plan),
        out_shape=jax.ShapeDtypeStruct((plan.rows, plan.width), F32),
        in_specs=[SMEM] + [VMEM] * 6,
        out_specs=HBM,
        scratch_shapes=[
            halves_scratch(plan, plan.near),
            pltpu.VMEM((plan.pairs, plan.tile, plan.width), F32),
            pltpu.SemaphoreType.DMA((plan.pairs,)),
        ],
        compiler_params=params(8),
        cost_estimate=cost(2 * plan.width * plan.rows**2, 0),
        name="second",
    )(side, away, far, band, inner, own, start)


def after(value, *others):
    return lax.optimization_barrier((value, *others))[0]


def per_device(hamiltonian, subspace, block_cols, far_list):
    block_rows, entries = block_cols.shape
    size = hamiltonian.shape[1] // entries
    device_count = lax.axis_size("rows")
    first_row = lax.axis_index("rows") * block_rows
    block_total = block_rows * device_count
    swap_level = (device_count // 8).bit_length() - 1
    plan = Plan(size, block_rows * size, subspace.shape[1], far_list.shape[1])

    side = (lax.axis_index("rows") % 2).astype(jnp.int32).reshape(1)

    def exchange(listed, sends):
        to_away, to_near = sends
        far = partner(listed, "rows", swap_level)
        return swap_chips(to_away, "rows"), far, partner(to_near, "rows", 0)

    start, block_cols, *sends = pack(plan, side, subspace, block_cols)
    asked = partner(after(far_list, start), "rows", swap_level)
    listed = gather_far(plan, side, asked, start)
    away, far, near = exchange(listed, (sends[0], after(sends[1], listed)))

    block_cols = after(block_cols, listed)
    edge, far_slots = 2 * plan.near, 2 * plan.far
    shift = block_cols - first_row + edge
    shift = jnp.where(shift < 0, shift + block_total, shift)
    shift = jnp.where(shift >= block_total, shift - block_total, shift)
    last = block_rows + 2 * edge - 2
    shift = shift + side[0] * (last - 4 * (shift >> 1))
    places = jnp.where(
        block_cols >= block_total,
        edge + block_cols - block_total,
        jnp.where(
            shift < edge,
            shift,
            jnp.where(
                shift < edge + block_rows,
                shift - edge + 2 * plan.outer,
                shift - block_rows + far_slots,
            ),
        ),
    )
    every = jnp.arange(plan.places, dtype=jnp.int32)[None, None, :]
    entry = jnp.arange(entries, dtype=jnp.int32)[None, :, None]
    hit = places[:, :, None] == every
    inverse = entries + jnp.sum(jnp.where(hit, entry - entries, 0), axis=1)

    band, inner = make_band(plan, side, inverse, hamiltonian.T, start)

    inner = run_middle(plan, side, away, near, band, inner)
    value, listed, *sends = run_first(plan, side, asked, far, band, inner, start)
    away, far, near = exchange(listed, sends)
    inner = run_inner(plan, value, near, band)
    far = split_far(plan, after(far, inner))
    return run_second(plan, side, away, far, band, inner, value, start)


def solution(mesh):
    placed = (P("rows", None), P("rows", None), P("rows", None), P("rows", None))
    return jax.shard_map(
        per_device, mesh=mesh, in_specs=placed, out_specs=P("rows", None), check_vma=False
    )
```

```python
import functools

import jax
import jax.numpy as jnp
from jax import lax
from jax.experimental import pallas as pl
from jax.experimental.pallas import tpu as pltpu
from jax.sharding import PartitionSpec as P

CENTER = 0.25
HALF_WIDTH = 1.5
REACH = 13
F32 = jnp.float32
VMEM = pl.BlockSpec(memory_space=pltpu.VMEM)
HBM = pl.BlockSpec(memory_space=pltpu.HBM)
SMEM = pl.BlockSpec(memory_space=pltpu.SMEM)


def partner(value, axis, bit):
    mask = 2**bit
    pairs = [(source, source ^ mask) for source in range(lax.axis_size(axis))]
    return lax.ppermute(value, axis, pairs)


def swap_chips(value, axis):
    devices = lax.axis_size(axis)
    pairs = [(i, (i + (1 if i % 2 else -1)) % devices) for i in range(devices)]
    return lax.ppermute(value, axis, pairs)


def split(value):
    high = value.astype(jnp.bfloat16)
    return high, (value - high.astype(F32)).astype(jnp.bfloat16)


def fold(sums):
    width, tile = sums.shape[0] // 2, sums.shape[1] // 2
    small = sums[width:, tile:] + sums[width:, :tile] + sums[:width, tile:]
    return small + sums[:width, :tile]


def params(limit):
    return pltpu.CompilerParams(vmem_limit_bytes=limit * 2**20)


def cost(flops, moved):
    return pl.CostEstimate(flops=flops, bytes_accessed=moved, transcendentals=0)


class Plan:
    def __init__(self, size, rows, width, slots):
        self.size, self.rows, self.width = size, rows, width
        self.tile = 2 * size
        self.pairs = rows // self.tile
        self.near = (REACH + 1) // 2
        self.far = slots * size // self.tile
        self.edge = self.near * self.tile
        self.half = width // 2
        self.whole = self.edge - self.tile
        self.outer = 2 * self.near + self.far
        self.places = 2 * (self.outer + self.pairs)
        self.depth = max(sum(run[2] for run in self.runs(p)) for p in range(self.pairs))

    def outer_range(self, p):
        extra = p + self.near - self.pairs + 1
        return min(p, self.near), self.near + self.far + max(0, extra)

    def spans(self, p):
        begin, end = self.outer_range(p)
        row = self.near - begin
        return {
            "away": (begin, self.near, 0),
            "far": (0, self.far, row),
            "near": (0, end - self.near - self.far, row + self.far),
        }

    def own_range(self, p):
        return max(0, p - self.near), min(self.pairs, p + self.near + 1)

    def runs(self, p):
        begin, end = self.outer_range(p)
        rows = (end - begin) * self.tile
        outer = (2 * begin, 0, rows)
        begin, end = self.own_range(p)
        return outer, (2 * (self.outer + begin), rows, (end - begin) * self.tile)

    def mirrored(self, t, side):
        return t + side[0] * (self.pairs - 1 - 2 * t)


def write_far(plan, side, asked, source, write):
    tile, size = plan.tile, plan.size
    lane = lax.broadcasted_iota(jnp.int32, (source.shape[0], tile), 1)

    def block(slot, want):
        index = lax.rem(asked[0, slot] + 2 * plan.pairs, 2 * plan.pairs)
        at = plan.mirrored(lax.div(index, 2), side) * tile
        value = source[:, pl.ds(pl.multiple_of(at, tile), tile)]
        return jnp.where(lax.rem(index, 2) == want, value, pltpu.roll(value, size, 1))

    for t in range(plan.far):
        value = jnp.where(lane < size, block(2 * t, 0), block(2 * t + 1, 1))
        write(t * tile, value)


def write_sends(plan, side, at, value, to_away, to_near):
    tile, half, skip = plan.tile, plan.half, plan.rows - plan.edge
    if at < plan.whole:
        to_away[:, at : at + tile] = value[:half]
        to_away[:, plan.edge + at : plan.edge + at + tile] = value[half:]
    elif at == plan.whole:
        lane = lax.broadcasted_iota(jnp.int32, (half, tile), 1)
        turned = pltpu.roll(value, plan.size, 1)
        even = jnp.where(lane < plan.size, value[:half], turned[half:])
        odd = jnp.where(lane < plan.size, turned[:half], value[half:])
        to_away[:, at : at + tile] = jnp.where(side[0] == 0, even, odd)
    if at >= skip:
        to_near[:, at - skip : at - skip + tile] = value


def away_tile(plan, side, away, t):
    at, tile = t * plan.tile, plan.tile
    packed = away[:, at : at + tile]
    if at < plan.whole:
        rest = away[:, plan.edge + at : plan.edge + at + tile]
        return jnp.concatenate([packed, rest], axis=0)
    turned = pltpu.roll(packed, plan.size, 1)
    even = jnp.concatenate([turned, packed], axis=0)
    odd = jnp.concatenate([packed, turned], axis=0)
    return jnp.where(side[0] == 0, even, odd)


def send_shapes(plan):
    shapes = ((plan.half, plan.edge + plan.whole), (plan.width, plan.edge))
    return [jax.ShapeDtypeStruct(shape, F32) for shape in shapes]


def pack_kernel(plan, chunks, natural, codes, turned, held, *rest):
    sends, staged, sems = rest[:-2], *rest[-2:]
    side = parity()
    tile, count = plan.tile, plan.pairs // chunks
    step = count * tile

    def fetch(c):
        return pltpu.make_async_copy(
            natural.at[pl.ds(c * step, step), :],
            staged.at[pl.ds(c * step, step), :],
            sems.at[c],
        )

    for c in range(chunks):
        fetch(c).start()
    copy = pltpu.make_async_copy(codes, held, sems.at[chunks])
    copy.start()
    for c in range(chunks):
        fetch(c).wait()
    for t in range(plan.pairs):
        at = pl.multiple_of(plan.mirrored(t, side) * tile, tile)
        value = staged[pl.ds(at, tile), :].T
        turned[:, t * tile : (t + 1) * tile] = value
        write_sends(plan, side, t * tile, value, *sends)
    copy.wait()


def pack(plan, natural, codes):
    chunks = 4 if plan.pairs % 4 == 0 else 1
    return pl.pallas_call(
        functools.partial(pack_kernel, plan, chunks),
        out_shape=[
            pltpu.VMEM((plan.width, plan.rows), F32),
            pltpu.VMEM(codes.shape, codes.dtype),
        ]
        + send_shapes(plan),
        in_specs=[HBM, HBM],
        out_specs=[VMEM] * 4,
        scratch_shapes=[
            pltpu.VMEM((plan.rows, plan.width), F32),
            pltpu.SemaphoreType.DMA((chunks + 1,)),
        ],
        compiler_params=params(8),
        name="pack",
    )(*(pltpu.with_memory_space_constraint(x, pltpu.HBM) for x in (natural, codes)))


def far_kernel(plan, asked, turned, out):
    def write(at, value):
        out[:, at : at + plan.tile] = value

    write_far(plan, parity(), asked, turned, write)


def gather_far(plan, asked, turned):
    return pl.pallas_call(
        functools.partial(far_kernel, plan),
        out_shape=jax.ShapeDtypeStruct((plan.width, plan.far * plan.tile), F32),
        in_specs=[SMEM, VMEM],
        out_specs=VMEM,
        compiler_params=params(8),
        name="far",
    )(asked, turned)


def own_halves(plan, vectors, halves):
    for at in range(0, plan.rows, plan.tile):
        high, low = split(vectors[:, at : at + plan.tile])
        halves[: plan.width, at : at + plan.tile] = high
        halves[plan.width :, at : at + plan.tile] = low


def own_product(plan, p, halves, band):
    begin, end = (plan.tile * bound for bound in plan.own_range(p))
    _, (_, row, rows) = plan.runs(p)
    vectors = halves[:, begin:end]
    return fold(jnp.dot(vectors, band[p, row : row + rows, :], preferred_element_type=F32))


def band_kernel(
    plan, depth, table, ham_t, vectors, band, inner, staged, halves, inverse, sems
):
    size, tile = plan.size, plan.tile
    side = parity()
    group = staged.shape[2] // tile
    units = plan.pairs // group
    lane = lax.broadcasted_iota(jnp.int32, (size, tile), 1)

    def fetch(u):
        natural = u + side[0] * (units - 1 - 2 * u)
        at = pl.multiple_of(natural * group * tile, group * tile)
        held = staged.at[u, pl.ds(0, depth), :]
        return pltpu.make_async_copy(ham_t.at[:, pl.ds(at, group * tile)], held, sems.at[u])

    def store(p, at, high, low):
        band[p, at : at + size, :tile] = high
        band[p, at : at + size, tile:] = low

    copy = pltpu.make_async_copy(table, inverse, sems.at[units])
    copy.start()
    for u in range(units):
        fetch(u).start()
    for u in range(units):
        staged[u, depth:, :] = jnp.zeros((size, group * tile), F32)
    own_halves(plan, vectors, halves)
    copy.wait()

    for p in range(plan.pairs):
        u, t = p // group, p % group
        if t == 0:
            fetch(u).wait()
        lanes = pl.multiple_of((t + side[0] * (group - 1 - 2 * t)) * tile, tile)
        row = 2 * plan.mirrored(p, side)

        def block(q):
            even = pl.multiple_of(inverse[row, q] * size, size)
            odd = pl.multiple_of(inverse[row + 1, q] * size, size)
            first = staged[u, pl.ds(even, size), pl.ds(lanes, tile)]
            second = staged[u, pl.ds(odd, size), pl.ds(lanes, tile)]
            return jnp.where(lane < size, first, second)

        ready = None if p == 0 else own_product(plan, p - 1, halves, band)
        places = [(place + q, at + q * size) for place, at, rows in plan.runs(p) for q in range(rows // size)]
        waiting = []
        for begin in range(0, len(places), 2):
            batch = [(at, *split(block(q))) for q, at in places[begin : begin + 2]]
            for entry in waiting:
                store(p, *entry)
            waiting = batch
        for entry in waiting:
            store(p, *entry)
        if p > 0:
            inner[:, (p - 1) * tile : p * tile] = ready
    p = plan.pairs - 1
    inner[:, p * tile : (p + 1) * tile] = own_product(plan, p, halves, band)


def make_band(plan, inverse, ham_t, vectors):
    depth, rows = ham_t.shape
    size, tile = plan.size, plan.tile
    group = 2 if plan.pairs % 2 == 0 else 1
    return pl.pallas_call(
        functools.partial(band_kernel, plan, depth),
        out_shape=[
            pltpu.VMEM((plan.pairs, plan.depth, 2 * tile), jnp.bfloat16),
            pltpu.VMEM((plan.width, rows), F32),
        ],
        in_specs=[VMEM, HBM, VMEM],
        out_specs=[VMEM, VMEM],
        scratch_shapes=[
            pltpu.VMEM((plan.pairs // group, depth + size, group * tile), F32),
            pltpu.VMEM((2 * plan.width, rows), jnp.bfloat16),
            pltpu.SMEM(inverse.shape, inverse.dtype),
            pltpu.SemaphoreType.DMA((plan.pairs // group + 1,)),
        ],
        compiler_params=params(14),
        cost_estimate=cost(0, 2 * 4 * depth * rows),
        name="band",
    )(inverse, pltpu.with_memory_space_constraint(ham_t, pltpu.HBM), vectors)


def put_halves(plan, halves, tiles):
    for t, value in enumerate(tiles):
        high, low = split(value)
        halves[: plan.width, t * plan.tile : (t + 1) * plan.tile] = high
        halves[plan.width :, t * plan.tile : (t + 1) * plan.tile] = low


def message_product(plan, name, p, halves, band):
    first, last, row = plan.spans(p)[name]
    if first == last:
        return 0.0
    rows = slice(row * plan.tile, (row + last - first) * plan.tile)
    vectors = halves[:, first * plan.tile : last * plan.tile]
    return fold(jnp.dot(vectors, band[p, rows, :], preferred_element_type=F32))


def halves_scratch(plan, tiles):
    return pltpu.VMEM((2 * plan.width, tiles * plan.tile), jnp.bfloat16)


def near_tiles(plan, near):
    tile = plan.tile
    return [near[:, t * tile : (t + 1) * tile] for t in reversed(range(plan.near))]


def away_tiles(plan, side, away):
    return [away_tile(plan, side, away, t) for t in reversed(range(plan.near))]


def middle_kernel(plan, away, near, band, inner, out, away_halves, near_halves):
    put_halves(plan, away_halves, away_tiles(plan, parity(), away))
    put_halves(plan, near_halves, near_tiles(plan, near))
    for p in range(plan.pairs):
        lanes = slice(p * plan.tile, (p + 1) * plan.tile)
        total = inner[:, lanes] + message_product(plan, "away", p, away_halves, band)
        out[:, lanes] = total + message_product(plan, "near", p, near_halves, band)


def run_middle(plan, away, near, band, inner):
    return pl.pallas_call(
        functools.partial(middle_kernel, plan),
        out_shape=pltpu.VMEM((plan.width, plan.rows), F32),
        in_specs=[VMEM] * 4,
        out_specs=VMEM,
        scratch_shapes=[halves_scratch(plan, plan.near)] * 2,
        compiler_params=params(8),
        cost_estimate=cost(8 * plan.width * plan.rows**2, 0),
        name="middle",
    )(away, near, band, inner)


def inner_kernel(plan, vectors, near, band, out, halves, near_halves):
    own_halves(plan, vectors, halves)
    put_halves(plan, near_halves, near_tiles(plan, near))
    for p in range(plan.pairs):
        total = own_product(plan, p, halves, band)
        total += message_product(plan, "near", p, near_halves, band)
        out[:, p * plan.tile : (p + 1) * plan.tile] = total


def run_inner(plan, vectors, near, band):
    return pl.pallas_call(
        functools.partial(inner_kernel, plan),
        out_shape=pltpu.VMEM((plan.width, plan.rows), F32),
        in_specs=[VMEM] * 3,
        out_specs=VMEM,
        scratch_shapes=[halves_scratch(plan, plan.pairs), halves_scratch(plan, plan.near)],
        compiler_params=params(8),
        cost_estimate=cost(8 * plan.width * plan.rows**2, 0),
        name="inner",
    )(vectors, near, band)


def far_tiles(plan, far):
    return [far[:, t * plan.tile : (t + 1) * plan.tile] for t in range(plan.far)]


def far_split_kernel(plan, far, halves):
    put_halves(plan, halves, far_tiles(plan, far))


def split_far(plan, far):
    return pl.pallas_call(
        functools.partial(far_split_kernel, plan),
        out_shape=halves_scratch(plan, plan.far),
        in_specs=[VMEM],
        out_specs=VMEM,
        compiler_params=params(8),
        cost_estimate=cost(16 * plan.width * plan.rows**2, 0),
        name="split",
    )(far)


def first_kernel(
    plan, listed, far, band, inner, own, value, to_far, to_away, to_near, halves, asked, sem
):
    copy = pltpu.make_async_copy(listed, asked, sem)
    copy.start()
    side = parity()
    put_halves(plan, halves, far_tiles(plan, far))
    for p in range(plan.pairs):
        lanes = slice(p * plan.tile, (p + 1) * plan.tile)
        product = inner[:, lanes] - CENTER * own[:, lanes]
        product += message_product(plan, "far", p, halves, band)
        term = product * (1.0 / HALF_WIDTH)
        value[:, lanes] = term
        write_sends(plan, side, lanes.start, term, to_away, to_near)

    def write(at, term):
        to_far[:, at : at + plan.tile] = term

    copy.wait()
    write_far(plan, side, asked, value, write)


def run_first(plan, asked, far, band, inner, own):
    shapes = [jax.ShapeDtypeStruct(far.shape, F32)] + send_shapes(plan)
    return pl.pallas_call(
        functools.partial(first_kernel, plan),
        out_shape=[pltpu.VMEM((plan.width, plan.rows), F32)] + shapes,
        in_specs=[VMEM] * 5,
        out_specs=[VMEM] * (1 + len(shapes)),
        scratch_shapes=[
            halves_scratch(plan, plan.far),
            pltpu.SMEM(asked.shape, asked.dtype),
            pltpu.SemaphoreType.DMA,
        ],
        compiler_params=params(8),
        cost_estimate=cost(2 * plan.width * plan.rows**2, 0),
        name="first",
    )(asked, far, band, inner, own)


def second_kernel(plan, away, far, band, inner, own, start, out, halves, held, sems):
    side = parity()
    put_halves(plan, halves, away_tiles(plan, side, away))
    copies = []
    for p in range(plan.pairs):
        lanes = slice(p * plan.tile, (p + 1) * plan.tile)
        product = inner[:, lanes] - CENTER * own[:, lanes]
        product += message_product(plan, "far", p, far, band)
        product += message_product(plan, "away", p, halves, band)
        term = 2.0 / HALF_WIDTH * product - start[:, lanes]
        place = pl.multiple_of(plan.mirrored(p, side) * plan.tile, plan.tile)
        held[p] = term.T
        copies.append(
            pltpu.make_async_copy(held.at[p], out.at[pl.ds(place, plan.tile), :], sems.at[p])
        )
        copies[-1].start()
    for copy in copies:
        copy.wait()


def run_second(plan, away, far, band, inner, own, start):
    return pl.pallas_call(
        functools.partial(second_kernel, plan),
        out_shape=jax.ShapeDtypeStruct((plan.rows, plan.width), F32),
        in_specs=[VMEM] * 6,
        out_specs=HBM,
        scratch_shapes=[
            halves_scratch(plan, plan.near),
            pltpu.VMEM((plan.pairs, plan.tile, plan.width), F32),
            pltpu.SemaphoreType.DMA((plan.pairs,)),
        ],
        compiler_params=params(8),
        cost_estimate=cost(2 * plan.width * plan.rows**2, 0),
        name="second",
    )(away, far, band, inner, own, start)


def parity():
    return (lax.rem(lax.axis_index("rows"), 2),)


def after(value, *others):
    return lax.optimization_barrier((value, *others))[0]


def per_device(hamiltonian, subspace, block_cols, far_list):
    block_rows, entries = block_cols.shape
    size = hamiltonian.shape[1] // entries
    device_count = lax.axis_size("rows")
    first_row = lax.axis_index("rows") * block_rows
    block_total = block_rows * device_count
    swap_level = (device_count // 8).bit_length() - 1
    plan = Plan(size, block_rows * size, subspace.shape[1], far_list.shape[1])

    side = (lax.axis_index("rows") % 2).astype(jnp.int32).reshape(1)

    def exchange(listed, sends):
        to_away, to_near = sends
        far = partner(listed, "rows", swap_level)
        return swap_chips(to_away, "rows"), far, partner(to_near, "rows", 0)

    start, block_cols, *sends = pack(plan, subspace, block_cols)
    asked = partner(after(far_list, start), "rows", swap_level)
    listed = gather_far(plan, asked, start)
    away, far, near = exchange(listed, (sends[0], after(sends[1], listed)))

    block_cols = after(block_cols, listed)
    edge, far_slots = 2 * plan.near, 2 * plan.far
    shift = block_cols - first_row + edge
    shift = jnp.where(shift < 0, shift + block_total, shift)
    shift = jnp.where(shift >= block_total, shift - block_total, shift)
    last = block_rows + 2 * edge - 2
    shift = shift + side[0] * (last - 4 * (shift >> 1))
    places = jnp.where(
        block_cols >= block_total,
        edge + block_cols - block_total,
        jnp.where(
            shift < edge,
            shift,
            jnp.where(
                shift < edge + block_rows,
                shift - edge + 2 * plan.outer,
                shift - block_rows + far_slots,
            ),
        ),
    )
    every = jnp.arange(plan.places, dtype=jnp.int32)[None, None, :]
    entry = jnp.arange(entries, dtype=jnp.int32)[None, :, None]
    hit = places[:, :, None] == every
    inverse = entries + jnp.sum(jnp.where(hit, entry - entries, 0), axis=1)

    band, inner = make_band(plan, inverse, hamiltonian.T, start)

    inner = run_middle(plan, away, near, band, inner)
    value, listed, *sends = run_first(plan, asked, far, band, inner, start)
    away, far, near = exchange(listed, sends)
    inner = run_inner(plan, value, near, band)
    far = split_far(plan, after(far, inner))
    return run_second(plan, away, far, band, inner, value, start)


def solution(mesh):
    placed = (P("rows", None), P("rows", None), P("rows", None), P("rows", None))
    return jax.shard_map(
        per_device, mesh=mesh, in_specs=placed, out_specs=P("rows", None), check_vma=False
    )
```

```python
import functools

import jax
import jax.numpy as jnp
from jax import lax
from jax.experimental import pallas as pl
from jax.experimental.pallas import tpu as pltpu
from jax.sharding import PartitionSpec as P

CENTER = 0.25
HALF_WIDTH = 1.5
REACH = 13
F32 = jnp.float32
VMEM = pl.BlockSpec(memory_space=pltpu.VMEM)
HBM = pl.BlockSpec(memory_space=pltpu.HBM)
SMEM = pl.BlockSpec(memory_space=pltpu.SMEM)


def partner(value, axis, bit):
    mask = 2**bit
    pairs = [(source, source ^ mask) for source in range(lax.axis_size(axis))]
    return lax.ppermute(value, axis, pairs)


def swap_chips(value, axis):
    devices = lax.axis_size(axis)
    pairs = [(i, (i + (1 if i % 2 else -1)) % devices) for i in range(devices)]
    return lax.ppermute(value, axis, pairs)


def split(value):
    high = value.astype(jnp.bfloat16)
    return high, (value - high.astype(F32)).astype(jnp.bfloat16)


def fold(sums):
    width, tile = sums.shape[0] // 2, sums.shape[1] // 2
    small = sums[width:, tile:] + sums[width:, :tile] + sums[:width, tile:]
    return small + sums[:width, :tile]


def params(limit):
    return pltpu.CompilerParams(vmem_limit_bytes=limit * 2**20)


def cost(flops, moved):
    return pl.CostEstimate(flops=flops, bytes_accessed=moved, transcendentals=0)


class Plan:
    def __init__(self, size, rows, width, slots):
        self.size, self.rows, self.width = size, rows, width
        self.tile = 2 * size
        self.pairs = rows // self.tile
        self.near = (REACH + 1) // 2
        self.far = slots * size // self.tile
        self.edge = self.near * self.tile
        self.half = width // 2
        self.whole = self.edge - self.tile
        self.outer = 2 * self.near + self.far
        self.places = 2 * (self.outer + self.pairs)
        self.depth = max(sum(run[2] for run in self.runs(p)) for p in range(self.pairs))

    def outer_range(self, p):
        extra = p + self.near - self.pairs + 1
        return min(p, self.near), self.near + self.far + max(0, extra)

    def spans(self, p):
        begin, end = self.outer_range(p)
        row = self.near - begin
        return {
            "away": (begin, self.near, 0),
            "far": (0, self.far, row),
            "near": (0, end - self.near - self.far, row + self.far),
        }

    def own_range(self, p):
        return max(0, p - self.near), min(self.pairs, p + self.near + 1)

    def runs(self, p):
        begin, end = self.outer_range(p)
        rows = (end - begin) * self.tile
        outer = (2 * begin, 0, rows)
        begin, end = self.own_range(p)
        return outer, (2 * (self.outer + begin), rows, (end - begin) * self.tile)

    def mirrored(self, t, side):
        return t + side[0] * (self.pairs - 1 - 2 * t)


def write_far(plan, side, asked, source, write):
    tile, size = plan.tile, plan.size
    lane = lax.broadcasted_iota(jnp.int32, (source.shape[0], tile), 1)

    def block(slot, want):
        index = lax.rem(asked[0, slot] + 2 * plan.pairs, 2 * plan.pairs)
        at = plan.mirrored(lax.div(index, 2), side) * tile
        value = source[:, pl.ds(pl.multiple_of(at, tile), tile)]
        return jnp.where(lax.rem(index, 2) == want, value, pltpu.roll(value, size, 1))

    for t in range(plan.far):
        value = jnp.where(lane < size, block(2 * t, 0), block(2 * t + 1, 1))
        write(t * tile, value)


def write_sends(plan, side, at, value, to_away, to_near):
    tile, half, skip = plan.tile, plan.half, plan.rows - plan.edge
    if at < plan.whole:
        to_away[:, at : at + tile] = value[:half]
        to_away[:, plan.edge + at : plan.edge + at + tile] = value[half:]
    elif at == plan.whole:
        lane = lax.broadcasted_iota(jnp.int32, (half, tile), 1)
        turned = pltpu.roll(value, plan.size, 1)
        even = jnp.where(lane < plan.size, value[:half], turned[half:])
        odd = jnp.where(lane < plan.size, turned[:half], value[half:])
        to_away[:, at : at + tile] = jnp.where(side[0] == 0, even, odd)
    if at >= skip:
        to_near[:, at - skip : at - skip + tile] = value


def away_tile(plan, side, away, t):
    at, tile = t * plan.tile, plan.tile
    packed = away[:, at : at + tile]
    if at < plan.whole:
        rest = away[:, plan.edge + at : plan.edge + at + tile]
        return jnp.concatenate([packed, rest], axis=0)
    turned = pltpu.roll(packed, plan.size, 1)
    even = jnp.concatenate([turned, packed], axis=0)
    odd = jnp.concatenate([packed, turned], axis=0)
    return jnp.where(side[0] == 0, even, odd)


def send_shapes(plan):
    shapes = ((plan.half, plan.edge + plan.whole), (plan.width, plan.edge))
    return [jax.ShapeDtypeStruct(shape, F32) for shape in shapes]


def pack_kernel(plan, chunks, natural, codes, turned, held, *rest):
    sends, staged, sems = rest[:-2], *rest[-2:]
    side = parity()
    tile, count = plan.tile, plan.pairs // chunks
    step = count * tile

    def fetch(c):
        at = pl.multiple_of((c + side[0] * (chunks - 1 - 2 * c)) * step, step)
        return pltpu.make_async_copy(
            natural.at[pl.ds(at, step), :], staged.at[pl.ds(c * step, step), :], sems.at[c]
        )

    for c in range(chunks):
        fetch(c).start()
    copy = pltpu.make_async_copy(codes, held, sems.at[chunks])
    copy.start()
    for t in range(plan.pairs):
        c, u = t // count, t % count
        if u == 0:
            fetch(c).wait()
        at = c * step + (u + side[0] * (count - 1 - 2 * u)) * tile
        at = pl.multiple_of(at, tile)
        value = staged[pl.ds(at, tile), :].T
        turned[:, t * tile : (t + 1) * tile] = value
        write_sends(plan, side, t * tile, value, *sends)
    copy.wait()


def pack(plan, natural, codes):
    chunks = 4 if plan.pairs % 4 == 0 else 1
    return pl.pallas_call(
        functools.partial(pack_kernel, plan, chunks),
        out_shape=[
            pltpu.VMEM((plan.width, plan.rows), F32),
            pltpu.VMEM(codes.shape, codes.dtype),
        ]
        + send_shapes(plan),
        in_specs=[HBM, HBM],
        out_specs=[VMEM] * 4,
        scratch_shapes=[
            pltpu.VMEM((plan.rows, plan.width), F32),
            pltpu.SemaphoreType.DMA((chunks + 1,)),
        ],
        compiler_params=params(8),
        name="pack",
    )(*(pltpu.with_memory_space_constraint(x, pltpu.HBM) for x in (natural, codes)))


def far_kernel(plan, asked, turned, out):
    def write(at, value):
        out[:, at : at + plan.tile] = value

    write_far(plan, parity(), asked, turned, write)


def gather_far(plan, asked, turned):
    return pl.pallas_call(
        functools.partial(far_kernel, plan),
        out_shape=jax.ShapeDtypeStruct((plan.width, plan.far * plan.tile), F32),
        in_specs=[SMEM, VMEM],
        out_specs=VMEM,
        compiler_params=params(8),
        name="far",
    )(asked, turned)


def own_halves(plan, vectors, halves):
    for at in range(0, plan.rows, plan.tile):
        high, low = split(vectors[:, at : at + plan.tile])
        halves[: plan.width, at : at + plan.tile] = high
        halves[plan.width :, at : at + plan.tile] = low


def own_product(plan, p, halves, band):
    begin, end = (plan.tile * bound for bound in plan.own_range(p))
    _, (_, row, rows) = plan.runs(p)
    vectors = halves[:, begin:end]
    return fold(jnp.dot(vectors, band[p, row : row + rows, :], preferred_element_type=F32))


def band_kernel(
    plan, depth, table, ham_t, vectors, band, inner, staged, halves, inverse, sems
):
    size, tile = plan.size, plan.tile
    side = parity()
    group = staged.shape[2] // tile
    units = plan.pairs // group
    lane = lax.broadcasted_iota(jnp.int32, (size, tile), 1)

    def fetch(u):
        natural = u + side[0] * (units - 1 - 2 * u)
        at = pl.multiple_of(natural * group * tile, group * tile)
        held = staged.at[u, pl.ds(0, depth), :]
        return pltpu.make_async_copy(ham_t.at[:, pl.ds(at, group * tile)], held, sems.at[u])

    def store(p, at, high, low):
        band[p, at : at + size, :tile] = high
        band[p, at : at + size, tile:] = low

    copy = pltpu.make_async_copy(table, inverse, sems.at[units])
    copy.start()
    for u in range(units):
        fetch(u).start()
    for u in range(units):
        staged[u, depth:, :] = jnp.zeros((size, group * tile), F32)
    own_halves(plan, vectors, halves)
    copy.wait()

    for p in range(plan.pairs):
        u, t = p // group, p % group
        if t == 0:
            fetch(u).wait()
        lanes = pl.multiple_of((t + side[0] * (group - 1 - 2 * t)) * tile, tile)
        row = 2 * plan.mirrored(p, side)

        def block(q):
            even = pl.multiple_of(inverse[row, q] * size, size)
            odd = pl.multiple_of(inverse[row + 1, q] * size, size)
            first = staged[u, pl.ds(even, size), pl.ds(lanes, tile)]
            second = staged[u, pl.ds(odd, size), pl.ds(lanes, tile)]
            return jnp.where(lane < size, first, second)

        ready = None if p == 0 else own_product(plan, p - 1, halves, band)
        places = [(place + q, at + q * size) for place, at, rows in plan.runs(p) for q in range(rows // size)]
        waiting = []
        for begin in range(0, len(places), 2):
            batch = [(at, *split(block(q))) for q, at in places[begin : begin + 2]]
            for entry in waiting:
                store(p, *entry)
            waiting = batch
        for entry in waiting:
            store(p, *entry)
        if p > 0:
            inner[:, (p - 1) * tile : p * tile] = ready
    p = plan.pairs - 1
    inner[:, p * tile : (p + 1) * tile] = own_product(plan, p, halves, band)


def make_band(plan, inverse, ham_t, vectors):
    depth, rows = ham_t.shape
    size, tile = plan.size, plan.tile
    group = 2 if plan.pairs % 2 == 0 else 1
    return pl.pallas_call(
        functools.partial(band_kernel, plan, depth),
        out_shape=[
            pltpu.VMEM((plan.pairs, plan.depth, 2 * tile), jnp.bfloat16),
            pltpu.VMEM((plan.width, rows), F32),
        ],
        in_specs=[VMEM, HBM, VMEM],
        out_specs=[VMEM, VMEM],
        scratch_shapes=[
            pltpu.VMEM((plan.pairs // group, depth + size, group * tile), F32),
            pltpu.VMEM((2 * plan.width, rows), jnp.bfloat16),
            pltpu.SMEM(inverse.shape, inverse.dtype),
            pltpu.SemaphoreType.DMA((plan.pairs // group + 1,)),
        ],
        compiler_params=params(14),
        cost_estimate=cost(0, 2 * 4 * depth * rows),
        name="band",
    )(inverse, pltpu.with_memory_space_constraint(ham_t, pltpu.HBM), vectors)


def put_halves(plan, halves, tiles):
    for t, value in enumerate(tiles):
        high, low = split(value)
        halves[: plan.width, t * plan.tile : (t + 1) * plan.tile] = high
        halves[plan.width :, t * plan.tile : (t + 1) * plan.tile] = low


def message_product(plan, name, p, halves, band):
    first, last, row = plan.spans(p)[name]
    if first == last:
        return 0.0
    rows = slice(row * plan.tile, (row + last - first) * plan.tile)
    vectors = halves[:, first * plan.tile : last * plan.tile]
    return fold(jnp.dot(vectors, band[p, rows, :], preferred_element_type=F32))


def halves_scratch(plan, tiles):
    return pltpu.VMEM((2 * plan.width, tiles * plan.tile), jnp.bfloat16)


def near_tiles(plan, near):
    tile = plan.tile
    return [near[:, t * tile : (t + 1) * tile] for t in reversed(range(plan.near))]


def away_tiles(plan, side, away):
    return [away_tile(plan, side, away, t) for t in reversed(range(plan.near))]


def middle_kernel(plan, away, near, band, inner, out, away_halves, near_halves):
    put_halves(plan, away_halves, away_tiles(plan, parity(), away))
    put_halves(plan, near_halves, near_tiles(plan, near))
    for p in range(plan.pairs):
        lanes = slice(p * plan.tile, (p + 1) * plan.tile)
        total = inner[:, lanes] + message_product(plan, "away", p, away_halves, band)
        out[:, lanes] = total + message_product(plan, "near", p, near_halves, band)


def run_middle(plan, away, near, band, inner):
    return pl.pallas_call(
        functools.partial(middle_kernel, plan),
        out_shape=pltpu.VMEM((plan.width, plan.rows), F32),
        in_specs=[VMEM] * 4,
        out_specs=VMEM,
        scratch_shapes=[halves_scratch(plan, plan.near)] * 2,
        compiler_params=params(8),
        cost_estimate=cost(8 * plan.width * plan.rows**2, 0),
        name="middle",
    )(away, near, band, inner)


def inner_kernel(plan, vectors, near, band, out, halves, near_halves):
    own_halves(plan, vectors, halves)
    put_halves(plan, near_halves, near_tiles(plan, near))
    for p in range(plan.pairs):
        total = own_product(plan, p, halves, band)
        total += message_product(plan, "near", p, near_halves, band)
        out[:, p * plan.tile : (p + 1) * plan.tile] = total


def run_inner(plan, vectors, near, band):
    return pl.pallas_call(
        functools.partial(inner_kernel, plan),
        out_shape=pltpu.VMEM((plan.width, plan.rows), F32),
        in_specs=[VMEM] * 3,
        out_specs=VMEM,
        scratch_shapes=[halves_scratch(plan, plan.pairs), halves_scratch(plan, plan.near)],
        compiler_params=params(8),
        cost_estimate=cost(8 * plan.width * plan.rows**2, 0),
        name="inner",
    )(vectors, near, band)


def far_tiles(plan, far):
    return [far[:, t * plan.tile : (t + 1) * plan.tile] for t in range(plan.far)]


def far_split_kernel(plan, far, halves):
    put_halves(plan, halves, far_tiles(plan, far))


def split_far(plan, far):
    return pl.pallas_call(
        functools.partial(far_split_kernel, plan),
        out_shape=halves_scratch(plan, plan.far),
        in_specs=[VMEM],
        out_specs=VMEM,
        compiler_params=params(8),
        cost_estimate=cost(16 * plan.width * plan.rows**2, 0),
        name="split",
    )(far)


def first_kernel(
    plan, listed, far, band, inner, own, value, to_far, to_away, to_near, halves, asked, sem
):
    copy = pltpu.make_async_copy(listed, asked, sem)
    copy.start()
    side = parity()
    put_halves(plan, halves, far_tiles(plan, far))
    for p in range(plan.pairs):
        lanes = slice(p * plan.tile, (p + 1) * plan.tile)
        product = inner[:, lanes] - CENTER * own[:, lanes]
        product += message_product(plan, "far", p, halves, band)
        term = product * (1.0 / HALF_WIDTH)
        value[:, lanes] = term
        write_sends(plan, side, lanes.start, term, to_away, to_near)

    def write(at, term):
        to_far[:, at : at + plan.tile] = term

    copy.wait()
    write_far(plan, side, asked, value, write)


def run_first(plan, asked, far, band, inner, own):
    shapes = [jax.ShapeDtypeStruct(far.shape, F32)] + send_shapes(plan)
    return pl.pallas_call(
        functools.partial(first_kernel, plan),
        out_shape=[pltpu.VMEM((plan.width, plan.rows), F32)] + shapes,
        in_specs=[VMEM] * 5,
        out_specs=[VMEM] * (1 + len(shapes)),
        scratch_shapes=[
            halves_scratch(plan, plan.far),
            pltpu.SMEM(asked.shape, asked.dtype),
            pltpu.SemaphoreType.DMA,
        ],
        compiler_params=params(8),
        cost_estimate=cost(2 * plan.width * plan.rows**2, 0),
        name="first",
    )(asked, far, band, inner, own)


def second_kernel(plan, away, far, band, inner, own, start, out, halves, held, sems):
    side = parity()
    put_halves(plan, halves, away_tiles(plan, side, away))
    halves[:, plan.edge :] = far[...]
    copies = []
    for p in reversed(range(plan.pairs)):
        lanes = slice(p * plan.tile, (p + 1) * plan.tile)
        product = inner[:, lanes] - CENTER * own[:, lanes]
        begin = plan.outer_range(p)[0] * plan.tile
        vectors = far[...] if begin == plan.edge else halves[:, begin:]
        rows = band[p, : vectors.shape[1], :]
        product += fold(jnp.dot(vectors, rows, preferred_element_type=F32))
        term = 2.0 / HALF_WIDTH * product - start[:, lanes]
        place = pl.multiple_of(plan.mirrored(p, side) * plan.tile, plan.tile)
        held[p] = term.T
        copies.append(
            pltpu.make_async_copy(held.at[p], out.at[pl.ds(place, plan.tile), :], sems.at[p])
        )
        copies[-1].start()
    for copy in copies:
        copy.wait()


def run_second(plan, away, far, band, inner, own, start):
    return pl.pallas_call(
        functools.partial(second_kernel, plan),
        out_shape=jax.ShapeDtypeStruct((plan.rows, plan.width), F32),
        in_specs=[VMEM] * 6,
        out_specs=HBM,
        scratch_shapes=[
            halves_scratch(plan, plan.near + plan.far),
            pltpu.VMEM((plan.pairs, plan.tile, plan.width), F32),
            pltpu.SemaphoreType.DMA((plan.pairs,)),
        ],
        compiler_params=params(8),
        cost_estimate=cost(2 * plan.width * plan.rows**2, 0),
        name="second",
    )(away, far, band, inner, own, start)


def parity():
    return (lax.rem(lax.axis_index("rows"), 2),)


def after(value, *others):
    return lax.optimization_barrier((value, *others))[0]


def per_device(hamiltonian, subspace, block_cols, far_list):
    block_rows, entries = block_cols.shape
    size = hamiltonian.shape[1] // entries
    device_count = lax.axis_size("rows")
    first_row = lax.axis_index("rows") * block_rows
    block_total = block_rows * device_count
    swap_level = (device_count // 8).bit_length() - 1
    plan = Plan(size, block_rows * size, subspace.shape[1], far_list.shape[1])

    side = (lax.axis_index("rows") % 2).astype(jnp.int32).reshape(1)

    def exchange(listed, sends):
        to_away, to_near = sends
        far = partner(listed, "rows", swap_level)
        return swap_chips(to_away, "rows"), far, partner(to_near, "rows", 0)

    start, block_cols, *sends = pack(plan, subspace, block_cols)
    asked = partner(after(far_list, start), "rows", swap_level)
    listed = gather_far(plan, asked, start)
    away, far, near = exchange(listed, (sends[0], after(sends[1], listed)))

    block_cols = after(block_cols, listed)
    edge, far_slots = 2 * plan.near, 2 * plan.far
    shift = block_cols - first_row + edge
    shift = jnp.where(shift < 0, shift + block_total, shift)
    shift = jnp.where(shift >= block_total, shift - block_total, shift)
    last = block_rows + 2 * edge - 2
    shift = shift + side[0] * (last - 4 * (shift >> 1))
    places = jnp.where(
        block_cols >= block_total,
        edge + block_cols - block_total,
        jnp.where(
            shift < edge,
            shift,
            jnp.where(
                shift < edge + block_rows,
                shift - edge + 2 * plan.outer,
                shift - block_rows + far_slots,
            ),
        ),
    )
    every = jnp.arange(plan.places, dtype=jnp.int32)[None, None, :]
    entry = jnp.arange(entries, dtype=jnp.int32)[None, :, None]
    hit = places[:, :, None] == every
    inverse = entries + jnp.sum(jnp.where(hit, entry - entries, 0), axis=1)

    band, inner = make_band(plan, inverse, hamiltonian.T, start)

    inner = run_middle(plan, away, near, band, inner)
    value, listed, *sends = run_first(plan, asked, far, band, inner, start)
    away, far, near = exchange(listed, sends)
    inner = run_inner(plan, value, near, band)
    far = split_far(plan, after(far, inner))
    return run_second(plan, away, far, band, inner, value, start)


def solution(mesh):
    placed = (P("rows", None), P("rows", None), P("rows", None), P("rows", None))
    return jax.shard_map(
        per_device, mesh=mesh, in_specs=placed, out_specs=P("rows", None), check_vma=False
    )
```

```python
import functools

import jax
import jax.numpy as jnp
from jax import lax
from jax.experimental import pallas as pl
from jax.experimental.pallas import tpu as pltpu
from jax.sharding import PartitionSpec as P

CENTER = 0.25
HALF_WIDTH = 1.5
REACH = 13
F32 = jnp.float32
VMEM = pl.BlockSpec(memory_space=pltpu.VMEM)
HBM = pl.BlockSpec(memory_space=pltpu.HBM)
SMEM = pl.BlockSpec(memory_space=pltpu.SMEM)


def partner(value, axis, bit):
    mask = 2**bit
    pairs = [(source, source ^ mask) for source in range(lax.axis_size(axis))]
    return lax.ppermute(value, axis, pairs)


def swap_chips(value, axis):
    devices = lax.axis_size(axis)
    pairs = [(i, (i + (1 if i % 2 else -1)) % devices) for i in range(devices)]
    return lax.ppermute(value, axis, pairs)


def split(value):
    high = value.astype(jnp.bfloat16)
    return high, (value - high.astype(F32)).astype(jnp.bfloat16)


def fold(sums):
    width, tile = sums.shape[0] // 2, sums.shape[1] // 2
    small = sums[width:, tile:] + sums[width:, :tile] + sums[:width, tile:]
    return small + sums[:width, :tile]


def params(limit):
    return pltpu.CompilerParams(vmem_limit_bytes=limit * 2**20)


def cost(flops, moved):
    return pl.CostEstimate(flops=flops, bytes_accessed=moved, transcendentals=0)


class Plan:
    def __init__(self, size, rows, width, slots):
        self.size, self.rows, self.width = size, rows, width
        self.tile = 2 * size
        self.pairs = rows // self.tile
        self.near = (REACH + 1) // 2
        self.far = slots * size // self.tile
        self.edge = self.near * self.tile
        self.half = width // 2
        self.whole = self.edge - self.tile
        self.outer = 2 * self.near + self.far
        self.places = 2 * (self.outer + self.pairs)
        self.depth = max(sum(run[2] for run in self.runs(p)) for p in range(self.pairs))

    def outer_range(self, p):
        extra = p + self.near - self.pairs + 1
        return min(p, self.near), self.near + self.far + max(0, extra)

    def spans(self, p):
        begin, end = self.outer_range(p)
        row = self.near - begin
        return {
            "away": (begin, self.near, 0),
            "far": (0, self.far, row),
            "near": (0, end - self.near - self.far, row + self.far),
        }

    def own_range(self, p):
        return max(0, p - self.near), min(self.pairs, p + self.near + 1)

    def runs(self, p):
        begin, end = self.outer_range(p)
        rows = (end - begin) * self.tile
        outer = (2 * begin, 0, rows)
        begin, end = self.own_range(p)
        return outer, (2 * (self.outer + begin), rows, (end - begin) * self.tile)

    def mirrored(self, t, side):
        return t + side[0] * (self.pairs - 1 - 2 * t)


def write_far(plan, side, asked, source, write):
    tile, size = plan.tile, plan.size
    lane = lax.broadcasted_iota(jnp.int32, (source.shape[0], tile), 1)

    def block(slot, want):
        index = lax.rem(asked[0, slot] + 2 * plan.pairs, 2 * plan.pairs)
        at = plan.mirrored(lax.div(index, 2), side) * tile
        value = source[:, pl.ds(pl.multiple_of(at, tile), tile)]
        return jnp.where(lax.rem(index, 2) == want, value, pltpu.roll(value, size, 1))

    for t in range(plan.far):
        value = jnp.where(lane < size, block(2 * t, 0), block(2 * t + 1, 1))
        write(t * tile, value)


def write_sends(plan, side, at, value, to_away, to_near):
    tile, half, skip = plan.tile, plan.half, plan.rows - plan.edge
    if at < plan.whole:
        to_away[:, at : at + tile] = value[:half]
        to_away[:, plan.edge + at : plan.edge + at + tile] = value[half:]
    elif at == plan.whole:
        lane = lax.broadcasted_iota(jnp.int32, (half, tile), 1)
        turned = pltpu.roll(value, plan.size, 1)
        even = jnp.where(lane < plan.size, value[:half], turned[half:])
        odd = jnp.where(lane < plan.size, turned[:half], value[half:])
        to_away[:, at : at + tile] = jnp.where(side[0] == 0, even, odd)
    if at >= skip:
        to_near[:, at - skip : at - skip + tile] = value


def away_tile(plan, side, away, t):
    at, tile = t * plan.tile, plan.tile
    packed = away[:, at : at + tile]
    if at < plan.whole:
        rest = away[:, plan.edge + at : plan.edge + at + tile]
        return jnp.concatenate([packed, rest], axis=0)
    turned = pltpu.roll(packed, plan.size, 1)
    even = jnp.concatenate([turned, packed], axis=0)
    odd = jnp.concatenate([packed, turned], axis=0)
    return jnp.where(side[0] == 0, even, odd)


def send_shapes(plan):
    shapes = ((plan.half, plan.edge + plan.whole), (plan.width, plan.edge))
    return [jax.ShapeDtypeStruct(shape, F32) for shape in shapes]


def pack_kernel(plan, chunks, natural, codes, turned, held, *rest):
    sends, staged, sems = rest[:-2], *rest[-2:]
    side = parity()
    tile, count = plan.tile, plan.pairs // chunks
    step = count * tile

    def fetch(c):
        at = pl.multiple_of((c + side[0] * (chunks - 1 - 2 * c)) * step, step)
        return pltpu.make_async_copy(
            natural.at[pl.ds(at, step), :], staged.at[pl.ds(c * step, step), :], sems.at[c]
        )

    for c in range(chunks):
        fetch(c).start()
    copy = pltpu.make_async_copy(codes, held, sems.at[chunks])
    copy.start()
    for t in range(plan.pairs):
        c, u = t // count, t % count
        if u == 0:
            fetch(c).wait()
        at = c * step + (u + side[0] * (count - 1 - 2 * u)) * tile
        at = pl.multiple_of(at, tile)
        value = staged[pl.ds(at, tile), :].T
        turned[:, t * tile : (t + 1) * tile] = value
        write_sends(plan, side, t * tile, value, *sends)
    copy.wait()


def pack(plan, natural, codes):
    chunks = 4 if plan.pairs % 4 == 0 else 1
    return pl.pallas_call(
        functools.partial(pack_kernel, plan, chunks),
        out_shape=[
            pltpu.VMEM((plan.width, plan.rows), F32),
            pltpu.VMEM(codes.shape, codes.dtype),
        ]
        + send_shapes(plan),
        in_specs=[HBM, HBM],
        out_specs=[VMEM] * 4,
        scratch_shapes=[
            pltpu.VMEM((plan.rows, plan.width), F32),
            pltpu.SemaphoreType.DMA((chunks + 1,)),
        ],
        compiler_params=params(8),
        name="pack",
    )(*(pltpu.with_memory_space_constraint(x, pltpu.HBM) for x in (natural, codes)))


def far_kernel(plan, asked, turned, out):
    def write(at, value):
        out[:, at : at + plan.tile] = value

    write_far(plan, parity(), asked, turned, write)


def gather_far(plan, asked, turned):
    return pl.pallas_call(
        functools.partial(far_kernel, plan),
        out_shape=jax.ShapeDtypeStruct((plan.width, plan.far * plan.tile), F32),
        in_specs=[SMEM, VMEM],
        out_specs=VMEM,
        compiler_params=params(8),
        name="far",
    )(asked, turned)


def own_halves(plan, vectors, halves):
    for at in range(0, plan.rows, plan.tile):
        high, low = split(vectors[:, at : at + plan.tile])
        halves[: plan.width, at : at + plan.tile] = high
        halves[plan.width :, at : at + plan.tile] = low


def own_product(plan, p, halves, band):
    begin, end = (plan.tile * bound for bound in plan.own_range(p))
    _, (_, row, rows) = plan.runs(p)
    vectors = halves[:, begin:end]
    return fold(jnp.dot(vectors, band[p, row : row + rows, :], preferred_element_type=F32))


def band_kernel(
    plan, depth, table, ham_t, vectors, band, inner, staged, halves, inverse, sems
):
    size, tile = plan.size, plan.tile
    side = parity()
    group = staged.shape[2] // tile
    units = plan.pairs // group
    lane = lax.broadcasted_iota(jnp.int32, (size, tile), 1)

    def fetch(u):
        natural = u + side[0] * (units - 1 - 2 * u)
        at = pl.multiple_of(natural * group * tile, group * tile)
        held = staged.at[u, pl.ds(0, depth), :]
        return pltpu.make_async_copy(ham_t.at[:, pl.ds(at, group * tile)], held, sems.at[u])

    def store(p, at, high, low):
        band[p, at : at + size, :tile] = high
        band[p, at : at + size, tile:] = low

    copy = pltpu.make_async_copy(table, inverse, sems.at[units])
    copy.start()
    for u in range(units):
        fetch(u).start()
    for u in range(units):
        staged[u, depth:, :] = jnp.zeros((size, group * tile), F32)
    own_halves(plan, vectors, halves)
    copy.wait()

    for p in range(plan.pairs):
        u, t = p // group, p % group
        if t == 0:
            fetch(u).wait()
        lanes = pl.multiple_of((t + side[0] * (group - 1 - 2 * t)) * tile, tile)
        row = 2 * plan.mirrored(p, side)

        def block(q):
            even = pl.multiple_of(inverse[row, q] * size, size)
            odd = pl.multiple_of(inverse[row + 1, q] * size, size)
            first = staged[u, pl.ds(even, size), pl.ds(lanes, tile)]
            second = staged[u, pl.ds(odd, size), pl.ds(lanes, tile)]
            return jnp.where(lane < size, first, second)

        ready = None if p == 0 else own_product(plan, p - 1, halves, band)
        places = [(place + q, at + q * size) for place, at, rows in plan.runs(p) for q in range(rows // size)]
        waiting = []
        for begin in range(0, len(places), 2):
            batch = [(at, *split(block(q))) for q, at in places[begin : begin + 2]]
            for entry in waiting:
                store(p, *entry)
            waiting = batch
        for entry in waiting:
            store(p, *entry)
        if p > 0:
            inner[:, (p - 1) * tile : p * tile] = ready
    p = plan.pairs - 1
    inner[:, p * tile : (p + 1) * tile] = own_product(plan, p, halves, band)


def make_band(plan, inverse, ham_t, vectors):
    depth, rows = ham_t.shape
    size, tile = plan.size, plan.tile
    group = 2 if plan.pairs % 2 == 0 else 1
    return pl.pallas_call(
        functools.partial(band_kernel, plan, depth),
        out_shape=[
            pltpu.VMEM((plan.pairs, plan.depth, 2 * tile), jnp.bfloat16),
            pltpu.VMEM((plan.width, rows), F32),
        ],
        in_specs=[VMEM, HBM, VMEM],
        out_specs=[VMEM, VMEM],
        scratch_shapes=[
            pltpu.VMEM((plan.pairs // group, depth + size, group * tile), F32),
            pltpu.VMEM((2 * plan.width, rows), jnp.bfloat16),
            pltpu.SMEM(inverse.shape, inverse.dtype),
            pltpu.SemaphoreType.DMA((plan.pairs // group + 1,)),
        ],
        compiler_params=params(14),
        cost_estimate=cost(0, 2 * 4 * depth * rows),
        name="band",
    )(inverse, pltpu.with_memory_space_constraint(ham_t, pltpu.HBM), vectors)


def put_halves(plan, halves, tiles):
    for t, value in enumerate(tiles):
        high, low = split(value)
        halves[: plan.width, t * plan.tile : (t + 1) * plan.tile] = high
        halves[plan.width :, t * plan.tile : (t + 1) * plan.tile] = low


def message_product(plan, name, p, halves, band):
    first, last, row = plan.spans(p)[name]
    if first == last:
        return 0.0
    rows = slice(row * plan.tile, (row + last - first) * plan.tile)
    vectors = halves[:, first * plan.tile : last * plan.tile]
    return fold(jnp.dot(vectors, band[p, rows, :], preferred_element_type=F32))


def halves_scratch(plan, tiles):
    return pltpu.VMEM((2 * plan.width, tiles * plan.tile), jnp.bfloat16)


def near_tiles(plan, near):
    tile = plan.tile
    return [near[:, t * tile : (t + 1) * tile] for t in reversed(range(plan.near))]


def away_tiles(plan, side, away):
    return [away_tile(plan, side, away, t) for t in reversed(range(plan.near))]


def middle_kernel(plan, away, near, band, inner, out, away_halves, near_halves):
    put_halves(plan, away_halves, away_tiles(plan, parity(), away))
    put_halves(plan, near_halves, near_tiles(plan, near))
    for p in range(plan.pairs):
        lanes = slice(p * plan.tile, (p + 1) * plan.tile)
        total = inner[:, lanes] + message_product(plan, "away", p, away_halves, band)
        out[:, lanes] = total + message_product(plan, "near", p, near_halves, band)


def run_middle(plan, away, near, band, inner):
    return pl.pallas_call(
        functools.partial(middle_kernel, plan),
        out_shape=pltpu.VMEM((plan.width, plan.rows), F32),
        in_specs=[VMEM] * 4,
        out_specs=VMEM,
        scratch_shapes=[halves_scratch(plan, plan.near)] * 2,
        compiler_params=params(8),
        cost_estimate=cost(8 * plan.width * plan.rows**2, 0),
        name="middle",
    )(away, near, band, inner)


def inner_kernel(plan, vectors, band, out, halves):
    own_halves(plan, vectors, halves)
    for p in range(plan.pairs):
        out[:, p * plan.tile : (p + 1) * plan.tile] = own_product(plan, p, halves, band)


def run_inner(plan, vectors, band):
    return pl.pallas_call(
        functools.partial(inner_kernel, plan),
        out_shape=pltpu.VMEM((plan.width, plan.rows), F32),
        in_specs=[VMEM] * 2,
        out_specs=VMEM,
        scratch_shapes=[halves_scratch(plan, plan.pairs)],
        compiler_params=params(8),
        cost_estimate=cost(8 * plan.width * plan.rows**2, 0),
        name="inner",
    )(vectors, band)


def near_kernel(plan, near, band, inner, out, halves):
    put_halves(plan, halves, near_tiles(plan, near))
    for p in range(plan.pairs):
        lanes = slice(p * plan.tile, (p + 1) * plan.tile)
        out[:, lanes] = inner[:, lanes] + message_product(plan, "near", p, halves, band)


def add_near(plan, near, band, inner):
    return pl.pallas_call(
        functools.partial(near_kernel, plan),
        out_shape=pltpu.VMEM((plan.width, plan.rows), F32),
        in_specs=[VMEM] * 3,
        out_specs=VMEM,
        scratch_shapes=[halves_scratch(plan, plan.near)],
        compiler_params=params(8),
        cost_estimate=cost(2 * plan.width * plan.rows**2, 0),
        name="near",
    )(near, band, inner)


def far_tiles(plan, far):
    return [far[:, t * plan.tile : (t + 1) * plan.tile] for t in range(plan.far)]


def far_split_kernel(plan, far, halves):
    put_halves(plan, halves, far_tiles(plan, far))


def split_far(plan, far):
    return pl.pallas_call(
        functools.partial(far_split_kernel, plan),
        out_shape=halves_scratch(plan, plan.far),
        in_specs=[VMEM],
        out_specs=VMEM,
        compiler_params=params(8),
        cost_estimate=cost(16 * plan.width * plan.rows**2, 0),
        name="split",
    )(far)


def first_kernel(
    plan, listed, far, band, inner, own, value, to_far, to_away, to_near, halves, asked, sem
):
    copy = pltpu.make_async_copy(listed, asked, sem)
    copy.start()
    side = parity()
    put_halves(plan, halves, far_tiles(plan, far))
    for p in range(plan.pairs):
        lanes = slice(p * plan.tile, (p + 1) * plan.tile)
        product = inner[:, lanes] - CENTER * own[:, lanes]
        product += message_product(plan, "far", p, halves, band)
        term = product * (1.0 / HALF_WIDTH)
        value[:, lanes] = term
        write_sends(plan, side, lanes.start, term, to_away, to_near)

    def write(at, term):
        to_far[:, at : at + plan.tile] = term

    copy.wait()
    write_far(plan, side, asked, value, write)


def run_first(plan, asked, far, band, inner, own):
    shapes = [jax.ShapeDtypeStruct(far.shape, F32)] + send_shapes(plan)
    return pl.pallas_call(
        functools.partial(first_kernel, plan),
        out_shape=[pltpu.VMEM((plan.width, plan.rows), F32)] + shapes,
        in_specs=[VMEM] * 5,
        out_specs=[VMEM] * (1 + len(shapes)),
        scratch_shapes=[
            halves_scratch(plan, plan.far),
            pltpu.SMEM(asked.shape, asked.dtype),
            pltpu.SemaphoreType.DMA,
        ],
        compiler_params=params(8),
        cost_estimate=cost(2 * plan.width * plan.rows**2, 0),
        name="first",
    )(asked, far, band, inner, own)


def second_kernel(plan, away, far, band, inner, own, start, out, halves, held, sems):
    side = parity()
    put_halves(plan, halves, away_tiles(plan, side, away))
    halves[:, plan.edge :] = far[...]
    copies = []
    for p in reversed(range(plan.pairs)):
        lanes = slice(p * plan.tile, (p + 1) * plan.tile)
        product = inner[:, lanes] - CENTER * own[:, lanes]
        begin = plan.outer_range(p)[0] * plan.tile
        vectors = far[...] if begin == plan.edge else halves[:, begin:]
        rows = band[p, : vectors.shape[1], :]
        product += fold(jnp.dot(vectors, rows, preferred_element_type=F32))
        term = 2.0 / HALF_WIDTH * product - start[:, lanes]
        place = pl.multiple_of(plan.mirrored(p, side) * plan.tile, plan.tile)
        held[p] = term.T
        copies.append(
            pltpu.make_async_copy(held.at[p], out.at[pl.ds(place, plan.tile), :], sems.at[p])
        )
        copies[-1].start()
    for copy in copies:
        copy.wait()


def run_second(plan, away, far, band, inner, own, start):
    return pl.pallas_call(
        functools.partial(second_kernel, plan),
        out_shape=jax.ShapeDtypeStruct((plan.rows, plan.width), F32),
        in_specs=[VMEM] * 6,
        out_specs=HBM,
        scratch_shapes=[
            halves_scratch(plan, plan.near + plan.far),
            pltpu.VMEM((plan.pairs, plan.tile, plan.width), F32),
            pltpu.SemaphoreType.DMA((plan.pairs,)),
        ],
        compiler_params=params(8),
        cost_estimate=cost(2 * plan.width * plan.rows**2, 0),
        name="second",
    )(away, far, band, inner, own, start)


def parity():
    return (lax.rem(lax.axis_index("rows"), 2),)


def after(value, *others):
    return lax.optimization_barrier((value, *others))[0]


def per_device(hamiltonian, subspace, block_cols, far_list):
    block_rows, entries = block_cols.shape
    size = hamiltonian.shape[1] // entries
    device_count = lax.axis_size("rows")
    first_row = lax.axis_index("rows") * block_rows
    block_total = block_rows * device_count
    swap_level = (device_count // 8).bit_length() - 1
    plan = Plan(size, block_rows * size, subspace.shape[1], far_list.shape[1])

    side = (lax.axis_index("rows") % 2).astype(jnp.int32).reshape(1)

    def exchange(listed, sends):
        to_away, to_near = sends
        far = partner(listed, "rows", swap_level)
        return swap_chips(to_away, "rows"), far, partner(to_near, "rows", 0)

    start, block_cols, *sends = pack(plan, subspace, block_cols)
    asked = partner(after(far_list, start), "rows", swap_level)
    listed = gather_far(plan, asked, start)
    away, far, near = exchange(listed, (sends[0], after(sends[1], listed)))

    block_cols = after(block_cols, listed)
    edge, far_slots = 2 * plan.near, 2 * plan.far
    shift = block_cols - first_row + edge
    shift = jnp.where(shift < 0, shift + block_total, shift)
    shift = jnp.where(shift >= block_total, shift - block_total, shift)
    last = block_rows + 2 * edge - 2
    shift = shift + side[0] * (last - 4 * (shift >> 1))
    places = jnp.where(
        block_cols >= block_total,
        edge + block_cols - block_total,
        jnp.where(
            shift < edge,
            shift,
            jnp.where(
                shift < edge + block_rows,
                shift - edge + 2 * plan.outer,
                shift - block_rows + far_slots,
            ),
        ),
    )
    every = jnp.arange(plan.places, dtype=jnp.int32)[None, None, :]
    entry = jnp.arange(entries, dtype=jnp.int32)[None, :, None]
    hit = places[:, :, None] == every
    inverse = entries + jnp.sum(jnp.where(hit, entry - entries, 0), axis=1)

    band, inner = make_band(plan, inverse, hamiltonian.T, start)

    inner = run_middle(plan, away, near, band, inner)
    value, listed, to_away, to_near = run_first(plan, asked, far, band, inner, start)
    far, away = partner(listed, "rows", swap_level), swap_chips(to_away, "rows")
    inner = run_inner(plan, value, band)
    cores = [[i, i + 1] for i in range(0, device_count, 2)]
    both = lax.all_gather(to_near, "rows", axis_index_groups=cores)
    near = lax.dynamic_index_in_dim(both, 1 - side[0], keepdims=False)
    inner = add_near(plan, near, band, inner)
    far = split_far(plan, after(far, inner))
    return run_second(plan, away, far, band, inner, value, start)


def solution(mesh):
    placed = (P("rows", None), P("rows", None), P("rows", None), P("rows", None))
    return jax.shard_map(
        per_device, mesh=mesh, in_specs=placed, out_specs=P("rows", None), check_vma=False
    )
```

```python
import functools

import jax
import jax.numpy as jnp
from jax import lax
from jax.experimental import pallas as pl
from jax.experimental.pallas import tpu as pltpu
from jax.sharding import PartitionSpec as P

CENTER = 0.25
HALF_WIDTH = 1.5
REACH = 13
F32 = jnp.float32
VMEM = pl.BlockSpec(memory_space=pltpu.VMEM)
HBM = pl.BlockSpec(memory_space=pltpu.HBM)
SMEM = pl.BlockSpec(memory_space=pltpu.SMEM)


def partner(value, axis, bit):
    mask = 2**bit
    pairs = [(source, source ^ mask) for source in range(lax.axis_size(axis))]
    return lax.ppermute(value, axis, pairs)


def swap_chips(value, axis):
    devices = lax.axis_size(axis)
    pairs = [(i, (i + (1 if i % 2 else -1)) % devices) for i in range(devices)]
    return lax.ppermute(value, axis, pairs)


def split(value):
    high = value.astype(jnp.bfloat16)
    return high, (value - high.astype(F32)).astype(jnp.bfloat16)


def fold(sums):
    width, tile = sums.shape[0] // 2, sums.shape[1] // 2
    small = sums[width:, tile:] + sums[width:, :tile] + sums[:width, tile:]
    return small + sums[:width, :tile]


def params(limit):
    return pltpu.CompilerParams(vmem_limit_bytes=limit * 2**20)


def cost(flops, moved):
    return pl.CostEstimate(flops=flops, bytes_accessed=moved, transcendentals=0)


class Plan:
    def __init__(self, size, rows, width, slots):
        self.size, self.rows, self.width = size, rows, width
        self.tile = 2 * size
        self.pairs = rows // self.tile
        self.near = (REACH + 1) // 2
        self.far = slots * size // self.tile
        self.edge = self.near * self.tile
        self.half = width // 2
        self.whole = self.edge - self.tile
        self.outer = 2 * self.near + self.far
        self.places = 2 * (self.outer + self.pairs)
        self.depth = max(sum(run[2] for run in self.runs(p)) for p in range(self.pairs))

    def outer_range(self, p):
        extra = p + self.near - self.pairs + 1
        return min(p, self.near), self.near + self.far + max(0, extra)

    def spans(self, p):
        begin, end = self.outer_range(p)
        row = self.near - begin
        return {
            "away": (begin, self.near, 0),
            "far": (0, self.far, row),
            "near": (0, end - self.near - self.far, row + self.far),
        }

    def own_range(self, p):
        return max(0, p - self.near), min(self.pairs, p + self.near + 1)

    def runs(self, p):
        begin, end = self.outer_range(p)
        rows = (end - begin) * self.tile
        outer = (2 * begin, 0, rows)
        begin, end = self.own_range(p)
        return outer, (2 * (self.outer + begin), rows, (end - begin) * self.tile)

    def mirrored(self, t, side):
        return t + side[0] * (self.pairs - 1 - 2 * t)


def write_far(plan, side, asked, source, write):
    tile, size = plan.tile, plan.size
    lane = lax.broadcasted_iota(jnp.int32, (source.shape[0], tile), 1)

    def block(slot, want):
        index = lax.rem(asked[0, slot] + 2 * plan.pairs, 2 * plan.pairs)
        at = plan.mirrored(lax.div(index, 2), side) * tile
        value = source[:, pl.ds(pl.multiple_of(at, tile), tile)]
        return jnp.where(lax.rem(index, 2) == want, value, pltpu.roll(value, size, 1))

    for t in range(plan.far):
        value = jnp.where(lane < size, block(2 * t, 0), block(2 * t + 1, 1))
        write(t * tile, value)


def write_sends(plan, side, at, value, to_away, to_near):
    tile, half, skip = plan.tile, plan.half, plan.rows - plan.edge
    if at < plan.whole:
        to_away[:, at : at + tile] = value[:half]
        to_away[:, plan.edge + at : plan.edge + at + tile] = value[half:]
    elif at == plan.whole:
        lane = lax.broadcasted_iota(jnp.int32, (half, tile), 1)
        turned = pltpu.roll(value, plan.size, 1)
        even = jnp.where(lane < plan.size, value[:half], turned[half:])
        odd = jnp.where(lane < plan.size, turned[:half], value[half:])
        to_away[:, at : at + tile] = jnp.where(side[0] == 0, even, odd)
    if at >= skip and to_near is not None:
        to_near[:, at - skip : at - skip + tile] = value


def away_tile(plan, side, away, t):
    at, tile = t * plan.tile, plan.tile
    packed = away[:, at : at + tile]
    if at < plan.whole:
        rest = away[:, plan.edge + at : plan.edge + at + tile]
        return jnp.concatenate([packed, rest], axis=0)
    turned = pltpu.roll(packed, plan.size, 1)
    even = jnp.concatenate([turned, packed], axis=0)
    odd = jnp.concatenate([packed, turned], axis=0)
    return jnp.where(side[0] == 0, even, odd)


def send_shapes(plan):
    shapes = ((plan.half, plan.edge + plan.whole), (plan.width, plan.edge))
    return [jax.ShapeDtypeStruct(shape, F32) for shape in shapes]


def pack_kernel(plan, chunks, natural, codes, turned, held, *rest):
    sends, staged, sems = rest[:-2], *rest[-2:]
    side = parity()
    tile, count = plan.tile, plan.pairs // chunks
    step = count * tile

    def fetch(c):
        at = pl.multiple_of((c + side[0] * (chunks - 1 - 2 * c)) * step, step)
        return pltpu.make_async_copy(
            natural.at[pl.ds(at, step), :], staged.at[pl.ds(c * step, step), :], sems.at[c]
        )

    for c in range(chunks):
        fetch(c).start()
    copy = pltpu.make_async_copy(codes, held, sems.at[chunks])
    copy.start()
    for t in range(plan.pairs):
        c, u = t // count, t % count
        if u == 0:
            fetch(c).wait()
        at = c * step + (u + side[0] * (count - 1 - 2 * u)) * tile
        at = pl.multiple_of(at, tile)
        value = staged[pl.ds(at, tile), :].T
        turned[:, t * tile : (t + 1) * tile] = value
        write_sends(plan, side, t * tile, value, *sends)
    copy.wait()


def pack(plan, natural, codes):
    chunks = 4 if plan.pairs % 4 == 0 else 1
    return pl.pallas_call(
        functools.partial(pack_kernel, plan, chunks),
        out_shape=[
            pltpu.VMEM((plan.width, plan.rows), F32),
            pltpu.VMEM(codes.shape, codes.dtype),
        ]
        + send_shapes(plan),
        in_specs=[HBM, HBM],
        out_specs=[VMEM] * 4,
        scratch_shapes=[
            pltpu.VMEM((plan.rows, plan.width), F32),
            pltpu.SemaphoreType.DMA((chunks + 1,)),
        ],
        compiler_params=params(8),
        name="pack",
    )(*(pltpu.with_memory_space_constraint(x, pltpu.HBM) for x in (natural, codes)))


def far_kernel(plan, asked, turned, out):
    def write(at, value):
        out[:, at : at + plan.tile] = value

    write_far(plan, parity(), asked, turned, write)


def gather_far(plan, asked, turned):
    return pl.pallas_call(
        functools.partial(far_kernel, plan),
        out_shape=jax.ShapeDtypeStruct((plan.width, plan.far * plan.tile), F32),
        in_specs=[SMEM, VMEM],
        out_specs=VMEM,
        compiler_params=params(8),
        name="far",
    )(asked, turned)


def own_halves(plan, vectors, halves):
    for at in range(0, plan.rows, plan.tile):
        high, low = split(vectors[:, at : at + plan.tile])
        halves[: plan.width, at : at + plan.tile] = high
        halves[plan.width :, at : at + plan.tile] = low


def own_product(plan, p, halves, band):
    begin, end = (plan.tile * bound for bound in plan.own_range(p))
    _, (_, row, rows) = plan.runs(p)
    vectors = halves[:, begin:end]
    return fold(jnp.dot(vectors, band[p, row : row + rows, :], preferred_element_type=F32))


def band_kernel(
    plan, depth, table, ham_t, vectors, band, inner, staged, halves, inverse, sems
):
    size, tile = plan.size, plan.tile
    side = parity()
    group = staged.shape[2] // tile
    units = plan.pairs // group
    lane = lax.broadcasted_iota(jnp.int32, (size, tile), 1)

    def fetch(u):
        natural = u + side[0] * (units - 1 - 2 * u)
        at = pl.multiple_of(natural * group * tile, group * tile)
        held = staged.at[u, pl.ds(0, depth), :]
        return pltpu.make_async_copy(ham_t.at[:, pl.ds(at, group * tile)], held, sems.at[u])

    def store(p, at, high, low):
        band[p, at : at + size, :tile] = high
        band[p, at : at + size, tile:] = low

    copy = pltpu.make_async_copy(table, inverse, sems.at[units])
    copy.start()
    for u in range(units):
        fetch(u).start()
    for u in range(units):
        staged[u, depth:, :] = jnp.zeros((size, group * tile), F32)
    own_halves(plan, vectors, halves)
    copy.wait()

    for p in range(plan.pairs):
        u, t = p // group, p % group
        if t == 0:
            fetch(u).wait()
        lanes = pl.multiple_of((t + side[0] * (group - 1 - 2 * t)) * tile, tile)
        row = 2 * plan.mirrored(p, side)

        def block(q):
            even = pl.multiple_of(inverse[row, q] * size, size)
            odd = pl.multiple_of(inverse[row + 1, q] * size, size)
            first = staged[u, pl.ds(even, size), pl.ds(lanes, tile)]
            second = staged[u, pl.ds(odd, size), pl.ds(lanes, tile)]
            return jnp.where(lane < size, first, second)

        ready = None if p == 0 else own_product(plan, p - 1, halves, band)
        places = [(place + q, at + q * size) for place, at, rows in plan.runs(p) for q in range(rows // size)]
        waiting = []
        for begin in range(0, len(places), 2):
            batch = [(at, *split(block(q))) for q, at in places[begin : begin + 2]]
            for entry in waiting:
                store(p, *entry)
            waiting = batch
        for entry in waiting:
            store(p, *entry)
        if p > 0:
            inner[:, (p - 1) * tile : p * tile] = ready
    p = plan.pairs - 1
    inner[:, p * tile : (p + 1) * tile] = own_product(plan, p, halves, band)


def make_band(plan, inverse, ham_t, vectors):
    depth, rows = ham_t.shape
    size, tile = plan.size, plan.tile
    group = 2 if plan.pairs % 2 == 0 else 1
    return pl.pallas_call(
        functools.partial(band_kernel, plan, depth),
        out_shape=[
            pltpu.VMEM((plan.pairs, plan.depth, 2 * tile), jnp.bfloat16),
            pltpu.VMEM((plan.width, rows), F32),
        ],
        in_specs=[VMEM, HBM, VMEM],
        out_specs=[VMEM, VMEM],
        scratch_shapes=[
            pltpu.VMEM((plan.pairs // group, depth + size, group * tile), F32),
            pltpu.VMEM((2 * plan.width, rows), jnp.bfloat16),
            pltpu.SMEM(inverse.shape, inverse.dtype),
            pltpu.SemaphoreType.DMA((plan.pairs // group + 1,)),
        ],
        compiler_params=params(14),
        cost_estimate=cost(0, 2 * 4 * depth * rows),
        name="band",
    )(inverse, pltpu.with_memory_space_constraint(ham_t, pltpu.HBM), vectors)


def put_halves(plan, halves, tiles):
    for t, value in enumerate(tiles):
        high, low = split(value)
        halves[: plan.width, t * plan.tile : (t + 1) * plan.tile] = high
        halves[plan.width :, t * plan.tile : (t + 1) * plan.tile] = low


def message_product(plan, name, p, halves, band):
    first, last, row = plan.spans(p)[name]
    if first == last:
        return 0.0
    rows = slice(row * plan.tile, (row + last - first) * plan.tile)
    vectors = halves[:, first * plan.tile : last * plan.tile]
    return fold(jnp.dot(vectors, band[p, rows, :], preferred_element_type=F32))


def halves_scratch(plan, tiles):
    return pltpu.VMEM((2 * plan.width, tiles * plan.tile), jnp.bfloat16)


def near_tiles(plan, near):
    tile = plan.tile
    return [near[:, t * tile : (t + 1) * tile] for t in reversed(range(plan.near))]


def away_tiles(plan, side, away):
    return [away_tile(plan, side, away, t) for t in reversed(range(plan.near))]


def middle_kernel(plan, away, near, band, inner, out, away_halves, near_halves):
    put_halves(plan, away_halves, away_tiles(plan, parity(), away))
    put_halves(plan, near_halves, near_tiles(plan, near))
    for p in range(plan.pairs):
        lanes = slice(p * plan.tile, (p + 1) * plan.tile)
        total = inner[:, lanes] + message_product(plan, "away", p, away_halves, band)
        out[:, lanes] = total + message_product(plan, "near", p, near_halves, band)


def run_middle(plan, away, near, band, inner):
    return pl.pallas_call(
        functools.partial(middle_kernel, plan),
        out_shape=pltpu.VMEM((plan.width, plan.rows), F32),
        in_specs=[VMEM] * 4,
        out_specs=VMEM,
        scratch_shapes=[halves_scratch(plan, plan.near)] * 2,
        compiler_params=params(8),
        cost_estimate=cost(8 * plan.width * plan.rows**2, 0),
        name="middle",
    )(away, near, band, inner)


def inner_kernel(plan, vectors, low, high, band, out, halves, near_halves):
    own_halves(plan, vectors, halves)
    tiles = zip(near_tiles(plan, low), near_tiles(plan, high))
    put_halves(plan, near_halves, [jnp.concatenate(pair, axis=0) for pair in tiles])
    for p in range(plan.pairs):
        total = own_product(plan, p, halves, band)
        total += message_product(plan, "near", p, near_halves, band)
        out[:, p * plan.tile : (p + 1) * plan.tile] = total


def run_inner(plan, vectors, low, high, band):
    return pl.pallas_call(
        functools.partial(inner_kernel, plan),
        out_shape=pltpu.VMEM((plan.width, plan.rows), F32),
        in_specs=[VMEM] * 4,
        out_specs=VMEM,
        scratch_shapes=[halves_scratch(plan, plan.pairs), halves_scratch(plan, plan.near)],
        compiler_params=params(8),
        cost_estimate=cost(1, 1),
        name="inner",
    )(vectors, low, high, band)


def far_tiles(plan, far):
    return [far[:, t * plan.tile : (t + 1) * plan.tile] for t in range(plan.far)]


def far_split_kernel(plan, far, halves):
    put_halves(plan, halves, far_tiles(plan, far))


def split_far(plan, far):
    return pl.pallas_call(
        functools.partial(far_split_kernel, plan),
        out_shape=halves_scratch(plan, plan.far),
        in_specs=[VMEM],
        out_specs=VMEM,
        compiler_params=params(8),
        cost_estimate=cost(16 * plan.width * plan.rows**2, 0),
        name="split",
    )(far)


def first_kernel(
    plan, listed, far, band, inner, own, value, to_far, to_away, low, high, halves, asked, sem
):
    copy = pltpu.make_async_copy(listed, asked, sem)
    copy.start()
    side = parity()
    put_halves(plan, halves, far_tiles(plan, far))
    for p in range(plan.pairs):
        lanes = slice(p * plan.tile, (p + 1) * plan.tile)
        product = inner[:, lanes] - CENTER * own[:, lanes]
        product += message_product(plan, "far", p, halves, band)
        term = product * (1.0 / HALF_WIDTH)
        value[:, lanes] = term
        write_sends(plan, side, lanes.start, term, to_away, None)
        at = lanes.start - plan.rows + plan.edge
        if at >= 0:
            low[:, at : at + plan.tile] = term[: plan.half]
            high[:, at : at + plan.tile] = term[plan.half :]

    def write(at, term):
        to_far[:, at : at + plan.tile] = term

    copy.wait()
    write_far(plan, side, asked, value, write)


def run_first(plan, asked, far, band, inner, own):
    near = jax.ShapeDtypeStruct((plan.half, plan.edge), F32)
    shapes = [jax.ShapeDtypeStruct(far.shape, F32), send_shapes(plan)[0], near, near]
    return pl.pallas_call(
        functools.partial(first_kernel, plan),
        out_shape=[pltpu.VMEM((plan.width, plan.rows), F32)] + shapes,
        in_specs=[VMEM] * 5,
        out_specs=[VMEM] * (1 + len(shapes)),
        scratch_shapes=[
            halves_scratch(plan, plan.far),
            pltpu.SMEM(asked.shape, asked.dtype),
            pltpu.SemaphoreType.DMA,
        ],
        compiler_params=params(8),
        cost_estimate=cost(2 * plan.width * plan.rows**2, 0),
        name="first",
    )(asked, far, band, inner, own)


def second_kernel(plan, away, far, band, inner, own, start, out, halves, held, sems):
    side = parity()
    put_halves(plan, halves, away_tiles(plan, side, away))
    halves[:, plan.edge :] = far[...]
    copies = []
    for p in reversed(range(plan.pairs)):
        lanes = slice(p * plan.tile, (p + 1) * plan.tile)
        product = inner[:, lanes] - CENTER * own[:, lanes]
        begin = plan.outer_range(p)[0] * plan.tile
        vectors = far[...] if begin == plan.edge else halves[:, begin:]
        rows = band[p, : vectors.shape[1], :]
        product += fold(jnp.dot(vectors, rows, preferred_element_type=F32))
        term = 2.0 / HALF_WIDTH * product - start[:, lanes]
        place = pl.multiple_of(plan.mirrored(p, side) * plan.tile, plan.tile)
        held[p] = term.T
        copies.append(
            pltpu.make_async_copy(held.at[p], out.at[pl.ds(place, plan.tile), :], sems.at[p])
        )
        copies[-1].start()
    for copy in copies:
        copy.wait()


def run_second(plan, away, far, band, inner, own, start):
    return pl.pallas_call(
        functools.partial(second_kernel, plan),
        out_shape=jax.ShapeDtypeStruct((plan.rows, plan.width), F32),
        in_specs=[VMEM] * 6,
        out_specs=HBM,
        scratch_shapes=[
            halves_scratch(plan, plan.near + plan.far),
            pltpu.VMEM((plan.pairs, plan.tile, plan.width), F32),
            pltpu.SemaphoreType.DMA((plan.pairs,)),
        ],
        compiler_params=params(8),
        cost_estimate=cost(2 * plan.width * plan.rows**2, 0),
        name="second",
    )(away, far, band, inner, own, start)


def parity():
    return (lax.rem(lax.axis_index("rows"), 2),)


def after(value, *others):
    return lax.optimization_barrier((value, *others))[0]


def per_device(hamiltonian, subspace, block_cols, far_list):
    block_rows, entries = block_cols.shape
    size = hamiltonian.shape[1] // entries
    device_count = lax.axis_size("rows")
    first_row = lax.axis_index("rows") * block_rows
    block_total = block_rows * device_count
    swap_level = (device_count // 8).bit_length() - 1
    plan = Plan(size, block_rows * size, subspace.shape[1], far_list.shape[1])

    side = (lax.axis_index("rows") % 2).astype(jnp.int32).reshape(1)

    def exchange(listed, sends):
        to_away, to_near = sends
        far = partner(listed, "rows", swap_level)
        return swap_chips(to_away, "rows"), far, partner(to_near, "rows", 0)

    start, block_cols, *sends = pack(plan, subspace, block_cols)
    asked = partner(after(far_list, start), "rows", swap_level)
    listed = gather_far(plan, asked, start)
    away, far, near = exchange(listed, (sends[0], after(sends[1], listed)))

    block_cols = after(block_cols, listed)
    edge, far_slots = 2 * plan.near, 2 * plan.far
    shift = block_cols - first_row + edge
    shift = jnp.where(shift < 0, shift + block_total, shift)
    shift = jnp.where(shift >= block_total, shift - block_total, shift)
    last = block_rows + 2 * edge - 2
    shift = shift + side[0] * (last - 4 * (shift >> 1))
    places = jnp.where(
        block_cols >= block_total,
        edge + block_cols - block_total,
        jnp.where(
            shift < edge,
            shift,
            jnp.where(
                shift < edge + block_rows,
                shift - edge + 2 * plan.outer,
                shift - block_rows + far_slots,
            ),
        ),
    )
    every = jnp.arange(plan.places, dtype=jnp.int32)[None, None, :]
    entry = jnp.arange(entries, dtype=jnp.int32)[None, :, None]
    hit = places[:, :, None] == every
    inverse = entries + jnp.sum(jnp.where(hit, entry - entries, 0), axis=1)

    band, inner = make_band(plan, inverse, hamiltonian.T, start)

    inner = run_middle(plan, away, near, band, inner)
    value, listed, to_away, *to_near = run_first(plan, asked, far, band, inner, start)
    far, away = partner(listed, "rows", swap_level), swap_chips(to_away, "rows")
    low, high = (partner(part, "rows", 0) for part in to_near)
    inner = run_inner(plan, value, low, high, band)
    far = split_far(plan, after(far, inner))
    return run_second(plan, away, far, band, inner, value, start)


def solution(mesh):
    placed = (P("rows", None), P("rows", None), P("rows", None), P("rows", None))
    return jax.shard_map(
        per_device, mesh=mesh, in_specs=placed, out_specs=P("rows", None), check_vma=False
    )
```
